128 devices in a mesh: ctx: 32 (over x, y, core), head: 4 (over z).
Axes of the slice: x: 4, y: 4, z: 4, core: 2. Of those that a mesh axis runs over, the one named last changes fastest.
Arguments:
- queries: bfloat16 [8192, 3072], P('ctx', 'head'), may hold values from -128 to 128
- keys: bfloat16 [8192, 3072], P('ctx', 'head'), may hold values from -4 to 4
- values: bfloat16 [8192, 3072], P('ctx', 'head'), may hold values from -4 to 4
- block_mask: int32 [64, 64], P('ctx'), may hold values from 0 to 1, as said below
- w_out: bfloat16 [3072, 3072], P('head'), may hold values from -0.109375 to 0.109375
Outputs:
- projected: bfloat16 [8192, 3072], P('ctx', 'head')
The draws below stay inside these ranges and needn't reach their ends.
Inputs may be any that keep to these rules, and one draw needn't show every extreme that they name: Entries are 0 or 1. block_mask[a, b] is 1 where query block a and key block b lie in the same frame of 256 tokens; elsewhere it can be 1 only where their frame distance is a power of two.
All inputs are finite; a program needn't handle non-finite values.
Results may differ from the reference program's by a relative error of at most 0.017.
Values may be sent and summed in bfloat16 or wider, within the bound.
A program may use at most 128 MiB of HBM per device.

```python
import jax
import jax.numpy as jnp
from jax import lax

D = 3072
HEADS = 24
HEAD_DIM = 128
BLOCK = 128
FRAME_TOK = 256
TOKENS = 8192


def draw_keys(key, part):
    key = jax.random.fold_in(key, 3)
    rows = jnp.clip(jax.random.normal(key, (TOKENS, D), jnp.float32), -4.0, 4.0)
    return rows.astype(jnp.bfloat16)


def draw_queries(key, part):
    key = jax.random.fold_in(key, 7)
    rows = jnp.clip(jax.random.normal(key, (TOKENS, D), jnp.float32), -4.0, 4.0)
    return rows.astype(jnp.bfloat16)


def draw_block_mask(key, part):
    key = jax.random.fold_in(key, 5)
    count = TOKENS // BLOCK
    per_frame = FRAME_TOK // BLOCK
    frame = jnp.arange(count, dtype=jnp.int32) // per_frame
    apart = jnp.abs(frame[:, None] - frame[None, :])
    power = (apart > 0) & (apart & apart - 1 == 0)
    limit = jnp.where(apart == 1, 8, jnp.where(apart == 2, 4, 2))
    bits = jax.random.randint(key, (count, count), 0, 8)
    return ((apart == 0) | power & (bits < limit)).astype(jnp.int32)


def steps_of(rng, dims, pieces, least, largest):
    def one(dim, shards_of):
        heights = jax.random.uniform(jax.random.fold_in(jax.random.fold_in(rng, 6), dim), (shards_of,), jnp.float32, least / len(pieces), largest / len(pieces))
        return jnp.repeat(jnp.exp(heights), dims[dim] // shards_of).reshape((-1,) + (1,) * (len(dims) - dim - 1))

    loudness = one(*pieces[0])
    for cut in pieces[1:]:
        loudness = loudness * one(*cut)
    return loudness


def gaussian(own_key, extent, deviation, most, pieces=(), held_as=jnp.bfloat16):
    factor_of = steps_of(own_key, extent, pieces, -0.22, 0.18) if pieces else 1.0
    drawn = jax.random.normal(own_key, extent, jnp.float32) * deviation * factor_of
    return jnp.minimum(jnp.maximum(drawn, -most), most).astype(held_as)


def setup_inputs(seed: int = 0) -> dict:
    seeds = jax.random.split(jax.random.key(seed), 6)
    return {
        "queries": draw_queries(jax.random.fold_in(seeds[5], 71), 0),
        "keys": draw_keys(jax.random.fold_in(seeds[5], 71), 0),
        "values": gaussian(seeds[2], (TOKENS, D), 1.0, 4.0, ((0, 32), (1, 4))),
        "block_mask": draw_block_mask(jax.random.fold_in(seeds[5], 71), 0),
        "w_out": gaussian(seeds[4], (D, D), D ** -0.5, 0.109375, ((0, 4),)),
    }


def reference(queries, keys, values, block_mask, w_out):
    allowed = jnp.repeat(jnp.repeat(block_mask > 0, BLOCK, axis=0), BLOCK, axis=1)
    allowed = allowed | (jnp.arange(TOKENS)[None, :] < FRAME_TOK)
    scale = HEAD_DIM ** -0.5
    q_heads = queries.reshape(TOKENS, HEADS, HEAD_DIM).transpose(1, 0, 2)
    k_heads = keys.reshape(TOKENS, HEADS, HEAD_DIM).transpose(1, 0, 2)
    v_heads = values.reshape(TOKENS, HEADS, HEAD_DIM).transpose(1, 0, 2)

    def one_head(triple):
        q_one, k_one, v_one = triple
        scores = jnp.dot(q_one, k_one.T, preferred_element_type=jnp.float32) * scale
        scores = jnp.where(allowed, scores, jnp.float32(-1e30))
        top = jnp.max(scores, axis=1, keepdims=True)
        weights = jnp.where(allowed, jnp.exp(scores - top), jnp.float32(0.0))
        denom = jnp.sum(weights, axis=1, keepdims=True)
        mixed = jnp.dot(weights.astype(jnp.bfloat16), v_one, preferred_element_type=jnp.float32)
        return mixed / denom

    result = lax.map(one_head, (q_heads, k_heads, v_heads))
    attended = result.transpose(1, 0, 2).reshape(TOKENS, D).astype(jnp.bfloat16)
    return jnp.dot(attended, w_out, preferred_element_type=jnp.float32).astype(jnp.bfloat16)
```

```python
import functools

import jax
import jax.numpy as jnp
from jax import lax
from jax.experimental import pallas as pl
from jax.experimental.pallas import tpu as pltpu
from jax.sharding import PartitionSpec as P

HEAD_DIM = 128
BLOCK = 128
FRAME = 256
HEADS_CORE = 3
MESH = pl.DeviceIdType.MESH
NEG = -1e30
EXP2_SCALE = HEAD_DIM ** (-0.5) * 1.4426950408889634

ROUTES = (
    ((10802005, 2945991, 2945991, 2679686), (2413381, 2945991, 2945991, 6874022)),
    ((1048832, 1065216, 1065220, 256), (1065216, 260, 260, 1048580)),
    ((8, 2129920, 2129920, 33288), (2129920, 2130440, 33288, 32776)),
    ((65, 532480, 65, 524288), (1, 524289, 524289, 532480)),
    ((0, 0, 0, 0), (0, 0, 0, 0)),
    ((0, 1314880, 1183744, 1314881), (0, 1314881, 1048576, 1314881)),
    ((524426, 2056, 532618, 0), (532618, 8, 8330, 0)),
    ((0, 0, 0, 0), (0, 0, 0, 0)),
)
ANCHOR_ROUTES = ((274570, 4, 262152, 8320), (291010, 0, 2097160, 16512))
ORDER = (5, 6, 1, 2, 7, 3, 4)
OFFSET = {1: -1, 2: 1, 5: -4, 6: 4}
WAYS = 6
FULL = ((0, 0, 512), (1, 0, 512))
DIAGONAL = ((0, 0, 256), (1, 256, 512))
TILES = {0: FULL, 1: ((0, 0, 512), (1, 256, 512)), 2: ((0, 0, 256), (1, 0, 512))}
ANCHOR_TILES = ((0, 0, 256), (1, 0, 256))


def bits_at(packed, p):
    group = p // 4
    word = jnp.where(group == 0, packed[0], jnp.where(group == 1, packed[1], jnp.where(group == 2, packed[2], packed[3])))
    return (word >> (WAYS * (p % 4))) & 63


def used(packed, direction):
    return any((packed[p // 4] >> (WAYS * (p % 4) + direction)) & 1 for p in range(16))


def kernel(
    q_ref, k_ref, v_ref, mask_ref, w_ref, out_ref,
    kv, qs, masks, bias, wts, att, attended, top, total, accum, proj,
    kv_recv, kv_send, q_recv, q_local, kv_local, swap_send,
    w_recv, w_send, w_local, w_pass_recv, w_pass_send, att_recv, att_send, mask_sem,
):
    i = lax.axis_index("ctx")
    z = lax.axis_index("head")
    c = i % 2
    p = i // 2
    x = p // 4
    y = p % 4
    twin = (p * 2 + 1 - c, z)

    def neighbour(direction):
        if direction == 0:
            return ((x + 1) % 4) * 4 + y
        if direction == 1:
            return ((x + 3) % 4) * 4 + y
        if direction == 2:
            return x * 4 + (y + 1) % 4
        if direction == 3:
            return x * 4 + (y + 3) % 4
        if direction == 4:
            return ((x + 2) % 4) * 4 + y
        return x * 4 + (y + 2) % 4

    def slot_of(delta, there):
        near = (delta == 2) == (there % 4 < 2)
        slot = jnp.where((delta == 2) | (delta == -2), jnp.where(near, 3, 4), 7)
        slot = jnp.where(delta == -1, 1, jnp.where(delta == 1, 2, slot))
        return jnp.where(delta == -4, 5, jnp.where(delta == 4, 6, slot))

    def source_of(slot):
        if slot == 7:
            return jnp.where(p < 8, p + 8, p - 8)
        if slot == 3:
            return jnp.where(y < 2, p + 2, p - 2)
        if slot == 4:
            return jnp.where(y < 2, p - 2, p + 2)
        return p + OFFSET[slot]

    def remote(src, dst, send, recv, device):
        return pltpu.make_async_remote_copy(
            src_ref=src, dst_ref=dst, send_sem=send, recv_sem=recv, device_id=device, device_id_type=MESH
        )

    barrier = pltpu.get_barrier_semaphore()
    greeted = [(neighbour(d) * 2 + c, z) for d in range(WAYS)] + [twin]
    for dz in (1, 2, 3):
        greeted += [(i, (z + dz) % 4), (p * 2 + 1 - c, (z + dz) % 4)]
    for device in greeted:
        pl.semaphore_signal(barrier, inc=1, device_id=device, device_id_type=MESH)
    pl.semaphore_wait(barrier, len(greeted))

    my_rows = pl.ds(pl.multiple_of(c * FRAME, FRAME), FRAME)
    twin_rows = pl.ds(pl.multiple_of((1 - c) * FRAME, FRAME), FRAME)

    def columns(core, h):
        return pl.ds(pl.multiple_of((HEADS_CORE * core + h) * HEAD_DIM, HEAD_DIM), HEAD_DIM)

    def swap_kv(h, which):
        ref = (k_ref, v_ref)[which]
        return remote(ref.at[:, columns(1 - c, h)], kv.at[0, which, h, my_rows, :], swap_send.at[which, h], kv_recv.at[0, which, h], twin)

    def swap_q(h):
        return remote(q_ref.at[:, columns(1 - c, h)], qs.at[h, my_rows, :], swap_send.at[2, h], q_recv.at[h], twin)

    def keep_kv(h, which):
        ref = (k_ref, v_ref)[which]
        return pltpu.make_async_copy(ref.at[:, columns(c, h)], kv.at[0, which, h, my_rows, :], kv_local.at[which, h])

    def keep_q(h):
        return pltpu.make_async_copy(q_ref.at[:, columns(c, h)], qs.at[h, my_rows, :], q_local.at[h])

    swap_mask = remote(mask_ref, masks.at[c], mask_sem.at[0], mask_sem.at[1], twin)
    keep_mask = pltpu.make_async_copy(mask_ref, masks.at[c], mask_sem.at[2])
    for h in range(HEADS_CORE):
        swap_kv(h, 0).start()
        keep_kv(h, 0).start()
        swap_kv(h, 1).start()
        keep_kv(h, 1).start()
        if h == 0:
            swap_mask.start()
            keep_mask.start()
        swap_q(h).start()
        keep_q(h).start()

    def w_block(h, core, zz):
        rows = pl.ds(pl.multiple_of((HEADS_CORE * core + h) * HEAD_DIM, HEAD_DIM), HEAD_DIM)
        return w_ref.at[rows, pl.ds(pl.multiple_of(zz * 768, 768), 768)]

    def w_copy(h, dz):
        zz = (z + dz) % 4
        return remote(w_block(h, c, zz), wts.at[h, z * 2 + c], w_send.at[h, dz - 1], w_recv.at[h, dz - 1], (i, zz))

    def w_keep(h, core):
        return pltpu.make_async_copy(w_block(h, core, z), wts.at[h, z * 2 + core], w_local.at[h, core])

    def w_pass(h, dz):
        place = ((z + 4 - dz) % 4) * 2 + c
        return remote(wts.at[h, place], wts.at[h, place], w_pass_send.at[h, dz - 1], w_pass_recv.at[h, dz - 1], twin)

    for h in range(HEADS_CORE):
        for dz in (1, 3, 2):
            w_copy(h, dz).start()
    for h in range(HEADS_CORE):
        for core in (0, 1):
            w_keep(h, core).start()

    def send_on(slot, which, direction, h, packed, source, anchor, guard):
        there = neighbour(direction)
        device = (there * 2 + c, z)
        if anchor:
            here = kv.at[slot, which, h, 0:FRAME, :]
            dst = kv.at[8, which, h, 0:FRAME, :]
            sem = kv_send.at[8, which, direction]
            recv = kv_recv.at[8, which, h]
        else:
            target = slot_of(source - there, there)
            here = kv.at[slot, which, h]
            dst = kv.at[target, which, h]
            sem = kv_send.at[slot, which, direction]
            recv = kv_recv.at[target, which, h]
        return remote(here, dst, sem, recv, device)

    def pass_on(slot, which, h, packed, source, anchor=False, guard=None):
        bits = bits_at(packed, p)
        for direction in range(WAYS):
            if not used(packed, direction):
                continue
            go = ((bits >> direction) & 1) == 1
            if guard is not None:
                go = go & guard

            @pl.when(go)
            def _():
                copy = send_on(slot, which, direction, h, packed, source, anchor, guard)

                @pl.when(h > 0)
                def _():
                    copy.wait_send()

                copy.start()

    def wait_kv(slot, which, h, rows=512):
        here = kv.at[slot, which, h, 0:rows, :]
        remote(here, here, kv_send.at[0, 0, 0], kv_recv.at[slot, which, h], twin).wait_recv()

    def anchor_on(slot, h, guard):
        for which in (0, 1):
            pass_on(slot, which, h, ANCHOR_ROUTES[which], 0, anchor=True, guard=guard)

    def own_out(h):
        for which in (0, 1):
            keep_kv(h, which).wait()
            swap_kv(h, which).wait_recv()
            pass_on(0, which, h, ROUTES[0][which], p)
        anchor_on(0, h, p == 0)

    own_out(0)

    keep_mask.wait()
    swap_mask.wait_recv()
    for s in range(16):
        for b in range(4):
            for core in (0, 1):
                bit = masks[core, :, 4 * s + b : 4 * s + b + 1]
                wide = jnp.broadcast_to(bit, (2, BLOCK))
                row = jnp.where(wide > 0, 0.0, NEG).astype(jnp.float32)
                if s == 0 and b < 2:
                    row = jnp.full((2, BLOCK), NEG, jnp.float32)
                bias[s, core, :, b * BLOCK : (b + 1) * BLOCK] = row

    def attend(slot, h, source, tiles):
        for frame, first, last in tiles:
            rows = slice(frame * FRAME, (frame + 1) * FRAME)
            keys = kv[slot, 0, h, first:last, :]
            values = kv[slot, 1, h, first:last, :]
            scores = lax.dot_general(
                qs[h, rows, :], keys, (((1,), (1,)), ((), ())), preferred_element_type=jnp.float32
            )
            scores = scores * EXP2_SCALE
            if source is not None:
                added = bias[source, frame, :, first:last]
                scores = (scores.reshape(2, BLOCK, last - first) + added[:, None, :]).reshape(FRAME, last - first)
            before = top[rows, :]
            now = jnp.maximum(before, jnp.max(scores, axis=1, keepdims=True))
            weights = jnp.exp2(scores - now)
            factor = jnp.exp2(before - now)
            total[rows, :] = total[rows, :] * factor + jnp.sum(weights, axis=1, keepdims=True)
            mixed = jnp.dot(weights.astype(jnp.bfloat16), values, preferred_element_type=jnp.float32)
            accum[rows, :] = accum[rows, :] * factor + mixed
            top[rows, :] = now

    def att_copy(h, dz, cross):
        core = 1 - c if cross else c
        rows = twin_rows if cross else my_rows
        return remote(
            attended.at[h, rows, :], att.at[h, z * 2 + c], att_send.at[h, dz, cross], att_recv.at[h, dz, cross],
            (p * 2 + core, (z + dz) % 4),
        )

    def project(h):
        for dz in range(4):
            for cross in (0, 1):
                if dz or cross:
                    att_copy(h, dz, cross).wait_recv()
        for dz in (1, 2, 3):
            w_pass(h, dz).wait_recv()
        for core in (0, 1):
            w_keep(h, core).wait()
        for n in range(3):
            cols = slice(n * 256, (n + 1) * 256)
            part = proj[:, cols]
            for pair in range(4):
                left = jnp.concatenate([att[h, 2 * pair], att[h, 2 * pair + 1]], axis=1)
                right = jnp.concatenate([wts[h, 2 * pair, :, cols], wts[h, 2 * pair + 1, :, cols]], axis=0)
                part = part + jnp.dot(left, right, preferred_element_type=jnp.float32)
            proj[:, cols] = part

    proj[...] = jnp.zeros_like(proj)
    anchor_slot = jnp.where(p == 0, 0, jnp.where(p == 1, 1, jnp.where(p == 2, 3, jnp.where(p == 4, 5, jnp.where(p == 8, 7, 8)))))

    def phase(h, carry):
        keep_q(h).wait()
        swap_q(h).wait_recv()
        top[...] = jnp.full_like(top, NEG)
        total[...] = jnp.zeros_like(total)
        accum[...] = jnp.zeros_like(accum)
        attend(0, h, p, TILES[0])
        for place, slot in enumerate(ORDER):
            source = source_of(slot)

            def arrive():
                for which in (0, 1):
                    wait_kv(slot, which, h)
                    pass_on(slot, which, h, ROUTES[slot][which], source)
                if slot in (1, 3, 5, 7):
                    anchor_on(slot, h, source == 0)
                attend(slot, h, source, TILES.get(slot, DIAGONAL))

            if slot == 7:
                arrive()
            else:
                pl.when((source >= 0) & (source < 16))(arrive)
            if place == 3:
                @pl.when(h < HEADS_CORE - 1)
                def _():
                    own_out(h + 1)

        @pl.when(anchor_slot == 8)
        def _():
            for which in (0, 1):
                wait_kv(8, which, h, FRAME)
            anchor_on(8, h, anchor_slot == 8)

        attend(anchor_slot, h, None, ANCHOR_TILES)
        attended[h] = (accum[...] / total[...]).astype(jnp.bfloat16)
        for dz in (1, 3, 2, 0):
            for cross in (0, 1):
                if dz or cross:
                    att_copy(h, dz, cross).start()
        att[h, z * 2 + c] = attended[h, my_rows, :]
        for dz in (1, 3, 2):
            w_copy(h, dz).wait_recv()
            w_pass(h, dz).start()

        @pl.when(h > 0)
        def _():
            project(h - 1)

        return carry

    lax.fori_loop(0, HEADS_CORE, phase, 0)
    project(HEADS_CORE - 1)
    out_ref[...] = proj[...].astype(jnp.bfloat16)

    last = HEADS_CORE - 1
    for h in range(HEADS_CORE):
        for which in (0, 1):
            swap_kv(h, which).wait_send()
        swap_q(h).wait_send()
        for dz in range(4):
            if dz:
                w_copy(h, dz).wait_send()
                w_pass(h, dz).wait_send()
            for cross in (0, 1):
                if dz or cross:
                    att_copy(h, dz, cross).wait_send()
    swap_mask.wait_send()

    def drain(slot, which, packed, source, anchor, guard=None):
        bits = bits_at(packed, p)
        for direction in range(WAYS):
            if used(packed, direction):
                go = ((bits >> direction) & 1) == 1
                if guard is not None:
                    go = go & guard

                @pl.when(go)
                def _():
                    send_on(slot, which, direction, last, packed, source, anchor, guard).wait_send()

    for which in (0, 1):
        drain(0, which, ROUTES[0][which], p, False)
        for slot in ORDER:
            drain(slot, which, ROUTES[slot][which], source_of(slot), False)
        drain(8, which, ANCHOR_ROUTES[which], 0, True)


def body(queries, keys, values, block_mask, w_out):
    bf16, f32, dma = jnp.bfloat16, jnp.float32, pltpu.SemaphoreType.DMA
    heads = HEADS_CORE
    anywhere = pl.BlockSpec(memory_space=pl.ANY)
    return pl.pallas_call(
        kernel,
        out_shape=jax.ShapeDtypeStruct((FRAME, 768), bf16),
        in_specs=[anywhere, anywhere, anywhere, pl.BlockSpec(memory_space=pltpu.VMEM), anywhere],
        out_specs=pl.BlockSpec(memory_space=pltpu.VMEM),
        scratch_shapes=[
            pltpu.VMEM((9, 2, heads, 2 * FRAME, HEAD_DIM), bf16),
            pltpu.VMEM((heads, 2 * FRAME, HEAD_DIM), bf16),
            pltpu.VMEM((2, 2, 64), jnp.int32),
            pltpu.VMEM((16, 2, 2, 2 * FRAME), f32),
            pltpu.VMEM((heads, 8, HEAD_DIM, 768), bf16),
            pltpu.VMEM((heads, 8, FRAME, HEAD_DIM), bf16),
            pltpu.VMEM((heads, 2 * FRAME, HEAD_DIM), bf16),
            pltpu.VMEM((2 * FRAME, 1), f32),
            pltpu.VMEM((2 * FRAME, 1), f32),
            pltpu.VMEM((2 * FRAME, HEAD_DIM), f32),
            pltpu.VMEM((FRAME, 768), f32),
            dma((9, 2, heads)), dma((9, 2, WAYS)), dma((heads,)), dma((heads,)), dma((2, heads)), dma((3, heads)),
            dma((heads, 3)), dma((heads, 3)), dma((heads, 2)), dma((heads, 3)), dma((heads, 3)),
            dma((heads, 4, 2)), dma((heads, 4, 2)), dma((3,)),
        ],
        compiler_params=pltpu.CompilerParams(
            collective_id=0, has_side_effects=True, vmem_limit_bytes=48 * 1024 * 1024
        ),
        name="radial_attention",
    )(queries, keys, values, block_mask, w_out)


def solution(mesh):
    placed = (P("ctx", "head"), P("ctx", "head"), P("ctx", "head"), P("ctx", None), P("head", None))
    return jax.shard_map(
        body, mesh=mesh, in_specs=placed, out_specs=P("ctx", "head"), check_vma=False
    )
```

```python
import jax
import jax.numpy as jnp
from jax import lax
from jax.experimental import pallas as pl
from jax.experimental.pallas import tpu as pltpu
from jax.sharding import PartitionSpec as P

HEAD_DIM = 128
BLOCK = 128
FRAME = 256
HEADS_CORE = 3
MESH = pl.DeviceIdType.MESH
NEG = -1e30
EXP2_SCALE = HEAD_DIM ** (-0.5) * 1.4426950408889634

STEPS = (
    (17024, 262784, 525952, 787584, 1049472, 1312512, 1574784, 1836416, 2098048, 2360192, 2623232, 2884992, 3146496, 3409664, 3670784, 3933440),
    (164544, 296128, 558784, 820416, 1082176, 1345344, 1606336, 1869248, 2130880, 2394048, 2655936, 2917568, 3179328, 3442496, 3704128, 3966272),
    (1048582, 513, 262657, 4104, 24709, 262277, 524421, 787077, 1048709, 2097665, 1572869, 1835525, 2097157, 2359429, 3407873, 2883589),
    (263234, 524290, 787458, 524801, 1310722, 1049089, 1311233, 1572865, 3147014, 2622466, 2359809, 2621441, 3408898, 3146241, 3933186, 3670529),
    (1082694, 1310982, 1573126, 1835270, 2097414, 1573890, 1836034, 2883846, 2359362, 3408134, 2884610, 3932422, 2129989, 3671106, 2621637, 20488),
    (656, 168513, 820290, 557633, 180421, 2359302, 2621702, 8, 3178822, 2130497, 3670278, 1868485, 3440706, 2392261, 3441217, 2917061),
    (180944, 557122, 525968, 1867846, 1343554, 295109, 557253, 819909, 2098064, 2655298, 1605829, 2654273, 3146512, 3179073, 3966018, 3933456),
    (524420, 1343814, 557776, 787600, 2131270, 1081921, 1344065, 1606209, 2130896, 3440966, 2392641, 3965254, 3179344, 3409168, 3670800, 3966288),
    (2097159, 262800, 3, 820432, 1049360, 2392134, 1868866, 1836432, 8199, 2361104, 2917442, 2884752, 3670532, 3442000, 3704656, 1835015),
    (557252, 296656, 2621703, 263235, 1082192, 1311888, 1574288, 1869008, 1835521, 2394064, 3703110, 2917584, 1048583, 1310983, 1572871, 3408131),
    (262226, 2359303, 2654407, 295427, 786433, 1345360, 1606608, 3932167, 2621572, 262151, 2623376, 3145730, 3703876, 3932164, 20488, 1867847),
    (2129991, 786564, 174147, 2883591, 1572996, 1835012, 3670023, 131144, 188487, 2883716, 2654928, 8, 1081671, 8264, 3145987, 3440963),
    (360450, 2392135, 787474, 2916551, 3145735, 8, 1048835, 1310979, 1867841, 294983, 524295, 786439, 2884161, 3964996, 1605831, 2883733),
    (4768, 4625, 1573142, 1049666, 819265, 3407879, 3702855, 3964999, 2654404, 2097681, 2097411, 2360067, 2097173, 3145745, 3933202, 3702849),
    (168672, 1311062, 262673, 524817, 24725, 1867972, 524437, 787093, 3147030, 3408150, 2884626, 3932438, 3408914, 2359381, 2654213, 3670545),
    (1049878, 884932, 820306, 1835286, 1311762, 262293, 1836050, 2098242, 1572867, 2916420, 3670294, 819271, 3146528, 1343815, 3178819, 3933472),
    (524436, 168529, 1605718, 2136, 3178567, 1049105, 1081411, 1343811, 2392066, 1310869, 557127, 2392387, 3179360, 3670098, 2621589, 3966304),
    (1082710, 263840, 525472, 787616, 1606340, 3440711, 2621462, 2359300, 2359314, 2130513, 2129987, 147528, 2130005, 16408, 204872, 1835031),
    (263202, 296160, 558304, 820448, 172245, 1573906, 557269, 24, 3179862, 3440982, 2917458, 3965270, 3441746, 3179089, 3966034, 2917077),
    (557780, 524306, 1605702, 557649, 1049376, 295125, 1868882, 819925, 2097952, 2360480, 3703126, 2884768, 24, 3408672, 3671328, 3409171),
    (1048870, 786452, 295505, 1310724, 1082208, 1081937, 1574560, 1836448, 2130784, 2392800, 2622624, 2917600, 40, 2884611, 3703648, 3703377),
    (296034, 4641, 294977, 131144, 1344594, 1312544, 1606496, 1869280, 16407, 2621458, 2655456, 1835029, 3670548, 3442016, 1572887, 204872),
    (294930, 1311014, 1049092, 2883735, 2097430, 1344864, 1310801, 1573457, 2393170, 8, 1572885, 2621969, 2621443, 147464, 2654421, 2884261),
    (1082726, 819412, 2621463, 1343556, 786961, 2359574, 2097668, 3932183, 1081413, 1835075, 2359825, 3146770, 147560, 1311063, 3146067, 3442003),
    (2097175, 166497, 6163, 1048594, 524291, 2072, 2129988, 1312019, 2621588, 1310725, 4104, 3407876, 2916353, 3702786, 3933218, 3670625),
    (525476, 1343846, 1146948, 262675, 1574036, 1835156, 2654278, 2916422, 1671235, 2883732, 131144, 1868501, 2883665, 1343639, 2621605, 20584),
    (2195543, 1343510, 1573222, 2916567, 2131286, 786435, 1048851, 147544, 2360354, 1867779, 1605845, 2654801, 2654275, 3932180, 3408417, 2916581),
    (558308, 525346, 2654423, 1835046, 819281, 2392406, 72, 1572897, 3147046, 262167, 2392145, 3178578, 1048855, 159832, 3966050, 1867991),
    (2097447, 557138, 163923, 1081426, 622659, 1605698, 3670039, 2392132, 1835089, 1343557, 3145732, 3440708, 3408994, 2981955, 8216, 3408675),
    (2195815, 2359575, 787490, 294995, 1310754, 1867988, 1836066, 1343827, 180311, 200776, 2883618, 786455, 3702868, 2359461, 2654437, 3442019),
    (15, 2359463, 1048596, 2883751, 3145751, 819267, 1081683, 787109, 3179878, 2916564, 524311, 2359571, 2621459, 3965012, 135256, 2072),
    (15, 558178, 2621607, 1868134, 1606356, 131160, 524453, 1606241, 2654932, 294999, 2097427, 2392403, 8, 40, 3407889, 1835111),
    (15, 2457687, 262177, 262179, 24741, 3407895, 3702871, 3965015, 1572883, 2097697, 3244612, 3932454, 1081687, 3146273, 1573223, 196696),
    (15, 2392295, 820322, 1146882, 1344610, 1573922, 1868898, 2098258, 1048597, 3408166, 2917474, 24, 196680, 2392293, 1605719, 1867815),
    (15, 786468, 1146964, 2916583, 3178583, 262309, 196616, 819941, 2622628, 8216, 557143, 819287, 147544, 3671074, 3146019, 3702817),
    (15, 884964, 2654439, 1310740, 786977, 1049121, 1311265, 2195458, 1605715, 2622498, 2130003, 3244098, 1048871, 1311015, 3440721, 196648),
    (15, 15, 14371, 296035, 180453, 3440727, 557285, 2359316, 1081429, 2130529, 3670310, 3965286, 2884129, 3179105, 4200, 15),
    (15, 15, 163939, 1867862, 1573028, 1835172, 1343505, 1605649, 8231, 3440998, 3145876, 2360611, 3671076, 2884627, 3244051, 15),
    (15, 15, 1049124, 1343572, 2098470, 196680, 24, 2088, 1933329, 1836051, 1573029, 1835173, 2654291, 3932196, 3178595, 15),
    (15, 15, 295009, 196632, 1606372, 295141, 2097684, 2883606, 1048613, 2655330, 2359905, 3407892, 1081703, 1343847, 139304, 15),
    (15, 15, 1081444, 40, 524307, 1081953, 1048867, 1311011, 172135, 1343573, 3703142, 3145762, 3703396, 3702802, 3440737, 15),
    (15, 15, 1671206, 1049698, 2131302, 1867876, 131160, 2392148, 1835617, 2654290, 524327, 1868389, 2981905, 2916435, 1671335, 15),
    (15, 15, 15, 1310756, 819297, 3407911, 2654294, 1344867, 2655460, 1867859, 2097187, 131160, 2621475, 3965028, 15, 15),
    (15, 15, 15, 524321, 622675, 786451, 3670055, 2916438, 1081445, 2883812, 3178580, 2392931, 3440674, 2457621, 15, 15),
    (15, 15, 15, 1081378, 3145767, 819283, 1081443, 2195474, 1572899, 196696, 2392097, 3506260, 2097189, 2883875, 15, 15),
    (15, 15, 15, 1343588, 524323, 104, 2195540, 3932199, 2392162, 262183, 24, 786471, 2654307, 2917475, 15, 15),
    (15, 15, 15, 557153, 3178599, 3440743, 2621478, 151656, 1867809, 1310757, 196696, 104, 2916449, 3702882, 15, 15),
    (15, 15, 15, 196712, 622691, 1671250, 3702887, 2883622, 1671267, 8232, 557159, 3179618, 2195557, 196712, 15, 15),
    (15, 15, 15, 15, 15, 2359334, 1343585, 3965031, 15, 1836067, 2130275, 819303, 15, 15, 15, 15),
    (15, 15, 15, 15, 15, 131112, 2654310, 2098210, 15, 1343589, 1605733, 3407908, 15, 15, 15, 15),
    (15, 15, 15, 15, 15, 786467, 104, 2916454, 15, 133224, 40, 2621473, 15, 15, 15, 15),
    (15, 15, 15, 15, 15, 2392166, 131112, 2359332, 15, 295015, 3145764, 131112, 15, 15, 15, 15),
    (15, 15, 15, 15, 15, 819299, 2097252, 2130018, 15, 2916388, 3178596, 3440740, 15, 15, 15, 15),
    (15, 15, 15, 15, 15, 1671266, 2195492, 2457700, 15, 1933411, 196712, 2719841, 15, 15, 15, 15),
)
COUNT = len(STEPS)
LAG = 12
VMEM_LIMIT = 60 * 1024 * 1024
W_STEPS = (18, 30, 42)


def pick(values, p):
    values = list(values)
    while len(values) & (len(values) - 1):
        values.append(values[-1])
    bit = 1
    while len(values) > 1:
        odd = (p // bit) % 2 == 1
        values = [jnp.where(odd, b, a) for a, b in zip(values[::2], values[1::2])]
        bit *= 2
    return values[0]


def kernel(
    q_ref, k_ref, v_ref, mask_ref, w_ref, out_ref,
    kv, qs, masks, bias, wts, att, attended, top, total, accum, proj,
    kv_recv, kv_send, q_recv, q_local, kv_local, swap_send,
    w_recv, w_send, w_local, w_pass_recv, w_pass_send, att_recv, att_send, mask_sem,
):
    i = lax.axis_index("ctx")
    z = lax.axis_index("head")
    c = i % 2
    p = i // 2
    x = p // 4
    y = p % 4
    twin = (p * 2 + 1 - c, z)
    neighbours = (((x + 1) % 4) * 4 + y, ((x + 3) % 4) * 4 + y, x * 4 + (y + 1) % 4, x * 4 + (y + 3) % 4)

    def slot_of(delta):
        slot = jnp.where(delta == -2, 3, jnp.where(delta == 2, 4, 7))
        slot = jnp.where(delta == -1, 1, jnp.where(delta == 1, 2, slot))
        return jnp.where(delta == -4, 5, jnp.where(delta == 4, 6, slot))

    def remote(src, dst, send, recv, device):
        return pltpu.make_async_remote_copy(
            src_ref=src, dst_ref=dst, send_sem=send, recv_sem=recv, device_id=device, device_id_type=MESH
        )

    barrier = pltpu.get_barrier_semaphore()
    greeted = [(there * 2 + c, z) for there in neighbours] + [twin]
    for dz in (1, 2, 3):
        greeted += [(i, (z + dz) % 4), (p * 2 + 1 - c, (z + dz) % 4)]
    for device in greeted:
        pl.semaphore_signal(barrier, inc=1, device_id=device, device_id_type=MESH)

    my_rows = pl.ds(pl.multiple_of(c * FRAME, FRAME), FRAME)
    twin_rows = pl.ds(pl.multiple_of((1 - c) * FRAME, FRAME), FRAME)

    def columns(core, h):
        return pl.ds(pl.multiple_of((HEADS_CORE * core + h) * HEAD_DIM, HEAD_DIM), HEAD_DIM)

    def swap_kv(h, which):
        ref = (k_ref, v_ref)[which]
        return remote(ref.at[:, columns(1 - c, h)], kv.at[0, which, h, my_rows, :], swap_send.at[which, h], kv_recv.at[0, which, h], twin)

    def swap_q(h):
        return remote(q_ref.at[:, columns(1 - c, h)], qs.at[h, my_rows, :], swap_send.at[2, h], q_recv.at[h], twin)

    def keep_kv(h, which):
        ref = (k_ref, v_ref)[which]
        return pltpu.make_async_copy(ref.at[:, columns(c, h)], kv.at[0, which, h, my_rows, :], kv_local.at[which, h])

    def keep_q(h):
        return pltpu.make_async_copy(q_ref.at[:, columns(c, h)], qs.at[h, my_rows, :], q_local.at[h])

    swap_mask = remote(mask_ref, masks.at[c], mask_sem.at[0], mask_sem.at[1], twin)
    keep_mask = pltpu.make_async_copy(mask_ref, masks.at[c], mask_sem.at[2])

    def w_block(h, core, zz):
        rows = pl.ds(pl.multiple_of((HEADS_CORE * core + h) * HEAD_DIM, HEAD_DIM), HEAD_DIM)
        return w_ref.at[rows, pl.ds(pl.multiple_of(zz * 768, 768), 768)]

    def w_copy(h, dz):
        zz = (z + dz) % 4
        return remote(w_block(h, c, zz), wts.at[h, z * 2 + c], w_send.at[h, dz - 1], w_recv.at[h, dz - 1], (i, zz))

    def w_keep(h, core):
        return pltpu.make_async_copy(w_block(h, core, z), wts.at[h, z * 2 + core], w_local.at[h, core])

    def w_pass(h, dz):
        place = ((z + 4 - dz) % 4) * 2 + c
        return remote(wts.at[h, place], wts.at[h, place], w_pass_send.at[h, dz - 1], w_pass_recv.at[h, dz - 1], twin)

    for h in range(HEADS_CORE):
        keep_kv(h, 0).start()
        keep_kv(h, 1).start()
        keep_q(h).start()
    keep_mask.start()
    pl.semaphore_wait(barrier, len(greeted))
    for h in range(HEADS_CORE):
        swap_kv(h, 0).start()
        swap_kv(h, 1).start()
        swap_q(h).start()
        if h == 0:
            swap_mask.start()
    for h in range(HEADS_CORE):
        for dz in (1, 3, 2):
            w_copy(h, dz).start()
    for h in range(HEADS_CORE):
        for core in (0, 1):
            w_keep(h, core).start()

    words = [pick(line, p) for line in STEPS]
    top[...] = jnp.full_like(top, NEG)
    total[...] = jnp.zeros_like(total)
    accum[...] = jnp.zeros_like(accum)
    proj[...] = jnp.zeros_like(proj)

    keep_mask.wait()
    swap_mask.wait_recv()
    for s in range(16):
        for b in range(4):
            for core in (0, 1):
                if s == 0 and b < 2:
                    row = jnp.full((2, BLOCK), NEG, jnp.float32)
                else:
                    wide = jnp.broadcast_to(masks[core, :, 4 * s + b : 4 * s + b + 1], (2, BLOCK))
                    row = jnp.where(wide > 0, 0.0, NEG).astype(jnp.float32)
                bias[s, core, b // 2, :, (b % 2) * BLOCK : (b % 2 + 1) * BLOCK] = row
    bias[16] = jnp.zeros_like(bias[16])

    def attend(slot, h, source, frame, half):
        rows = pl.ds(pl.multiple_of(frame * FRAME, FRAME), FRAME)
        held = pl.ds(pl.multiple_of(half * FRAME, FRAME), FRAME)
        keys = kv[slot, 0, h, held, :]
        values = kv[slot, 1, h, held, :]
        scores = lax.dot_general(
            qs[h, rows, :], keys, (((1,), (1,)), ((), ())), preferred_element_type=jnp.float32
        )
        added = bias[source, frame, half]
        scores = (scores * EXP2_SCALE).reshape(2, BLOCK, FRAME) + added[:, None, :]
        scores = scores.reshape(FRAME, FRAME)
        before = top[h, rows, :]
        now = jnp.maximum(before, jnp.max(scores, axis=1, keepdims=True))
        weights = jnp.exp2(scores - now)
        factor = jnp.exp2(before - now)
        total[h, rows, :] = total[h, rows, :] * factor + jnp.sum(weights, axis=1, keepdims=True)
        mixed = jnp.dot(weights.astype(jnp.bfloat16), values, preferred_element_type=jnp.float32)
        accum[h, rows, :] = accum[h, rows, :] * factor + mixed
        top[h, rows, :] = now

    def att_copy(h, dz, cross):
        core = 1 - c if cross else c
        rows = twin_rows if cross else my_rows
        return remote(
            attended.at[h, rows, :], att.at[h, z * 2 + c], att_send.at[h, dz, cross], att_recv.at[h, dz, cross],
            (p * 2 + core, (z + dz) % 4),
        )

    def project(h):
        for dz in range(4):
            for cross in (0, 1):
                if dz or cross:
                    att_copy(h, dz, cross).wait_recv()
        for dz in (1, 2, 3):
            w_pass(h, dz).wait_recv()
        for core in (0, 1):
            w_keep(h, core).wait()
        for n in range(3):
            cols = slice(n * 256, (n + 1) * 256)
            part = proj[:, cols]
            for pair in range(4):
                left = jnp.concatenate([att[h, 2 * pair], att[h, 2 * pair + 1]], axis=1)
                right = jnp.concatenate([wts[h, 2 * pair, :, cols], wts[h, 2 * pair + 1, :, cols]], axis=0)
                part = part + jnp.dot(left, right, preferred_element_type=jnp.float32)
            proj[:, cols] = part

    def passed(word, direction, anchor):
        slot = word & 15
        h = (word >> 4) & 3
        which = (word >> 6) & 1
        there = neighbours[direction]
        if anchor:
            return remote(
                kv.at[slot, which, h, 0:FRAME, :], kv.at[8, which, h, 0:FRAME, :],
                kv_send.at[8, which, h, direction], kv_recv.at[8, which, h], (there * 2 + c, z),
            )
        target = slot_of(((word >> 18) & 15) - there)
        return remote(
            kv.at[slot, which, h], kv.at[target, which, h],
            kv_send.at[slot, which, h, direction], kv_recv.at[target, which, h], (there * 2 + c, z),
        )

    def each_passed(word, action):
        for anchor in (False, True):
            @pl.when(((word >> (11 if anchor else 7)) & 15) > 0)
            def _():
                for direction in range(4):
                    @pl.when(((word >> (direction + (11 if anchor else 7))) & 1) == 1)
                    def _():
                        action(passed(word, direction, anchor))

    def start(copy):
        copy.start()

    def finish(copy):
        copy.wait_send()

    def step(n, recent):
        word = pick(words, n)
        slot = word & 15
        h = (word >> 4) & 3
        which = (word >> 6) & 1

        @pl.when(slot < 15)
        def _():
            first = kv.at[slot, which, h, 0:FRAME, :]
            whole = kv.at[slot, which, h]
            own = kv.at[0, which, h, my_rows, :]

            @pl.when((slot > 0) & (slot < 8))
            def _():
                remote(whole, whole, kv_send.at[0, 0, 0, 0], kv_recv.at[slot, which, h], twin).wait_recv()

            @pl.when((slot == 0) | (slot == 8))
            def _():
                remote(first, first, kv_send.at[0, 0, 0, 0], kv_recv.at[slot, which, h], twin).wait_recv()

            @pl.when(slot == 0)
            def _():
                pltpu.make_async_copy(own, own, kv_local.at[which, h]).wait()

            each_passed(word, start)

            @pl.when((slot == 0) & (which == 1))
            def _():
                keep_q(h).wait()
                swap_q(h).wait_recv()

            @pl.when(((word >> 15) & 1) == 1)
            def _():
                source = (word >> 18) & 15
                attend(slot, h, source, 0, 0)
                attend(slot, h, source, 1, 1)

                @pl.when(slot < 2)
                def _():
                    attend(slot, h, source, 0, 1)

                @pl.when((slot == 0) | (slot == 2))
                def _():
                    attend(slot, h, source, 1, 0)

            @pl.when(((word >> 17) & 1) == 1)
            def _():
                attend(slot, h, 16, 0, 0)
                attend(slot, h, 16, 1, 0)

            @pl.when(((word >> 16) & 1) == 1)
            def _():
                attended[h] = (accum[h] / total[h]).astype(jnp.bfloat16)
                for dz in (1, 3, 2, 0):
                    for cross in (0, 1):
                        if dz or cross:
                            att_copy(h, dz, cross).start()
                att[h, z * 2 + c] = attended[h, my_rows, :]

        for h_w in range(HEADS_CORE):
            @pl.when(n == W_STEPS[h_w])
            def _():
                for dz in (1, 3, 2):
                    w_copy(h_w, dz).wait_recv()
                    w_pass(h_w, dz).start()

        each_passed(recent[0], finish)
        return recent[1:] + (word,)

    recent = lax.fori_loop(0, COUNT, step, (jnp.int32(15),) * LAG)
    for h in range(HEADS_CORE):
        project(h)
    out_ref[...] = proj[...].astype(jnp.bfloat16)

    for word in recent:
        each_passed(word, finish)
    for h in range(HEADS_CORE):
        for which in (0, 1):
            swap_kv(h, which).wait_send()
        swap_q(h).wait_send()
        for dz in range(4):
            if dz:
                w_copy(h, dz).wait_send()
                w_pass(h, dz).wait_send()
            for cross in (0, 1):
                if dz or cross:
                    att_copy(h, dz, cross).wait_send()
    swap_mask.wait_send()


def body(queries, keys, values, block_mask, w_out):
    bf16, f32, dma = jnp.bfloat16, jnp.float32, pltpu.SemaphoreType.DMA
    heads = HEADS_CORE
    anywhere = pl.BlockSpec(memory_space=pl.ANY)
    return pl.pallas_call(
        kernel,
        out_shape=jax.ShapeDtypeStruct((FRAME, 768), bf16),
        in_specs=[anywhere, anywhere, anywhere, pl.BlockSpec(memory_space=pltpu.VMEM), anywhere],
        out_specs=pl.BlockSpec(memory_space=pltpu.VMEM),
        scratch_shapes=[
            pltpu.VMEM((9, 2, heads, 2 * FRAME, HEAD_DIM), bf16),
            pltpu.VMEM((heads, 2 * FRAME, HEAD_DIM), bf16),
            pltpu.VMEM((2, 2, 64), jnp.int32),
            pltpu.VMEM((17, 2, 2, 2, FRAME), f32),
            pltpu.VMEM((heads, 8, HEAD_DIM, 768), bf16),
            pltpu.VMEM((heads, 8, FRAME, HEAD_DIM), bf16),
            pltpu.VMEM((heads, 2 * FRAME, HEAD_DIM), bf16),
            pltpu.VMEM((heads, 2 * FRAME, 1), f32),
            pltpu.VMEM((heads, 2 * FRAME, 1), f32),
            pltpu.VMEM((heads, 2 * FRAME, HEAD_DIM), f32),
            pltpu.VMEM((FRAME, 768), f32),
            dma((9, 2, heads)), dma((9, 2, heads, 4)), dma((heads,)), dma((heads,)), dma((2, heads)), dma((3, heads)),
            dma((heads, 3)), dma((heads, 3)), dma((heads, 2)), dma((heads, 3)), dma((heads, 3)),
            dma((heads, 4, 2)), dma((heads, 4, 2)), dma((3,)),
        ],
        compiler_params=pltpu.CompilerParams(
            collective_id=0, has_side_effects=True, vmem_limit_bytes=VMEM_LIMIT
        ),
        name="radial_attention",
    )(queries, keys, values, block_mask, w_out)


def solution(mesh):
    placed = (P("ctx", "head"), P("ctx", "head"), P("ctx", "head"), P("ctx", None), P("head", None))
    return jax.shard_map(
        body, mesh=mesh, in_specs=placed, out_specs=P("ctx", "head"), check_vma=False
    )
```

```python
import jax
import jax.numpy as jnp
from jax import lax
from jax.experimental import pallas as pl
from jax.experimental.pallas import tpu as pltpu
from jax.sharding import PartitionSpec as P

HEAD_DIM = 128
BLOCK = 128
FRAME = 256
HEADS_CORE = 3
MESH = pl.DeviceIdType.MESH
NEG = -1e30
EXP2_SCALE = HEAD_DIM ** (-0.5) * 1.4426950408889634

STEPS = (
    (21120, 263808, 525952, 787584, 1049344, 1311616, 1574528, 1836160, 2097920, 2360064, 2622592, 2884736, 3146496, 3409152, 3671808, 3933440),
    (704, 262848, 526016, 787648, 1049280, 1312704, 1574208, 1836480, 2097984, 2360768, 2623296, 2885056, 3146560, 3409728, 3671872, 3933504),
    (131081, 262153, 524297, 2056, 1048585, 1310729, 1572873, 1835017, 2097161, 2359305, 2621449, 2883593, 8, 3407881, 3670025, 3932169),
    (263170, 6657, 262145, 786441, 133, 262277, 524421, 786565, 3145990, 1310853, 1572997, 1835653, 3145737, 3146241, 2621573, 2884229),
    (1049862, 524290, 787458, 524801, 2098438, 1049089, 1311233, 1573377, 1048773, 2097665, 2359809, 3932422, 3408898, 3671042, 3933186, 3670017),
    (131097, 1310726, 1573190, 1835334, 1310786, 1572866, 1836034, 2883910, 2360386, 2622466, 2884610, 2621505, 3145753, 2359493, 3408449, 3932185),
    (131113, 262169, 524313, 786457, 1048601, 2359558, 2621766, 1835033, 2097177, 3408134, 3670278, 2883609, 3145769, 3407897, 3670041, 3932201),
    (656, 262185, 524329, 786473, 1048617, 1310745, 1572889, 1835049, 2097193, 2359321, 2621465, 2883625, 3440706, 3407913, 3670057, 2916933),
    (17104, 170561, 295489, 557633, 180421, 1310761, 1572905, 819909, 3179846, 2359337, 2621481, 1868357, 3146512, 3179073, 3966018, 3702849),
    (524420, 557122, 820290, 787600, 2131270, 295109, 557253, 1836432, 2097936, 1343685, 2917442, 3965254, 3146576, 3703874, 3671312, 3933456),
    (2097415, 1343558, 525968, 787664, 1049360, 1081921, 1344065, 1836496, 2098128, 2130497, 3703110, 2884752, 2883585, 3409168, 3671888, 3933520),
    (557252, 263824, 525008, 2883719, 1049424, 1606722, 1868866, 8, 16391, 2655298, 2623120, 2884816, 1048775, 3409232, 1572999, 3409155),
    (2130247, 263376, 2621575, 2916423, 1572996, 2392134, 1573776, 1311491, 1835521, 3440966, 2623440, 2360067, 1081607, 8200, 3145987, 1835079),
    (1082438, 2359367, 2654535, 262147, 3145735, 1312656, 1574864, 2098178, 2622596, 2361232, 524295, 2393411, 3670020, 1310727, 1605959, 1867911),
    (262162, 786564, 3, 295491, 787009, 1311568, 3670023, 3932167, 172103, 2360656, 2097155, 786439, 2916929, 3932164, 3178563, 3440963),
    (4768, 2392327, 786450, 1835286, 16533, 10248, 1048835, 149576, 1868353, 262151, 557127, 3146818, 2097365, 147528, 2621589, 2884245),
    (10, 6673, 176195, 1048578, 3178567, 1835012, 1836050, 1343811, 3147030, 2883716, 2130243, 819271, 3702852, 1343559, 3933202, 3670097),
    (736, 884804, 1605638, 4184, 1606852, 3407879, 3702855, 3964999, 2654404, 2097681, 3670294, 2621969, 2097157, 3145745, 12296, 3933472),
    (1049878, 1310742, 1572886, 524817, 1049376, 131144, 1081667, 787093, 2098080, 294983, 2884626, 3932438, 3146528, 3964996, 2654277, 10),
    (360514, 263840, 525472, 1867782, 10, 1867844, 524437, 2129986, 10, 2916420, 2623392, 8, 10, 3408672, 3671328, 3933536),
    (296018, 10, 10, 787616, 1049440, 1049105, 1574688, 1836448, 2098016, 3408150, 10, 2883744, 3146592, 10, 10, 2917077),
    (2097239, 262880, 526048, 10, 1343490, 3440711, 10, 10, 1572867, 2360736, 2622944, 10, 2621443, 3409248, 3670880, 8),
    (1082710, 170577, 820306, 787680, 180437, 262293, 1574240, 1836512, 2392066, 10, 1573013, 2884832, 3408914, 2392069, 2654421, 1835031),
    (524436, 524306, 262673, 1868118, 2098454, 1312672, 1868882, 1573393, 3179862, 2361184, 2359825, 1835541, 2129989, 2359445, 3966034, 16472),
    (262178, 1343830, 1605718, 557649, 1311762, 10, 2621526, 2359300, 2359314, 2130513, 3703126, 2654801, 2883601, 3179089, 139336, 2884261),
    (1049894, 2593, 2621591, 2883735, 786961, 1312736, 1310737, 819925, 26647, 1310869, 2916434, 3965270, 2654275, 3671058, 3506177, 3670625),
    (557780, 525346, 19, 1081410, 524291, 1572946, 557269, 16408, 2621588, 2621458, 1605845, 2654209, 40, 8216, 2621477, 3409171),
    (525476, 2359319, 787490, 1310724, 2131030, 1081937, 2097156, 1606225, 1081349, 3440982, 2097171, 1868373, 3441746, 2883587, 3408417, 196680),
    (26, 1310758, 1048580, 131144, 1310754, 2359318, 2129988, 2392132, 2393170, 8, 3146244, 3407876, 196680, 2981955, 3933218, 1867863),
    (1082726, 168545, 2654295, 2916567, 1573524, 295125, 1344081, 2916358, 1671235, 1835011, 2392129, 2621473, 2916945, 135256, 2654437, 2917093),
    (2195735, 558178, 262689, 1049618, 557123, 1835156, 2654214, 1671233, 1835025, 2654290, 524311, 3146770, 2097189, 3703890, 3145811, 3442003),
    (557284, 1343590, 820322, 1409092, 3145751, 786499, 2120, 131160, 3147046, 3408166, 2359393, 131144, 1048855, 2359333, 4120, 26),
    (2097191, 26, 1146948, 524385, 1343586, 2392406, 196616, 3932183, 2360354, 131144, 1605701, 3440708, 24, 3145761, 26, 3408675),
    (2130279, 786644, 26, 2883751, 26, 885763, 3670039, 1572897, 165975, 262167, 3178564, 2359571, 3408994, 3932180, 3966050, 133144),
    (42, 2392407, 295521, 26, 819281, 24, 524453, 786597, 2654420, 2883732, 8, 3179602, 2884129, 1311063, 1572887, 3442019),
    (360546, 557138, 1573158, 263251, 165, 1573922, 1835042, 2098194, 26, 3440998, 557143, 786455, 26, 1343511, 131160, 3768337),
    (15, 786596, 1048596, 1835046, 2098470, 1049121, 1048595, 26, 3178854, 1933379, 26, 26, 1081687, 26, 1605719, 1835047),
    (15, 2359335, 2621543, 294931, 884737, 3407895, 26, 3965015, 2393186, 1310885, 2130003, 2072, 2621459, 3179105, 3407889, 1867879),
    (15, 819300, 165971, 1082450, 1605844, 26, 2621734, 1311571, 1572883, 8280, 2884706, 3932454, 3671060, 3671074, 3146083, 42),
    (15, 42, 1605990, 1868134, 172261, 262309, 557285, 819941, 1868369, 26, 196680, 3244034, 3670628, 16488, 1573159, 3702817),
    (15, 884756, 294993, 2916583, 2131302, 1606754, 1868898, 1343763, 1048597, 2622498, 3670310, 1835685, 131160, 2883603, 3178515, 4136),
    (15, 2457959, 14371, 262179, 1573028, 1081953, 1311265, 2359316, 2621604, 2097697, 8280, 2393427, 1048871, 2916691, 3506257, 196712),
    (15, 15, 2654247, 1049634, 1343570, 2359590, 24, 2883606, 8231, 1343717, 3145876, 3965286, 3702868, 3965012, 1605991, 15),
    (15, 15, 1146964, 1310804, 524307, 295141, 2654310, 2131026, 1081429, 1343573, 524327, 1868389, 2916449, 1310759, 42, 15),
    (15, 15, 42, 131096, 3178583, 1867860, 2654230, 3932199, 1835553, 2655330, 3703142, 131160, 2654291, 2883875, 16424, 15),
    (15, 15, 178275, 295523, 1606884, 786707, 1344097, 2916438, 2655460, 2130529, 2097187, 3146786, 1081703, 3932196, 3440737, 15),
    (15, 15, 1048612, 557089, 787041, 2392422, 2097172, 1311011, 1671251, 294999, 131096, 3407892, 3703844, 2457685, 135272, 15),
    (15, 15, 1146980, 1409044, 622675, 131160, 3702871, 2098210, 1048613, 131096, 3178580, 819287, 3440674, 1343591, 3244067, 15),
    (15, 15, 15, 42, 42, 40, 131160, 2457684, 42, 2883812, 557159, 2360611, 2195477, 3702882, 15, 15),
    (15, 15, 15, 4136, 3145767, 1835108, 1081427, 2883622, 1868385, 2916436, 2130019, 42, 42, 42, 15, 15),
    (15, 15, 15, 1082466, 524323, 1605650, 2195540, 42, 188519, 1835027, 2457681, 3506260, 131176, 3965028, 15, 15),
    (15, 15, 15, 1310756, 3178599, 3440727, 3670055, 1343843, 1081445, 1933395, 42, 786471, 2621475, 2916451, 15, 15),
    (15, 15, 15, 137320, 557155, 131176, 42, 2131042, 1572899, 42, 3146340, 2392419, 2654307, 131112, 15, 15),
    (15, 15, 15, 1409124, 884769, 884819, 10280, 3965031, 1671267, 40, 3178660, 3407908, 2195557, 2457701, 15, 15),
    (15, 15, 15, 15, 15, 42, 1048611, 2916454, 15, 2916900, 1572901, 819303, 15, 15, 15, 15),
    (15, 15, 15, 15, 15, 3407911, 2097188, 1605729, 15, 262183, 40, 2654305, 15, 15, 15, 15),
    (15, 15, 15, 15, 15, 787491, 3702887, 40, 15, 1835299, 2916386, 3440740, 15, 15, 15, 15),
    (15, 15, 15, 15, 15, 819299, 131176, 2359332, 15, 295015, 2392097, 3178594, 15, 15, 15, 15),
    (15, 15, 15, 15, 15, 3440743, 1081443, 131176, 15, 1867875, 1605733, 104, 15, 15, 15, 15),
    (15, 15, 15, 15, 15, 1933348, 2195556, 2457700, 15, 196712, 196712, 196648, 15, 15, 15, 15),
)
COUNT = len(STEPS)
LAG = 12
VMEM_LIMIT = 60 * 1024 * 1024


def pick(values, p):
    values = list(values)
    while len(values) & (len(values) - 1):
        values.append(values[-1])
    bit = 1
    while len(values) > 1:
        odd = (p // bit) % 2 == 1
        values = [jnp.where(odd, b, a) for a, b in zip(values[::2], values[1::2])]
        bit *= 2
    return values[0]


def kernel(
    q_ref, k_ref, v_ref, mask_ref, w_ref, out_ref,
    kv, qs, masks, bias, wts, att, attended, top, total, accum, proj,
    kv_recv, kv_send, own_send, first_send, q_recv, q_local, kv_local, swap_send,
    w_recv, w_send, w_local, w_pass_recv, w_pass_send, att_recv, att_send, mask_sem,
):
    i = lax.axis_index("ctx")
    z = lax.axis_index("head")
    c = i % 2
    p = i // 2
    x = p // 4
    y = p % 4
    twin = (p * 2 + 1 - c, z)
    neighbours = (((x + 1) % 4) * 4 + y, ((x + 3) % 4) * 4 + y, x * 4 + (y + 1) % 4, x * 4 + (y + 3) % 4)

    def slot_of(delta):
        slot = jnp.where(delta == -2, 3, jnp.where(delta == 2, 4, 7))
        slot = jnp.where(delta == -1, 1, jnp.where(delta == 1, 2, slot))
        return jnp.where(delta == -4, 5, jnp.where(delta == 4, 6, slot))

    def remote(src, dst, send, recv, device):
        return pltpu.make_async_remote_copy(
            src_ref=src, dst_ref=dst, send_sem=send, recv_sem=recv, device_id=device, device_id_type=MESH
        )

    barrier = pltpu.get_barrier_semaphore()
    greeted = [(there * 2 + core, z) for there in neighbours for core in (0, 1)] + [twin]
    for dz in (1, 2, 3):
        greeted += [(i, (z + dz) % 4), (p * 2 + 1 - c, (z + dz) % 4)]
    for device in greeted:
        pl.semaphore_signal(barrier, inc=1, device_id=device, device_id_type=MESH)

    my_rows = pl.ds(pl.multiple_of(c * FRAME, FRAME), FRAME)
    twin_rows = pl.ds(pl.multiple_of((1 - c) * FRAME, FRAME), FRAME)

    def columns(core, h):
        return pl.ds(pl.multiple_of((HEADS_CORE * core + h) * HEAD_DIM, HEAD_DIM), HEAD_DIM)

    def swap_kv(h, which):
        ref = (k_ref, v_ref)[which]
        return remote(ref.at[:, columns(1 - c, h)], kv.at[0, which, h, my_rows, :], swap_send.at[which, h], kv_recv.at[0, which, h], twin)

    def swap_q(h):
        return remote(q_ref.at[:, columns(1 - c, h)], qs.at[h, my_rows, :], swap_send.at[2, h], q_recv.at[h], twin)

    def keep_kv(h, which):
        ref = (k_ref, v_ref)[which]
        return pltpu.make_async_copy(ref.at[:, columns(c, h)], kv.at[0, which, h, my_rows, :], kv_local.at[which, h])

    def keep_q(h):
        return pltpu.make_async_copy(q_ref.at[:, columns(c, h)], qs.at[h, my_rows, :], q_local.at[h])

    swap_mask = remote(mask_ref, masks.at[c], mask_sem.at[0], mask_sem.at[1], twin)
    keep_mask = pltpu.make_async_copy(mask_ref, masks.at[c], mask_sem.at[2])

    def w_block(h, core, zz):
        rows = pl.ds(pl.multiple_of((HEADS_CORE * core + h) * HEAD_DIM, HEAD_DIM), HEAD_DIM)
        return w_ref.at[rows, pl.ds(pl.multiple_of(zz * 768, 768), 768)]

    def w_copy(h, dz):
        zz = (z + dz) % 4
        return remote(w_block(h, c, zz), wts.at[h, z * 2 + c], w_send.at[h, dz - 1], w_recv.at[h, dz - 1], (i, zz))

    def w_keep(h, core):
        return pltpu.make_async_copy(w_block(h, core, z), wts.at[h, z * 2 + core], w_local.at[h, core])

    def w_pass(h, dz):
        place = ((z + 4 - dz) % 4) * 2 + c
        return remote(wts.at[h, place], wts.at[h, place], w_pass_send.at[h, dz - 1], w_pass_recv.at[h, dz - 1], twin)

    def own_copy(h, which, group, direction):
        there = neighbours[direction]
        ref = (k_ref, v_ref)[which]
        target = slot_of(p - there)
        core = c if group == 0 else 1 - c
        return remote(
            ref.at[:, columns(core, h)], kv.at[target, which, h, my_rows, :],
            own_send.at[group, which, h, direction], kv_recv.at[target, which, h], (there * 2 + core, z),
        )

    def own_first(h, which, group, direction):
        ref = (k_ref, v_ref)[which]
        there = neighbours[direction]
        return remote(
            ref.at[:, columns(group, h)], kv.at[8, which, h, 0:FRAME, :],
            first_send.at[group, which, h, direction], kv_recv.at[8, which, h], (there * 2 + group, z),
        )

    def each_own(word, which, action):
        h = (word >> 4) & 3
        for direction in range(4):
            @pl.when(((word >> (7 + direction)) & 1) == 1)
            def _():
                for group in (0, 1):
                    action(own_copy(h, which, group, direction))

        @pl.when((((word >> 11) & 15) > 0) & (c == 0))
        def _():
            for direction in range(4):
                @pl.when(((word >> (11 + direction)) & 1) == 1)
                def _():
                    for group in (0, 1):
                        action(own_first(h, which, group, direction))

    def start(copy):
        copy.start()

    def finish(copy):
        copy.wait_send()

    for h in range(HEADS_CORE):
        keep_q(h).start()
        keep_kv(h, 0).start()
        keep_kv(h, 1).start()
    keep_mask.start()
    words = [pick(line, p) for line in STEPS]
    pl.semaphore_wait(barrier, len(greeted))
    each_own(words[0], 0, start)
    swap_mask.start()
    for h in range(HEADS_CORE):
        swap_q(h).start()
        swap_kv(h, 0).start()
        swap_kv(h, 1).start()
        if h == 0:
            each_own(words[1], 1, start)
    for h in range(HEADS_CORE):
        for dz in (1, 3, 2):
            w_copy(h, dz).start()
    for h in range(HEADS_CORE):
        for core in (0, 1):
            w_keep(h, core).start()

    top[...] = jnp.full_like(top, NEG)
    total[...] = jnp.zeros_like(total)
    accum[...] = jnp.zeros_like(accum)
    proj[...] = jnp.zeros_like(proj)

    keep_mask.wait()
    swap_mask.wait_recv()
    blocks = masks.shape[2]
    same = lax.broadcasted_iota(jnp.int32, (blocks, blocks), 0) == lax.broadcasted_iota(jnp.int32, (blocks, blocks), 1)
    anchor_rows = lax.broadcasted_iota(jnp.int32, (blocks, BLOCK), 0) < FRAME // BLOCK
    for core in (0, 1):
        for b in (0, 1):
            line = jnp.where(same, jnp.broadcast_to(masks[core, b : b + 1, :], (blocks, blocks)), 0)
            column = jnp.sum(line.astype(jnp.float32), axis=1, keepdims=True)
            wide = jnp.broadcast_to(column, (blocks, BLOCK))
            added = jnp.where((wide > 0) & ~anchor_rows, 0.0, NEG).astype(jnp.float32)
            for n in range(blocks // 2):
                bias[core, n, :, b * BLOCK : (b + 1) * BLOCK] = added[2 * n : 2 * n + 2, :]
        bias[core, 32] = jnp.zeros_like(bias[core, 32])

    def attend(slot, h, source, parts):
        scores = []
        for frame, halves in parts:
            rows = slice(frame * FRAME, (frame + 1) * FRAME)
            held = slice(halves[0] * FRAME, (halves[-1] + 1) * FRAME)
            scores.append(lax.dot_general(
                kv[slot, 0, h, held, :], qs[h, rows, :], (((1,), (1,)), ((), ())), preferred_element_type=jnp.float32
            ))
        weights = []
        factors = []
        for (frame, halves), score in zip(parts, scores):
            rows = slice(frame * FRAME, (frame + 1) * FRAME)
            length = len(halves) * FRAME
            score = score * EXP2_SCALE
            if source is not None:
                added = [bias[frame, source * 2 + half] for half in halves]
                added = added[0] if len(added) == 1 else jnp.concatenate(added, axis=0)
                score = (score.reshape(length // BLOCK, BLOCK, FRAME) + added[:, None, :]).reshape(length, FRAME)
            before = top[h, :, rows]
            now = jnp.maximum(before, jnp.max(score, axis=0, keepdims=True))
            weight = jnp.exp2(score - now)
            factor = jnp.exp2(before - now)
            total[h, :, rows] = total[h, :, rows] * factor + jnp.sum(weight, axis=0, keepdims=True)
            top[h, :, rows] = now
            weights.append(weight.astype(jnp.bfloat16))
            factors.append(factor)
        for (frame, halves), weight, factor in zip(parts, weights, factors):
            rows = slice(frame * FRAME, (frame + 1) * FRAME)
            held = slice(halves[0] * FRAME, (halves[-1] + 1) * FRAME)
            mixed = lax.dot_general(
                kv[slot, 1, h, held, :], weight, (((0,), (0,)), ((), ())), preferred_element_type=jnp.float32
            )
            accum[h, :, rows] = accum[h, :, rows] * factor + mixed

    def att_copy(h, dz, cross):
        core = 1 - c if cross else c
        rows = twin_rows if cross else my_rows
        return remote(
            attended.at[h, rows, :], att.at[h, z * 2 + c], att_send.at[h, dz, cross], att_recv.at[h, dz, cross],
            (p * 2 + core, (z + dz) % 4),
        )

    def project(h):
        for dz in range(4):
            for cross in (0, 1):
                if dz or cross:
                    att_copy(h, dz, cross).wait_recv()
        for dz in (1, 2, 3):
            w_pass(h, dz).wait_recv()
        for core in (0, 1):
            w_keep(h, core).wait()
        for n in range(3):
            cols = slice(n * 256, (n + 1) * 256)
            part = proj[:, cols]
            for pair in range(4):
                left = jnp.concatenate([att[h, 2 * pair], att[h, 2 * pair + 1]], axis=1)
                right = jnp.concatenate([wts[h, 2 * pair, :, cols], wts[h, 2 * pair + 1, :, cols]], axis=0)
                part = part + jnp.dot(left, right, preferred_element_type=jnp.float32)
            proj[:, cols] = part

    def passed(word, direction, anchor):
        slot = word & 15
        h = (word >> 4) & 3
        which = (word >> 6) & 1
        there = neighbours[direction]
        if anchor:
            return remote(
                kv.at[slot, which, h, 0:FRAME, :], kv.at[8, which, h, 0:FRAME, :],
                kv_send.at[8, which, h, direction], kv_recv.at[8, which, h], (there * 2 + c, z),
            )
        target = slot_of(((word >> 18) & 15) - there)
        return remote(
            kv.at[slot, which, h], kv.at[target, which, h],
            kv_send.at[slot, which, h, direction], kv_recv.at[target, which, h], (there * 2 + c, z),
        )

    def each_passed(word, action):
        for anchor in (False, True):
            @pl.when(((word >> (11 if anchor else 7)) & 15) > 0)
            def _():
                for direction in range(4):
                    @pl.when(((word >> (direction + (11 if anchor else 7))) & 1) == 1)
                    def _():
                        action(passed(word, direction, anchor))

    def each_sent(word, action):
        slot = word & 15
        which = (word >> 6) & 1

        @pl.when((slot > 0) & (slot < 9))
        def _():
            each_passed(word, action)

        for kind in (0, 1):
            pl.when((slot == 0) & (which == kind))(lambda: each_own(word, kind, action))

    def step(n, recent):
        word = pick(words, n)
        slot = word & 15
        h = (word >> 4) & 3
        which = (word >> 6) & 1
        source = (word >> 18) & 15

        @pl.when((slot > 0) & (slot < 8))
        def _():
            whole = kv.at[slot, which, h]
            remote(whole, whole, kv_send.at[0, 0, 0, 0], kv_recv.at[slot, which, h], twin).wait_recv()

        @pl.when(slot == 8)
        def _():
            first = kv.at[8, which, h, 0:FRAME, :]
            remote(first, first, kv_send.at[0, 0, 0, 0], kv_recv.at[8, which, h], twin).wait_recv()

        @pl.when(n > 1)
        def _():
            each_sent(word, start)

        @pl.when(slot == 9)
        def _():
            keep_q(h).wait()
            swap_q(h).wait_recv()
            for kind in (0, 1):
                keep_kv(h, kind).wait()
                swap_kv(h, kind).wait_recv()
            attend(0, h, p, ((0, (0, 1)), (1, (0, 1))))

        @pl.when(((word >> 15) & 1) == 1)
        def _():
            @pl.when(slot == 1)
            def _():
                attend(1, h, source, ((0, (0, 1)), (1, (1,))))

            @pl.when(slot == 2)
            def _():
                attend(2, h, source, ((0, (0,)), (1, (0, 1))))

            @pl.when((slot > 2) & (slot < 8))
            def _():
                attend(slot, h, source, ((0, (0,)), (1, (1,))))

        @pl.when(((word >> 17) & 1) == 1)
        def _():
            attend(jnp.where(slot == 9, 0, slot), h, None, ((0, (0,)), (1, (0,))))

        @pl.when(((word >> 16) & 1) == 1)
        def _():
            attended[h] = jnp.transpose(accum[h] / total[h]).astype(jnp.bfloat16)
            for dz in (2, 1, 3, 0):
                for cross in (0, 1):
                    if dz or cross:
                        att_copy(h, dz, cross).start()
            att[h, z * 2 + c] = attended[h, my_rows, :]

        @pl.when(slot == 10)
        def _():
            for dz in (1, 3, 2):
                w_copy(h, dz).wait_recv()
                w_pass(h, dz).start()

        each_sent(recent[0], finish)
        return recent[1:] + (word,)

    recent = lax.fori_loop(0, COUNT, step, (jnp.int32(15),) * LAG)

    def finish_heads(heads):
        for h in heads:
            for dz in range(4):
                for cross in (0, 1):
                    if dz or cross:
                        att_copy(h, dz, cross).wait_send()

    project(0)
    project(1)
    for word in recent:
        each_sent(word, finish)
    for h in range(HEADS_CORE):
        for which in (0, 1):
            swap_kv(h, which).wait_send()
        swap_q(h).wait_send()
        for dz in (1, 2, 3):
            w_copy(h, dz).wait_send()
            w_pass(h, dz).wait_send()
    swap_mask.wait_send()
    finish_heads((0, 1))
    project(2)
    out_ref[...] = proj[...].astype(out_ref.dtype)
    finish_heads((2,))


def body(queries, keys, values, block_mask, w_out):
    bf16, f32, dma = jnp.bfloat16, jnp.float32, pltpu.SemaphoreType.DMA
    heads = HEADS_CORE
    anywhere = pl.BlockSpec(memory_space=pl.ANY)
    return pl.pallas_call(
        kernel,
        out_shape=jax.ShapeDtypeStruct((FRAME, 768), bf16),
        in_specs=[anywhere, anywhere, anywhere, pl.BlockSpec(memory_space=pltpu.VMEM), anywhere],
        out_specs=pl.BlockSpec(memory_space=pltpu.VMEM),
        scratch_shapes=[
            pltpu.VMEM((9, 2, heads, 2 * FRAME, HEAD_DIM), bf16),
            pltpu.VMEM((heads, 2 * FRAME, HEAD_DIM), bf16),
            pltpu.VMEM((2, 2, 64), jnp.int32),
            pltpu.VMEM((2, 33, 2, FRAME), f32),
            pltpu.VMEM((heads, 8, HEAD_DIM, 768), bf16),
            pltpu.VMEM((heads, 8, FRAME, HEAD_DIM), bf16),
            pltpu.VMEM((heads, 2 * FRAME, HEAD_DIM), bf16),
            pltpu.VMEM((heads, 1, 2 * FRAME), f32),
            pltpu.VMEM((heads, 1, 2 * FRAME), f32),
            pltpu.VMEM((heads, HEAD_DIM, 2 * FRAME), f32),
            pltpu.VMEM((FRAME, 768), f32),
            dma((9, 2, heads)), dma((9, 2, heads, 4)), dma((2, 2, heads, 4)), dma((2, 2, heads, 4)), dma((heads,)), dma((heads,)), dma((2, heads)), dma((3, heads)),
            dma((heads, 3)), dma((heads, 3)), dma((heads, 2)), dma((heads, 3)), dma((heads, 3)),
            dma((heads, 4, 2)), dma((heads, 4, 2)), dma((3,)),
        ],
        compiler_params=pltpu.CompilerParams(
            collective_id=0, has_side_effects=True, vmem_limit_bytes=VMEM_LIMIT
        ),
        name="radial_attention",
    )(queries, keys, values, block_mask, w_out)


def solution(mesh):
    placed = (P("ctx", "head"), P("ctx", "head"), P("ctx", "head"), P("ctx", None), P("head", None))
    return jax.shard_map(
        body, mesh=mesh, in_specs=placed, out_specs=P("ctx", "head"), check_vma=False
    )
```

```python
import functools

import jax
import jax.numpy as jnp
from jax import lax
from jax.experimental import pallas as pl
from jax.experimental.pallas import tpu as pltpu
from jax.sharding import PartitionSpec as P

HEAD_DIM = 128
BLOCK = 128
FRAME = 256
HEADS_CORE = 3
MESH = pl.DeviceIdType.MESH
NEG = -1e30
EXP2_SCALE = HEAD_DIM ** (-0.5) * 1.4426950408889634

ARRIVALS = (
    (15, 15, 15, 15, 15, 15, 15, 15, 15, 15, 15, 15, 15, 15, 15, 15),
    (0, 15, 15, 15, 15, 15, 15, 15, 15, 15, 15, 15, 15, 15, 15, 15),
    (16448, 262153, 524297, 2120, 1048585, 1310729, 1572873, 1835017, 2097161, 2359305, 2621449, 2883593, 3145737, 3407881, 3670025, 3932169),
    (131081, 262169, 524313, 786441, 1048601, 1310745, 1572889, 1835033, 2097177, 2359321, 2621465, 2883609, 3145753, 3407897, 3670041, 3932185),
    (131097, 15, 15, 786457, 15, 15, 15, 15, 15, 15, 15, 15, 15, 15, 15, 15),
    (131113, 262185, 524329, 786473, 1048617, 1310761, 1572905, 1835049, 2097193, 2359337, 2621481, 2883625, 3145769, 3407913, 3670057, 3932201),
    (1048582, 1310790, 1572870, 524353, 16389, 2359302, 2621446, 1572865, 1048645, 1310725, 1572885, 1835077, 2097157, 2359365, 2621509, 2883653),
    (262210, 4097, 262145, 1835014, 2097222, 262149, 524293, 2883590, 3145734, 3407878, 3670022, 3932166, 3407874, 3145793, 3407873, 3670017),
    (1048662, 524290, 786434, 557057, 1310722, 1572866, 1310721, 2883670, 2359362, 2621506, 2359297, 2621441, 2129989, 3670018, 3932162, 2916357),
    (262162, 1343494, 1605702, 1867846, 163909, 1048577, 1835074, 1605697, 3178566, 2097153, 2883586, 3964998, 3440706, 2359381, 2621461, 3702849),
    (16, 165953, 819266, 15, 2097238, 294981, 557125, 786501, 1048661, 1343557, 1572901, 1835029, 15, 3178497, 3964994, 15),
    (16464, 524306, 294977, 1835046, 1310802, 2359318, 2654278, 819205, 2392066, 3440710, 3702854, 2654273, 15, 3702850, 3440705, 15),
    (2097159, 15, 15, 15, 8213, 1081409, 1343553, 2120, 15, 2129985, 2392129, 15, 15, 15, 15, 15),
    (524356, 4113, 15, 15, 15, 1605698, 1867778, 15, 15, 2621458, 2916418, 15, 2097189, 15, 3407969, 2883605),
    (15, 15, 786450, 524305, 15, 15, 15, 131080, 3145814, 15, 15, 15, 3407890, 15, 15, 3670033),
    (1081366, 15, 1572950, 2883671, 2129942, 15, 15, 1572881, 2359378, 15, 15, 3932182, 2130021, 15, 15, 2916437),
    (294994, 2359367, 262225, 524321, 1343506, 15, 524309, 15, 15, 15, 15, 2621521, 3440722, 20488, 15, 3702865),
    (1048614, 1310806, 1572966, 2883655, 2097190, 15, 2621526, 1605713, 3178518, 15, 15, 1867861, 2883649, 2359397, 2654293, 1835015),
    (262178, 557138, 262241, 2916359, 1310754, 2392150, 1310737, 786453, 2359330, 1310741, 3670038, 3965014, 2916353, 3145745, 3932178, 10),
    (10, 1343510, 2621511, 10, 180309, 1048593, 1835090, 3932167, 2621444, 3407894, 2359313, 2621537, 10, 3670098, 3145795, 1867847),
    (15, 524386, 819282, 4184, 10, 1572946, 557141, 819285, 16391, 2097169, 2883602, 1835045, 1048583, 3178577, 3965010, 15),
    (4128, 168017, 10, 1048578, 786497, 1048673, 1867794, 10, 10, 2654290, 3702870, 3145730, 1081415, 2392101, 2621541, 1835047),
    (15, 10, 2621463, 2916375, 819201, 2359334, 2654230, 3964999, 1835025, 3440726, 2916434, 10, 1048663, 3702802, 1572871, 3407875),
    (4192, 33, 15, 1048658, 8229, 1605650, 1310753, 2097218, 163911, 1310757, 2392145, 2359363, 15, 1310791, 10, 3440707),
    (15, 15, 2654215, 262147, 15, 262165, 10, 2097234, 15, 2097249, 524295, 2120, 8, 10, 1605703, 1835031),
    (524324, 2359399, 15, 294979, 3145735, 2120, 15, 15, 15, 2621474, 10, 15, 2621443, 12312, 15, 2883685),
    (557060, 2392071, 786530, 262163, 1572868, 10, 15, 15, 18455, 10, 557127, 15, 3670020, 1343495, 15, 3407891),
    (2129991, 786436, 10243, 1081362, 3178567, 294997, 15, 1310723, 3145830, 2129953, 15, 15, 2883601, 15, 3145747, 16472),
    (2097239, 557090, 2654295, 26, 1605700, 8216, 524325, 15, 2654276, 15, 15, 2392067, 3670036, 3932164, 1572887, 3440723),
    (524308, 2359319, 170051, 131080, 2129926, 15, 3670023, 1343555, 3178534, 15, 15, 3932198, 3702852, 3145761, 3932194, 15),
    (15, 557122, 2621543, 294995, 15, 15, 1048579, 786469, 2621460, 2883588, 3670054, 3965030, 24, 3178593, 2654245, 8264),
    (15, 163937, 819234, 1310724, 1572884, 15, 1835106, 3932183, 1867857, 12296, 2097155, 786439, 40, 3964996, 3965026, 26),
    (1081414, 15, 15, 262243, 786449, 1081377, 557157, 819301, 190551, 262151, 2883618, 2359315, 155752, 131160, 4120, 3670049),
    (15, 15, 1048660, 1343556, 524355, 15, 3702855, 16472, 1081349, 2654306, 3702886, 819271, 26, 1310807, 1605719, 3702881),
    (15, 2392151, 1048580, 1835030, 15, 3407879, 1867810, 3965015, 2621540, 3407910, 2916450, 133128, 1081367, 1343511, 1572967, 1867863),
    (360450, 26, 26, 2883687, 1605716, 1835076, 1081411, 2129938, 26, 294983, 2129987, 3178562, 1048615, 26, 1605671, 196616),
    (26, 786452, 8211, 133144, 26, 3440711, 2097236, 1310803, 2654292, 2654210, 524311, 2392147, 3702868, 3932180, 15, 2916389),
    (557140, 884820, 163923, 1048610, 3145751, 262181, 24, 26, 8231, 131144, 557143, 1867781, 2916433, 3965012, 15, 18536),
    (557156, 1310758, 1605654, 1146946, 3178583, 1867780, 8, 1343507, 1835041, 3440742, 3145732, 3145810, 3407906, 2883651, 26, 3407971),
    (2195479, 1343590, 1146948, 1310804, 1343586, 2392134, 15, 1572897, 2654244, 24, 15, 26, 2097237, 2916355, 20552, 196632),
    (1081446, 786532, 2654247, 1343508, 163941, 15, 131144, 2359364, 15, 1835027, 15, 2072, 131144, 2392069, 2654213, 3440675),
    (2097191, 819236, 294929, 1867862, 1343554, 8232, 26, 2916422, 2392082, 15, 26, 786455, 131160, 2392085, 3145763, 42),
    (295010, 884804, 1605670, 42, 819281, 786499, 3670039, 2916374, 1572867, 15, 1572869, 3407876, 2719811, 4200, 3178595, 1867879),
    (15, 2457639, 12323, 622673, 622595, 15, 147544, 2392068, 2392162, 26, 2056, 819287, 2883681, 2883603, 131160, 196648),
    (42, 42, 165987, 4136, 2130022, 15, 3702871, 2195458, 1835009, 15, 524327, 131160, 2621459, 3932196, 3178499, 15),
    (15, 15, 42, 131176, 1572964, 26, 1048595, 2097186, 15, 2883604, 2097171, 3506244, 3670052, 196680, 196616, 15),
    (2195559, 15, 1146900, 2916391, 524307, 15, 2621542, 2359316, 1605699, 2916436, 1605701, 3178514, 42, 3965028, 3407889, 15),
    (15, 15, 1048612, 294947, 3145767, 295013, 1048675, 2088, 1933377, 262167, 24, 3407892, 2129941, 2981971, 3440721, 15),
    (15, 15, 1081444, 557153, 42, 1835092, 8232, 2392148, 1081365, 1835075, 2359393, 1867877, 2719827, 1310759, 15, 15),
    (15, 15, 360481, 1081442, 786465, 1572962, 1081427, 196632, 1048613, 1343573, 557159, 2654225, 2621475, 42, 15, 15),
    (15, 15, 15, 1867878, 622675, 131080, 2129940, 42, 42, 139352, 3178564, 2359395, 3702884, 1343591, 42, 15),
    (15, 15, 15, 1310756, 1605668, 3407895, 2097156, 1310755, 1572883, 1867859, 15, 786471, 1081447, 2883619, 104, 15),
    (15, 15, 15, 1409124, 3178599, 884739, 2195524, 2883686, 1671251, 2883620, 15, 42, 3440738, 131112, 131112, 15),
    (15, 15, 15, 15, 819297, 3440727, 1409105, 1343587, 15, 15, 2130003, 3506260, 2654307, 2916451, 3244115, 15),
    (15, 15, 15, 15, 524323, 1835108, 1081379, 3932199, 1867873, 2088, 3145812, 15, 2981921, 3670050, 3506209, 15),
    (15, 15, 15, 15, 622691, 131160, 42, 3965031, 163943, 15, 196680, 2392099, 15, 3768418, 15, 15),
    (15, 15, 15, 15, 15, 15, 1343585, 2130018, 1572963, 2916420, 2097251, 819303, 15, 15, 15, 15),
    (15, 15, 15, 15, 15, 15, 155752, 131176, 1081445, 1933315, 3178516, 16424, 15, 15, 15, 15),
    (15, 15, 15, 15, 15, 786451, 2097188, 1605729, 1671203, 294999, 1605717, 3145826, 15, 15, 15, 15),
    (15, 15, 15, 15, 15, 1867796, 2654246, 2916390, 15, 1835043, 196696, 3407972, 15, 15, 15, 15),
    (15, 15, 15, 15, 15, 3407911, 3670055, 2359396, 15, 139368, 42, 3440676, 15, 15, 15, 15),
    (15, 15, 15, 15, 15, 819283, 3702887, 2457636, 15, 42, 2392097, 131176, 15, 15, 15, 15),
    (15, 15, 15, 15, 15, 42, 2195556, 15, 15, 2195537, 8296, 3178530, 15, 15, 15, 15),
    (15, 15, 15, 15, 15, 1146961, 15, 15, 15, 15, 3145764, 2719777, 15, 15, 15, 15),
    (15, 15, 15, 15, 15, 786531, 15, 15, 15, 262183, 1605733, 15, 15, 15, 15, 15),
    (15, 15, 15, 15, 15, 2392166, 15, 15, 15, 1343589, 2129955, 15, 15, 15, 15, 15),
    (15, 15, 15, 15, 15, 3440743, 15, 15, 15, 295015, 131112, 15, 15, 15, 15, 15),
    (15, 15, 15, 15, 15, 131176, 15, 15, 15, 1867875, 3244132, 15, 15, 15, 15, 15),
    (15, 15, 15, 15, 15, 819235, 15, 15, 15, 2981988, 15, 15, 15, 15, 15, 15),
    (15, 15, 15, 15, 15, 1867812, 15, 15, 15, 15, 15, 15, 15, 15, 15, 15),
    (15, 15, 15, 15, 15, 1671202, 15, 15, 15, 15, 15, 15, 15, 15, 15, 15),
)
SENDS = (
    (266354560, 67125120, 540544, 2097056, 266338336, 4096, 8, 69189664, 266342400, 67108896, 67108896, 2080800, 266862719, 127, 127, 2080895),
    (266878880, 17317792, 16793504, 69205888, 266867752, 84410400, 67637264, 2084872, 266867744, 525352, 17305608, 69194752, 266342527, 67637375, 67637375, 69193855),
    (268435455, 268435455, 268435455, 268435455, 268435455, 268435455, 268435455, 268435455, 268435455, 268435455, 268435455, 268435455, 268435455, 268435455, 268435455, 268435455),
    (268435455, 268435455, 268435455, 268435455, 268435455, 268435455, 268435455, 268435455, 268435455, 268435455, 268435455, 268435455, 268435455, 268435455, 268435455, 268435455),
    (266485640, 84557704, 84033416, 268435455, 266470527, 16913416, 84022399, 85968936, 266470416, 84022320, 84546600, 18874248, 266474623, 17564799, 84018303, 18859135),
    (267009960, 34357160, 100941736, 18874248, 267126911, 33817616, 17438847, 18874256, 267126832, 34211856, 34341936, 85983144, 266994815, 85972095, 17437823, 85972095),
    (14664575, 268424063, 268419967, 84443048, 268435333, 268435455, 268435455, 268435455, 268435455, 268435455, 268435455, 268435455, 268435333, 268435365, 268435365, 266960805),
    (268435455, 268435455, 268435455, 268419967, 81788927, 268435455, 268435333, 268435455, 14680063, 268435455, 268435455, 268419967, 268435455, 266895359, 268435455, 268435455),
    (98555775, 268435455, 268435455, 268435455, 268435455, 268435455, 268435455, 268425087, 73400319, 268435455, 268435455, 266371071, 268435455, 268435455, 268435455, 266436485),
    (268435344, 268435455, 268424063, 268424063, 268435365, 268435455, 268435455, 268435455, 268435455, 268435455, 268435455, 268424063, 268435455, 268435455, 268435341, 268435455),
    (266616831, 268435455, 268435455, 102760447, 98566143, 268435455, 268435365, 266960895, 268435455, 268435455, 268435455, 266567679, 266606719, 268435455, 268435455, 35637375),
    (268435455, 268435455, 268435455, 268435455, 268435455, 268435455, 268435455, 266436607, 268435455, 268435455, 268435455, 268435455, 268421247, 268435455, 268435455, 268425343),
    (268435455, 4227071, 4226960, 268435344, 266605439, 268435455, 268435455, 268435455, 266601253, 268435455, 268435455, 35651469, 267141119, 268421247, 4212863, 102760447),
    (268435455, 268435455, 34111408, 268422015, 268425087, 268435455, 268435455, 102760325, 268424063, 268435455, 268435455, 268435376, 268435455, 6291455, 268435455, 266567565),
    (266944391, 266895359, 268435455, 35651504, 268435341, 266355461, 71320447, 35651583, 268435455, 266355461, 266355469, 102760447, 23068671, 268425343, 268425343, 266502143),
    (268435455, 23068560, 268425087, 268435455, 268435455, 6291455, 4751359, 268435455, 268435455, 73400319, 6291455, 268420991, 268435455, 73400319, 266895359, 268435455),
    (268435455, 268435455, 268435455, 266633215, 268435455, 266880805, 268435455, 268435365, 81788927, 266883967, 268423952, 268435455, 90177535, 268435455, 73400319, 268435455),
    (268420991, 268425087, 268426111, 268435455, 31457279, 73400319, 268424973, 268435455, 268435455, 23068671, 102760447, 267091967, 268435455, 268435381, 268435455, 268435455),
    (268422015, 268435455, 268435455, 268435455, 90177535, 268435455, 268435455, 266502143, 98566143, 268435455, 268435455, 268425087, 268435455, 266502143, 268435455, 268435455),
    (268435455, 268420903, 268435455, 268435455, 268435373, 268435455, 268435455, 266567679, 266420100, 268435455, 266502143, 267157503, 268435455, 268435455, 268435455, 268435455),
    (21774244, 268435455, 268435455, 268435455, 268435455, 268435455, 268435455, 268435455, 268435455, 268435455, 268435455, 268435455, 268435455, 268435455, 268435455, 268420095),
    (268435455, 268435455, 268435455, 268435455, 266895359, 268435455, 268435373, 268435455, 268435455, 268435455, 268435455, 268435455, 268435367, 268435455, 268435381, 268435455),
    (31457279, 268435455, 268435455, 268435367, 268435455, 268435455, 268435455, 268435455, 266502143, 268435455, 268435455, 268435455, 266879999, 268435455, 268435455, 267076095),
    (268435455, 88244223, 21659647, 90177423, 268420885, 268435455, 268435455, 268435455, 268435455, 268435455, 268435455, 268435455, 266371071, 268435455, 268435455, 268435455),
    (268435376, 105545648, 268435455, 266403839, 268425343, 268435455, 268435455, 268435455, 268420991, 268435455, 268435455, 268435455, 268435455, 268435455, 268435455, 268435343),
    (268435455, 268435455, 88899583, 268435455, 268435455, 268435455, 88244223, 90177535, 268425087, 268435455, 268435455, 6291373, 268435455, 268435455, 21234687, 267222965),
    (268435455, 268435455, 268435455, 25165823, 268435455, 268435455, 266616831, 268435341, 268435455, 268435455, 267026431, 266698751, 268435455, 268435455, 88871935, 25165823),
    (268435455, 268435455, 268420095, 268435455, 268435455, 268435455, 102760447, 268419583, 268435455, 268435455, 23054101, 268423679, 268435455, 90177535, 268435455, 268435455),
    (268435455, 268419972, 268435455, 268435455, 268435332, 268435455, 268435349, 268435373, 268435364, 88229759, 268425087, 268435344, 268435455, 268435455, 268435343, 92274687),
    (268435455, 268421119, 268435455, 268435455, 268435455, 268425087, 268435455, 268423679, 268435455, 38541183, 90177535, 268435455, 268435455, 33849343, 268435455, 268423679),
    (268435332, 268435455, 268435383, 268435455, 14680063, 88244223, 268419583, 268435455, 31457164, 268435455, 268435455, 268435455, 268435455, 267157503, 268435349, 268435455),
    (48234495, 268435455, 268435455, 268435455, 48234495, 268435341, 268435455, 266928127, 267026431, 268435455, 268435455, 268435455, 266502143, 268435455, 268435455, 268420607),
    (268435455, 266633215, 106954751, 267190271, 268435455, 268435455, 268435455, 267091967, 268435455, 268435455, 268435455, 268419583, 268435455, 268435455, 268435455, 266633215),
    (81788927, 267157503, 39845804, 268435455, 268435455, 102746239, 268435381, 268435455, 27252863, 268435455, 268435455, 266534911, 268435455, 268425215, 268435455, 268435455),
    (268425215, 268435455, 268435455, 268435455, 268435364, 267157503, 268435455, 268435455, 268422015, 268435455, 268435455, 268435455, 268421119, 268435455, 268435455, 268435375),
    (268435340, 268435455, 268435455, 268435383, 268422015, 268435364, 268423679, 23068671, 268435455, 268435455, 268435455, 73400319, 268422143, 268435455, 268435455, 267146751),
    (268435455, 268435340, 268435455, 268435455, 268435455, 268435455, 268435455, 92263856, 268435455, 268435455, 268435455, 268420607, 268435455, 268435455, 38567935, 268435349),
    (268435455, 268435372, 268435455, 39845887, 268435455, 268435455, 268435455, 268435349, 268435455, 268435455, 268435455, 266436607, 267026431, 268435455, 106939799, 268435455),
    (268435372, 268422015, 268435455, 268435455, 268435455, 268435455, 268435455, 268420607, 266633215, 102760447, 268435332, 90177535, 39845887, 268423679, 268425215, 267180543),
    (94357503, 268426111, 268435455, 268435455, 268435340, 268435455, 106954751, 266698751, 268435455, 268435455, 39830015, 268435455, 268435455, 268435455, 268435455, 268435455),
    (39836543, 268435380, 268435455, 268435455, 39845887, 268425343, 268435372, 266633215, 268435372, 268435455, 268423679, 268435455, 268435455, 268435455, 268435455, 41929215),
    (268435348, 268435455, 268435455, 268435455, 106954668, 268435455, 268435455, 268435455, 268435455, 268420607, 268435455, 268424703, 268435455, 268435455, 268435455, 268435455),
    (268435455, 268435455, 268435455, 268435455, 268435455, 268435455, 268435455, 268435455, 39845780, 267157503, 268435455, 268435455, 268435455, 268435455, 268435455, 268435383),
    (111148980, 268435455, 268435455, 268435455, 268435455, 268435332, 268435455, 268435455, 268426111, 268435455, 268435455, 268435455, 267157503, 268435455, 268435455, 268435455),
    (268435455, 268435455, 268435455, 268435455, 115334015, 268423679, 268435455, 268435455, 268435455, 268422015, 268435455, 268435455, 268435455, 268435455, 268435455, 268435455),
    (115343359, 268435455, 268435455, 268435455, 268435381, 268435455, 268420607, 39845813, 115343359, 266616831, 268435455, 268422015, 266682367, 268435455, 268435455, 268435455),
    (268435455, 268435455, 268435455, 268435351, 268435455, 266633133, 268435455, 268435455, 268435455, 268435455, 268435455, 268435455, 268435455, 268435455, 268435455, 268435455),
    (268435455, 268435455, 268435455, 41943039, 268435455, 268435455, 268425727, 267223039, 268435455, 268435455, 268435455, 268426111, 268435455, 268435455, 268435455, 268435455),
    (268435455, 268435455, 268435455, 268435455, 268435380, 268435455, 268435455, 268435455, 268435380, 75497471, 267157503, 267222965, 268435455, 268435455, 268421631, 268435455),
    (268435455, 268435455, 268435455, 268435455, 109346815, 106954751, 92274687, 268435455, 268435455, 268435455, 268435455, 268435455, 268435455, 268435455, 268426239, 268435455),
    (268435455, 268435455, 268435455, 268435455, 268435455, 268435455, 268435455, 268435455, 268435455, 268435455, 268435455, 268435455, 268435455, 268435455, 268435455, 268435455),
    (268435455, 268435455, 268435455, 268435455, 266682367, 267141119, 268435455, 268421631, 48234495, 268435455, 268421247, 268435455, 267197439, 41943039, 268435455, 268435455),
    (268435455, 268435455, 268435455, 268435455, 268435455, 268435455, 268435455, 268435455, 268435455, 268435348, 268422015, 268435455, 268435455, 268435455, 268435455, 268435455),
    (268435455, 268435455, 268435455, 268435455, 268435455, 268422015, 268435455, 268425727, 44040191, 268425343, 92274687, 268435455, 268435455, 268425727, 268435455, 268435455),
    (268435455, 268435455, 268435455, 268435455, 268435348, 268435455, 268435455, 268435455, 267157503, 268435455, 268435372, 268425727, 268435455, 268435455, 268435455, 268435455),
    (268435455, 268435455, 268435455, 268435455, 268435455, 268435455, 268435455, 268435455, 268435455, 268426111, 268435455, 268435455, 268435455, 268435455, 268435455, 268435455),
    (268435455, 268435455, 268435455, 268435455, 268435455, 268435349, 268435455, 268435455, 268435455, 268435455, 268435455, 268421631, 268435455, 268435455, 268435455, 268435455),
    (268435455, 268435455, 268435455, 268435455, 268435455, 268435376, 268435455, 268435455, 268435455, 268435455, 268435455, 268435455, 268435455, 268435455, 268435455, 268435455),
    (268435455, 268435455, 268435455, 268435455, 268435455, 268435455, 268435348, 268435455, 268435455, 268435455, 268435455, 106954751, 268435455, 268435455, 268435455, 268435455),
    (268435455, 268435455, 268435455, 268435455, 268435455, 268435455, 268435455, 268435455, 268435455, 268435455, 268426111, 268435455, 268435455, 268435455, 268435455, 268435455),
    (268435455, 268435455, 268435455, 268435455, 268435455, 268435455, 268435455, 268435455, 268435455, 268435455, 268425727, 268435455, 268435455, 268435455, 268435455, 268435455),
    (268435455, 268435455, 268435455, 268435455, 268435455, 268435455, 268435455, 268435455, 268435455, 268435455, 268435455, 268435455, 268435455, 268435455, 268435455, 268435455),
    (268435455, 268435455, 268435455, 268435455, 268435455, 268435455, 268435455, 268435455, 268435455, 268435455, 268435455, 268435455, 268435455, 268435455, 268435455, 268435455),
    (268435455, 268435455, 268435455, 268435455, 268435455, 268435455, 268435455, 268435455, 268435455, 268421631, 268435455, 268435455, 268435455, 268435455, 268435455, 268435455),
    (268435455, 268435455, 268435455, 268435455, 268435455, 268435381, 268435455, 268435455, 268435455, 268435455, 268435455, 268435455, 268435455, 268435455, 268435455, 268435455),
    (268435455, 268435455, 268435455, 268435455, 268435455, 268435455, 268435455, 268435455, 268435455, 268435455, 268435455, 268435455, 268435455, 268435455, 268435455, 268435455),
    (268435455, 268435455, 268435455, 268435455, 268435455, 268435455, 268435455, 268435455, 268435455, 268435455, 268435455, 268435455, 268435455, 268435455, 268435455, 268435455),
    (268435455, 268435455, 268435455, 268435455, 268435455, 268435455, 268435455, 268435455, 268435455, 268435455, 268435455, 268435455, 268435455, 268435455, 268435455, 268435455),
    (268435455, 268435455, 268435455, 268435455, 268435455, 268435455, 268435455, 268435455, 268435455, 268435455, 268435455, 268435455, 268435455, 268435455, 268435455, 268435455),
    (268435455, 268435455, 268435455, 268435455, 268435455, 268435455, 268435455, 268435455, 268435455, 268435455, 268435455, 268435455, 268435455, 268435455, 268435455, 268435455),
    (268435455, 268435455, 268435455, 268435455, 268435455, 268435455, 268435455, 268435455, 268435455, 268435455, 268435455, 268435455, 268435455, 268435455, 268435455, 268435455),
)
COUNT = len(ARRIVALS)
LAG = 6
PARTS = 3
EARLY = 2
VMEM_LIMIT = 60 * 1024 * 1024


def pick(values, p):
    values = list(values)
    bit = 1
    while len(values) > 1:
        if len(values) % 2:
            values.append(values[-1])
        odd = (p // bit) % 2 == 1
        values = [jnp.where(odd, b, a) for a, b in zip(values[::2], values[1::2])]
        bit *= 2
    return values[0]


def kernel(
    q_ref, k_ref, v_ref, mask_ref, w_ref, out_ref,
    kv, qs, masks, bias, wts, att, attended, top, total, accum, proj,
    kv_recv, out_send, first_send, pass_send, q_recv, q_local, kv_local, swap_send,
    w_recv, w_send, w_local, w_pass_recv, w_pass_send, att_recv, att_send, mask_sem,
):
    i = lax.axis_index("ctx")
    z = lax.axis_index("head")
    c = i % 2
    p = i // 2
    x = p // 4
    y = p % 4
    twin = (p * 2 + 1 - c, z)
    neighbours = (((x + 1) % 4) * 4 + y, ((x + 3) % 4) * 4 + y, x * 4 + (y + 1) % 4, x * 4 + (y + 3) % 4)

    def slot_of(delta):
        slot = jnp.where(delta == -2, 3, jnp.where(delta == 2, 4, 7))
        slot = jnp.where(delta == -1, 1, jnp.where(delta == 1, 2, slot))
        return jnp.where(delta == -4, 5, jnp.where(delta == 4, 6, slot))

    def remote(src, dst, send, recv, device):
        return pltpu.make_async_remote_copy(
            src_ref=src, dst_ref=dst, send_sem=send, recv_sem=recv, device_id=device, device_id_type=MESH
        )

    barrier = pltpu.get_barrier_semaphore()
    greeted = [(there * 2 + core, z) for there in neighbours for core in (0, 1)] + [twin]
    for dz in (1, 2, 3):
        greeted += [(i, (z + dz) % 4), (p * 2 + 1 - c, (z + dz) % 4)]
    for device in greeted:
        pl.semaphore_signal(barrier, inc=1, device_id=device, device_id_type=MESH)

    my_rows = pl.ds(pl.multiple_of(c * FRAME, FRAME), FRAME)
    twin_rows = pl.ds(pl.multiple_of((1 - c) * FRAME, FRAME), FRAME)

    def columns(core, h):
        return pl.ds(pl.multiple_of((HEADS_CORE * core + h) * HEAD_DIM, HEAD_DIM), HEAD_DIM)

    def swap_kv(h, which):
        ref = (k_ref, v_ref)[which]
        return remote(ref.at[:, columns(1 - c, h)], kv.at[0, which, h, my_rows, :], swap_send.at[which, h], kv_recv.at[0, which, h], twin)

    def swap_q(h):
        return remote(q_ref.at[:, columns(1 - c, h)], qs.at[h, my_rows, :], swap_send.at[2, h], q_recv.at[h], twin)

    def keep_kv(h, which):
        ref = (k_ref, v_ref)[which]
        return pltpu.make_async_copy(ref.at[:, columns(c, h)], kv.at[0, which, h, my_rows, :], kv_local.at[which, h])

    def keep_q(h):
        return pltpu.make_async_copy(q_ref.at[:, columns(c, h)], qs.at[h, my_rows, :], q_local.at[h])

    swap_mask = remote(mask_ref, masks.at[c], mask_sem.at[0], mask_sem.at[1], twin)
    keep_mask = pltpu.make_async_copy(mask_ref, masks.at[c], mask_sem.at[2])

    def w_block(h, core, zz):
        rows = pl.ds(pl.multiple_of((HEADS_CORE * core + h) * HEAD_DIM, HEAD_DIM), HEAD_DIM)
        return w_ref.at[rows, pl.ds(pl.multiple_of(zz * 768, 768), 768)]

    def w_copy(h, dz):
        zz = (z + dz) % 4
        return remote(w_block(h, c, zz), wts.at[h, z * 2 + c], w_send.at[h, dz - 1], w_recv.at[h, dz - 1], (i, zz))

    def w_keep(h, core):
        return pltpu.make_async_copy(w_block(h, core, z), wts.at[h, z * 2 + core], w_local.at[h, core])

    def w_pass(h, dz):
        place = ((z + 4 - dz) % 4) * 2 + c
        return remote(wts.at[h, place], wts.at[h, place], w_pass_send.at[h, dz - 1], w_pass_recv.at[h, dz - 1], twin)

    def own_copy(h, which, group, direction, sem):
        there = neighbours[direction]
        ref = (k_ref, v_ref)[which]
        core = c if group == 0 else 1 - c
        return remote(
            ref.at[:, columns(core, h)], kv.at[slot_of(p - there), which, h, my_rows, :],
            sem, kv_recv.at[slot_of(p - there), which, h], (there * 2 + core, z),
        )

    def own_first(h, which, group, direction):
        ref = (k_ref, v_ref)[which]
        there = neighbours[direction]
        return remote(
            ref.at[:, columns(group, h)], kv.at[8, which, h, 0:FRAME, :],
            first_send.at[group, which, h, direction], kv_recv.at[8, which, h], (there * 2 + group, z),
        )

    def first_sent(word, action):
        slot = word & 15
        h = (word >> 4) & 3
        which = (word >> 6) & 1
        some = ((word >> 11) & 15) > 0

        @pl.when(some & (slot == 0) & (c == 0))
        def _():
            for direction in range(4):
                for kind in (0, 1):
                    @pl.when((((word >> (11 + direction)) & 1) == 1) & (which == kind))
                    def _():
                        for group in (0, 1):
                            action(own_first(h, kind, group, direction))

        @pl.when(some & (slot > 0))
        def _():
            for direction in range(4):
                @pl.when(((word >> (11 + direction)) & 1) == 1)
                def _():
                    action(remote(
                        kv.at[slot, which, h, 0:FRAME, :], kv.at[8, which, h, 0:FRAME, :],
                        pass_send.at[which, h, direction], kv_recv.at[8, which, h], (neighbours[direction] * 2 + c, z),
                    ))

    def out_done(direction, turn):
        whole = kv.at[0, 0, 0]
        remote(whole, whole, out_send.at[direction, turn], kv_recv.at[0, 0, 0], twin).wait_send()

    def send(packed, sent):
        after = []
        for direction in range(4):
            code = (packed >> (7 * direction)) & 127
            slot = code & 7
            h = (code >> 3) & 3
            which = (code >> 5) & 1
            turn = sent[direction] % 2

            @pl.when(code < 127)
            def _():
                pl.when(sent[direction] > 1)(lambda: out_done(direction, turn))
                sem = out_send.at[direction, turn]
                for kind in (0, 1):
                    @pl.when((slot == 0) & (which == kind))
                    def _():
                        for group in (0, 1):
                            own_copy(h, kind, group, direction, sem).start()

                @pl.when(slot > 0)
                def _():
                    there = neighbours[direction]
                    far = jnp.where(p < 8, 8, -8)
                    near = jnp.where(slot == 1, -1, jnp.where(slot == 2, 1, jnp.where(slot == 3, -2, 2)))
                    off = jnp.where(slot < 5, near, jnp.where(slot == 5, -4, jnp.where(slot == 6, 4, far)))
                    target = slot_of(p + off - there)
                    remote(
                        kv.at[slot, which, h], kv.at[target, which, h], sem, kv_recv.at[target, which, h], (there * 2 + c, z)
                    ).start()

            after.append(sent[direction] + jnp.where(code < 127, 1, 0))
        return tuple(after)

    def start(copy):
        copy.start()

    def finish(copy):
        copy.wait_send()

    for h in range(HEADS_CORE):
        keep_q(h).start()
        keep_kv(h, 0).start()
        keep_kv(h, 1).start()
    keep_mask.start()
    pl.semaphore_wait(barrier, len(greeted))
    sent = (jnp.int32(0),) * 4
    for n in range(EARLY):
        sent = send(pick(SENDS[n], p), sent)
        first_sent(pick(ARRIVALS[n], p), start)
    swap_mask.start()
    for h in range(HEADS_CORE):
        swap_q(h).start()
        swap_kv(h, 0).start()
        swap_kv(h, 1).start()
    for h in range(HEADS_CORE):
        for dz in (1, 3, 2):
            w_copy(h, dz).start()
    for h in range(HEADS_CORE):
        for core in (0, 1):
            w_keep(h, core).start()

    top[...] = jnp.full_like(top, NEG)
    total[...] = jnp.zeros_like(total)
    accum[...] = jnp.zeros_like(accum)
    proj[...] = jnp.zeros_like(proj)

    keep_mask.wait()
    swap_mask.wait_recv()
    blocks = masks.shape[2]
    same = lax.broadcasted_iota(jnp.int32, (blocks, blocks), 0) == lax.broadcasted_iota(jnp.int32, (blocks, blocks), 1)
    anchor_rows = lax.broadcasted_iota(jnp.int32, (blocks, BLOCK), 0) < FRAME // BLOCK
    for core in (0, 1):
        for b in (0, 1):
            line = jnp.where(same, jnp.broadcast_to(masks[core, b : b + 1, :], (blocks, blocks)), 0)
            column = jnp.sum(line.astype(jnp.float32), axis=1, keepdims=True)
            wide = jnp.broadcast_to(column, (blocks, BLOCK))
            added = jnp.where((wide > 0) & ~anchor_rows, 0.0, NEG).astype(jnp.float32)
            for n in range(blocks // 2):
                bias[core, n, :, b * BLOCK : (b + 1) * BLOCK] = added[2 * n : 2 * n + 2, :]
        bias[core, 32] = jnp.zeros_like(bias[core, 32])

    def attend(slot, h, source, parts):
        scores = []
        for frame, halves in parts:
            rows = slice(frame * FRAME, (frame + 1) * FRAME)
            held = slice(halves[0] * FRAME, (halves[-1] + 1) * FRAME)
            scores.append(lax.dot_general(
                kv[slot, 0, h, held, :], qs[h, rows, :], (((1,), (1,)), ((), ())), preferred_element_type=jnp.float32
            ))
        weights = []
        factors = []
        for (frame, halves), score in zip(parts, scores):
            rows = slice(frame * FRAME, (frame + 1) * FRAME)
            length = len(halves) * FRAME
            score = score * EXP2_SCALE
            if source is not None:
                added = [bias[frame, source * 2 + half] for half in halves]
                added = added[0] if len(added) == 1 else jnp.concatenate(added, axis=0)
                score = (score.reshape(length // BLOCK, BLOCK, FRAME) + added[:, None, :]).reshape(length, FRAME)
            before = top[h, :, rows]
            now = jnp.maximum(before, jnp.max(score, axis=0, keepdims=True))
            weight = jnp.exp2(score - now)
            factor = jnp.exp2(before - now)
            total[h, :, rows] = total[h, :, rows] * factor + jnp.sum(weight, axis=0, keepdims=True)
            top[h, :, rows] = now
            weights.append(weight.astype(jnp.bfloat16))
            factors.append(factor)
        for (frame, halves), weight, factor in zip(parts, weights, factors):
            rows = slice(frame * FRAME, (frame + 1) * FRAME)
            held = slice(halves[0] * FRAME, (halves[-1] + 1) * FRAME)
            mixed = lax.dot_general(
                kv[slot, 1, h, held, :], weight, (((0,), (0,)), ((), ())), preferred_element_type=jnp.float32
            )
            accum[h, :, rows] = accum[h, :, rows] * factor + mixed

    def att_copy(h, dz, cross):
        core = 1 - c if cross else c
        rows = twin_rows if cross else my_rows
        return remote(
            attended.at[h, rows, :], att.at[h, z * 2 + c], att_send.at[h, dz, cross], att_recv.at[h, dz, cross],
            (p * 2 + core, (z + dz) % 4),
        )

    def project(h):
        for dz in range(4):
            for cross in (0, 1):
                if dz or cross:
                    att_copy(h, dz, cross).wait_recv()
        for dz in (1, 2, 3):
            w_pass(h, dz).wait_recv()
        for core in (0, 1):
            w_keep(h, core).wait()
        for n in range(3):
            cols = slice(n * 256, (n + 1) * 256)
            part = proj[:, cols]
            for pair in range(4):
                left = jnp.concatenate([att[h, 2 * pair], att[h, 2 * pair + 1]], axis=1)
                right = jnp.concatenate([wts[h, 2 * pair, :, cols], wts[h, 2 * pair + 1, :, cols]], axis=0)
                part = part + jnp.dot(left, right, preferred_element_type=jnp.float32)
            proj[:, cols] = part

    def step(arrivals, sends, n, carry):
        sent, recent = carry
        word = pick(arrivals, n)
        slot = word & 15
        h = (word >> 4) & 3
        which = (word >> 6) & 1
        source = (word >> 18) & 15

        @pl.when((slot > 0) & (slot < 8))
        def _():
            whole = kv.at[slot, which, h]
            remote(whole, whole, pass_send.at[0, 0, 0], kv_recv.at[slot, which, h], twin).wait_recv()

        @pl.when(slot == 8)
        def _():
            first = kv.at[8, which, h, 0:FRAME, :]
            remote(first, first, pass_send.at[0, 0, 0], kv_recv.at[8, which, h], twin).wait_recv()

        first_sent(word, start)
        sent = send(pick(sends, n), sent)

        @pl.when(slot == 9)
        def _():
            keep_q(h).wait()
            swap_q(h).wait_recv()
            for kind in (0, 1):
                keep_kv(h, kind).wait()
                swap_kv(h, kind).wait_recv()
            attend(0, h, p, ((0, (0, 1)), (1, (0, 1))))

        @pl.when(((word >> 15) & 1) == 1)
        def _():
            @pl.when(slot == 1)
            def _():
                attend(1, h, source, ((0, (0, 1)), (1, (1,))))

            @pl.when(slot == 2)
            def _():
                attend(2, h, source, ((0, (0,)), (1, (0, 1))))

            @pl.when((slot > 2) & (slot < 8))
            def _():
                attend(slot, h, source, ((0, (0,)), (1, (1,))))

        @pl.when(((word >> 17) & 1) == 1)
        def _():
            attend(jnp.where(slot == 9, 0, slot), h, None, ((0, (0,)), (1, (0,))))

        @pl.when(((word >> 16) & 1) == 1)
        def _():
            attended[h] = jnp.transpose(accum[h] / total[h]).astype(jnp.bfloat16)
            for dz in (2, 1, 3, 0):
                for cross in (0, 1):
                    if dz or cross:
                        att_copy(h, dz, cross).start()
            att[h, z * 2 + c] = attended[h, my_rows, :]

        @pl.when(slot == 10)
        def _():
            for dz in (1, 3, 2):
                w_copy(h, dz).wait_recv()
                w_pass(h, dz).start()

        first_sent(recent[0], finish)
        return sent, recent[1:] + (word,)

    carry = sent, (jnp.int32(15),) * (LAG - EARLY) + tuple(pick(line, p) for line in ARRIVALS[:EARLY])
    length = -(-(COUNT - EARLY) // PARTS)
    for begin in range(EARLY, COUNT, length):
        end = min(begin + length, COUNT)
        arrivals = [pick(line, p) for line in ARRIVALS[begin:end]]
        sends = [pick(line, p) for line in SENDS[begin:end]]
        carry = lax.fori_loop(0, end - begin, functools.partial(step, arrivals, sends), carry)
    recent = carry[1]

    def finish_heads(heads):
        for h in heads:
            for dz in range(4):
                for cross in (0, 1):
                    if dz or cross:
                        att_copy(h, dz, cross).wait_send()

    project(0)
    project(1)
    for word in recent:
        first_sent(word, finish)
    for direction in range(4):
        for turn in (0, 1):
            out_done(direction, turn)
    for h in range(HEADS_CORE):
        for which in (0, 1):
            swap_kv(h, which).wait_send()
        swap_q(h).wait_send()
        for dz in (1, 2, 3):
            w_copy(h, dz).wait_send()
            w_pass(h, dz).wait_send()
    swap_mask.wait_send()
    finish_heads((0, 1))
    project(2)
    out_ref[...] = proj[...].astype(out_ref.dtype)
    finish_heads((2,))


def body(queries, keys, values, block_mask, w_out):
    bf16, f32, dma = jnp.bfloat16, jnp.float32, pltpu.SemaphoreType.DMA
    heads = HEADS_CORE
    anywhere = pl.BlockSpec(memory_space=pl.ANY)
    return pl.pallas_call(
        kernel,
        out_shape=jax.ShapeDtypeStruct((FRAME, 768), bf16),
        in_specs=[anywhere, anywhere, anywhere, pl.BlockSpec(memory_space=pltpu.VMEM), anywhere],
        out_specs=pl.BlockSpec(memory_space=pltpu.VMEM),
        scratch_shapes=[
            pltpu.VMEM((9, 2, heads, 2 * FRAME, HEAD_DIM), bf16),
            pltpu.VMEM((heads, 2 * FRAME, HEAD_DIM), bf16),
            pltpu.VMEM((2, 2, 64), jnp.int32),
            pltpu.VMEM((2, 33, 2, FRAME), f32),
            pltpu.VMEM((heads, 8, HEAD_DIM, 768), bf16),
            pltpu.VMEM((heads, 8, FRAME, HEAD_DIM), bf16),
            pltpu.VMEM((heads, 2 * FRAME, HEAD_DIM), bf16),
            pltpu.VMEM((heads, 1, 2 * FRAME), f32),
            pltpu.VMEM((heads, 1, 2 * FRAME), f32),
            pltpu.VMEM((heads, HEAD_DIM, 2 * FRAME), f32),
            pltpu.VMEM((FRAME, 768), f32),
            dma((9, 2, heads)), dma((4, 2)), dma((2, 2, heads, 4)), dma((2, heads, 4)), dma((heads,)), dma((heads,)), dma((2, heads)), dma((3, heads)),
            dma((heads, 3)), dma((heads, 3)), dma((heads, 2)), dma((heads, 3)), dma((heads, 3)),
            dma((heads, 4, 2)), dma((heads, 4, 2)), dma((3,)),
        ],
        compiler_params=pltpu.CompilerParams(
            collective_id=0, has_side_effects=True, vmem_limit_bytes=VMEM_LIMIT
        ),
        name="radial_attention",
    )(queries, keys, values, block_mask, w_out)


def solution(mesh):
    placed = (P("ctx", "head"), P("ctx", "head"), P("ctx", "head"), P("ctx", None), P("head", None))
    return jax.shard_map(
        body, mesh=mesh, in_specs=placed, out_specs=P("ctx", "head"), check_vma=False
    )
```

```python
import functools

import jax
import jax.numpy as jnp
from jax import lax
from jax.experimental import pallas as pl
from jax.experimental.pallas import tpu as pltpu
from jax.sharding import PartitionSpec as P

HEAD_DIM = 128
BLOCK = 128
FRAME = 256
HEADS_CORE = 3
MESH = pl.DeviceIdType.MESH
NEG = -1e30
EXP2_SCALE = HEAD_DIM ** (-0.5) * 1.4426950408889634

ARRIVALS = (
    (15, 15, 15, 15, 15, 15, 15, 15, 15, 15, 15, 15, 15, 15, 15, 15),
    (16384, 15, 15, 15, 15, 15, 15, 15, 15, 15, 15, 15, 15, 15, 15, 15),
    (20544, 262153, 524297, 786441, 1048585, 1310729, 1572873, 1835017, 2097161, 2359305, 2621449, 2883593, 3145737, 3407881, 3670025, 3932169),
    (131081, 262169, 524313, 4104, 1048601, 1310745, 1572889, 1835033, 2097177, 2359321, 2621465, 2883609, 3145753, 3407897, 524358, 3932185),
    (131097, 15, 15, 137288, 15, 15, 15, 15, 15, 15, 15, 15, 15, 15, 3670041, 15),
    (131113, 262185, 524329, 786457, 1048617, 1310761, 1572905, 1835049, 2097193, 2359337, 2621481, 2883625, 3145769, 3407913, 15, 3932201),
    (1048646, 3407877, 3670085, 786473, 16389, 262213, 524373, 786437, 1048645, 1310789, 1572869, 1835093, 2097173, 2359301, 3670057, 2883589),
    (262162, 65, 1572870, 3932165, 2097222, 2359366, 2621510, 1572929, 3145734, 3407878, 3670022, 2621441, 72, 262150, 2621445, 3670081),
    (1081350, 1310726, 262209, 1835014, 1310722, 1572882, 1310785, 2883590, 2359362, 2621506, 2359297, 3932182, 3407874, 3145729, 3407889, 786502),
    (294994, 3407893, 786498, 524353, 172101, 1048577, 1835010, 2916422, 3178566, 2097153, 2883650, 1867797, 2097189, 3670082, 3932162, 2916421),
    (4112, 524354, 3670037, 3932229, 2129926, 294917, 524293, 1605633, 1081349, 1310741, 1572885, 3932262, 3440706, 2359317, 2621461, 3702785),
    (80, 1343558, 1605702, 1867846, 1310738, 2359318, 2654214, 819269, 2392066, 3440710, 3702854, 2654273, 70, 262214, 3440721, 786454),
    (2097175, 81, 294913, 557057, 24661, 1081409, 1343489, 72, 15, 2129985, 2392129, 15, 22, 3145745, 3964994, 8),
    (15, 524370, 819202, 15, 15, 1572930, 1867842, 15, 15, 2654210, 2916354, 15, 15, 3702786, 2654293, 151624),
    (15, 15, 15, 15, 2097238, 15, 15, 15, 15, 15, 15, 1835077, 2130005, 15, 15, 15),
    (1048662, 167937, 15, 3932245, 1343554, 15, 15, 15, 15, 15, 15, 15, 15, 15, 3407969, 15),
    (262242, 3407909, 786514, 524369, 2129942, 15, 15, 2883670, 1048597, 15, 1605717, 2621457, 38, 15, 15, 2883605),
    (1048614, 1310742, 3670101, 1835094, 786433, 262229, 15, 1572945, 3145750, 1343573, 524359, 1835045, 3407954, 15, 1572887, 15),
    (294946, 557074, 1572950, 3932197, 101, 2392070, 557077, 147464, 2359378, 3407958, 2359377, 2621537, 3440658, 2359397, 3932178, 3670097),
    (524292, 3407973, 262161, 524385, 1310818, 1605634, 2621462, 2916374, 3178582, 2097233, 2883602, 15, 1048647, 262166, 3965010, 1835015),
    (10, 1343574, 3670117, 1867798, 10, 294933, 1310737, 786453, 1081429, 2621522, 1605701, 786503, 2883585, 3178561, 1572871, 2883685),
    (15, 524322, 1572966, 10, 1572868, 2392150, 1835090, 1605649, 2392082, 1343493, 2916434, 3145730, 3670084, 3670034, 3145731, 3670113),
    (15, 167953, 294993, 1048642, 15, 1605714, 524389, 819285, 1835089, 2129937, 3670038, 10, 10, 3178577, 1605703, 3407875),
    (4128, 10, 819218, 1081346, 15, 1048593, 2621542, 10, 10, 3440662, 2359393, 3178562, 24, 2392101, 10, 10),
    (96, 2359303, 10, 1835046, 172053, 2120, 1835042, 15, 1867793, 2621474, 10, 16456, 102, 3670050, 72, 3440707),
    (557124, 4129, 15, 15, 1605700, 10, 1343569, 88, 15, 10, 15, 15, 1081351, 262230, 3145747, 15),
    (15, 2392135, 2621527, 2883591, 3145735, 1081425, 10, 2097218, 15, 15, 15, 15, 3702788, 10, 1605719, 15),
    (524388, 786500, 2115, 262211, 3178567, 3407879, 15, 1310723, 2621444, 15, 557063, 786455, 1048599, 28680, 15, 15),
    (2097223, 2359319, 15, 2883671, 819265, 8280, 15, 3932183, 71, 15, 3702870, 15, 3407970, 15, 1572967, 3407955),
    (2129927, 819204, 786466, 2916423, 1572884, 3440711, 15, 1343555, 180231, 1310757, 2097155, 819207, 2916417, 3145825, 3932194, 1835095),
    (15, 163937, 2621511, 294915, 172069, 1835012, 15, 2883686, 24599, 262151, 2883682, 2359363, 3670100, 1310791, 3965026, 15),
    (524372, 622594, 1605654, 1048658, 1605716, 2359334, 3670087, 1572961, 190551, 2883588, 3670054, 1867877, 1081431, 3932164, 3178563, 3702801),
    (15, 15, 2654215, 1048610, 524291, 1867844, 3702791, 3932231, 2654276, 2097185, 524375, 2392067, 16424, 1310743, 2654277, 1867799),
    (557076, 2392151, 819298, 15, 1343570, 3407911, 1048643, 3964935, 1835073, 2130017, 2129987, 3145810, 15, 3964996, 131080, 2916389),
    (1081366, 786516, 163843, 2883687, 26, 1048673, 3670039, 15, 1835041, 294983, 2916386, 1867781, 131080, 3178529, 26, 3440659),
    (2195543, 26, 15, 262227, 3145815, 3440743, 2654246, 2129922, 15, 1343589, 72, 2359315, 2621443, 1343495, 3178579, 15),
    (26, 1310822, 8275, 15, 786513, 139288, 2056, 2097234, 1572867, 2916420, 15, 819287, 26, 2883587, 3407873, 3702817),
    (262210, 884756, 1048580, 26, 2097254, 786435, 1081347, 1310803, 24679, 2120, 3145748, 131080, 1048615, 8216, 3506241, 1933383),
    (557092, 15, 2654231, 2916375, 1343522, 3407959, 1867794, 26, 26, 1835027, 2097171, 3407876, 2883601, 15, 4120, 1835047),
    (1081446, 15, 26, 294931, 622659, 1835092, 1867874, 3965015, 2621524, 135176, 26, 15, 155736, 1343575, 15, 26),
    (360450, 2359335, 2621543, 1310724, 819217, 26, 557125, 1343507, 3145830, 15, 1572965, 15, 3702804, 262182, 3145763, 3407971),
    (15, 786532, 1146948, 262243, 524371, 2392166, 2097220, 2359364, 2654228, 26, 2392097, 26, 2883681, 26, 4136, 1867879),
    (2097255, 15, 10275, 1409092, 1572964, 1572898, 131144, 786469, 2621476, 2883668, 1605669, 2392147, 3440674, 3932180, 2621541, 2916437),
    (42, 2392167, 2654247, 88, 2129958, 819267, 26, 1605665, 1605699, 24, 3145796, 2359395, 2097157, 4136, 3178595, 16424),
    (2195495, 1343526, 172051, 15, 3178519, 196616, 1048595, 2457604, 15, 2916372, 131080, 2072, 2654275, 3965012, 1605671, 15),
    (15, 819236, 1048660, 2916391, 1605668, 40, 88, 2129938, 1867873, 131160, 557079, 147544, 2195525, 1310759, 196696, 15),
    (15, 622690, 1146900, 15, 622611, 1081377, 3702871, 3932199, 2359394, 262231, 3244036, 15, 3670052, 131144, 2654245, 16472),
    (15, 42, 1048612, 557073, 786465, 262245, 2654294, 2359316, 15, 294935, 524391, 3932230, 2916385, 2392133, 42, 196632),
    (15, 15, 262177, 1310804, 3145831, 1835044, 2195460, 1310819, 1933313, 1835011, 3178580, 3440708, 2621523, 2981955, 131176, 3440675),
    (15, 15, 163939, 40, 42, 786515, 1081427, 819301, 180263, 1933379, 2097187, 4030470, 2916433, 3702866, 3506209, 206952),
    (15, 15, 42, 1081362, 524387, 1867796, 3670055, 15, 1572883, 14440, 2392081, 2152, 1081447, 131160, 15, 42),
    (15, 15, 295009, 3932261, 557091, 3440663, 2097236, 131096, 3178534, 131112, 88, 3407892, 42, 3702882, 15, 15),
    (15, 15, 1605670, 1343508, 819297, 15, 139288, 1343523, 1671251, 2654306, 2130019, 2654241, 2719763, 2392149, 15, 15),
    (15, 15, 1146980, 196632, 3244071, 139368, 2195476, 2457684, 1048613, 2883684, 131096, 3178514, 3702884, 3932196, 15, 15),
    (15, 15, 15, 1867878, 15, 884755, 3702887, 42, 42, 262183, 2152, 3965014, 2130021, 1343591, 15, 15),
    (15, 15, 15, 42, 15, 42, 1048675, 2916390, 2654308, 1835043, 42, 3440724, 2621475, 2883683, 15, 15),
    (15, 15, 15, 557089, 15, 294949, 8232, 2359396, 1572963, 2654226, 2195539, 2719825, 131176, 2883667, 15, 15),
    (15, 15, 15, 131176, 15, 1605730, 557093, 40, 1081445, 1933395, 131112, 3145826, 2719843, 2981907, 15, 15),
    (15, 15, 15, 1310820, 15, 786531, 1310753, 2097250, 1605667, 42, 3145764, 2392099, 15, 42, 15, 15),
    (15, 15, 15, 1081442, 15, 1867876, 42, 3965031, 2457634, 3407910, 3702886, 42, 15, 3965028, 15, 15),
    (15, 15, 15, 294947, 15, 884771, 139368, 2129954, 15, 2916388, 3178596, 786471, 15, 131176, 15, 15),
    (15, 15, 15, 1409060, 15, 15, 1343585, 131176, 15, 1867875, 622631, 3407972, 15, 2981923, 15, 15),
    (15, 15, 15, 15, 15, 15, 1081379, 2457636, 15, 295015, 15, 131112, 15, 15, 15, 15),
    (15, 15, 15, 15, 15, 15, 2097188, 15, 15, 3506278, 15, 3440676, 15, 15, 15, 15),
    (15, 15, 15, 15, 15, 15, 2195556, 15, 15, 15, 15, 3178530, 15, 15, 15, 15),
    (15, 15, 15, 15, 15, 15, 15, 15, 15, 15, 15, 3964966, 15, 15, 15, 15),
    (15, 15, 15, 15, 15, 15, 15, 15, 15, 15, 15, 884839, 15, 15, 15, 15),
)
SENDS = (
    (266866688, 17301536, 67637288, 69193728, 266342432, 524320, 17301504, 2080808, 266342408, 67112960, 67112960, 69189632, 266338431, 131072, 67633184, 2081792),
    (266994720, 83890176, 83902336, 2081824, 266862592, 16781320, 67112968, 69193736, 266862608, 525320, 524296, 2084896, 266473599, 67768328, 4104, 69195808),
    (268435455, 268435455, 268435455, 268435455, 268435455, 268435455, 268435455, 268435455, 268435455, 268435455, 268435455, 268435455, 268435455, 268435455, 268435455, 268435455),
    (268435455, 268435455, 268435455, 268435455, 268435455, 268435455, 268435455, 268435455, 268435455, 268435455, 268435455, 268435455, 268435455, 268435455, 268435455, 268435455),
    (266354600, 100795432, 17448840, 268435455, 266474504, 67241000, 660520, 85972000, 266998824, 84541488, 84018216, 18863112, 266863743, 84677648, 268435455, 18874280),
    (266471472, 34214920, 34357168, 85983112, 266995752, 101323776, 84023328, 35636240, 266470527, 17568784, 34347135, 85967920, 266998911, 18859056, 17437480, 85983120),
    (81778815, 268435455, 268435455, 18874280, 268435455, 268435455, 268435455, 266436607, 268435365, 268435455, 268435455, 267091967, 268435341, 268435455, 34341936, 266436607),
    (268435455, 268435455, 268419967, 268435455, 81788927, 268435455, 268435455, 268435455, 14680063, 268435455, 268435455, 268435455, 268435455, 268435455, 268435455, 266895359),
    (14680063, 268435455, 268435455, 268419967, 6291455, 268435455, 268435455, 268435455, 268435455, 268435455, 268435455, 268435455, 6291455, 266371071, 268435455, 268424063),
    (266616712, 268435455, 268435455, 268435455, 268435455, 268435455, 268435455, 268435455, 81788927, 268435455, 268435455, 266567679, 268435455, 268435455, 268435455, 268435455),
    (268435455, 268435455, 268435455, 268435455, 268435455, 268435455, 268435455, 266371071, 268435455, 268435455, 268435341, 268435455, 73400319, 268435455, 268435455, 268435455),
    (268435455, 268435455, 268424063, 268435455, 268435455, 268435455, 268435455, 268435455, 268435455, 268435455, 268435455, 268435455, 268435455, 268435455, 268435455, 268420991),
    (268435455, 268435455, 268435455, 266371071, 268423941, 268435455, 268435455, 268435455, 268435333, 268435455, 268435455, 102745901, 268435455, 268435455, 268435455, 268435455),
    (268435344, 268435455, 268435455, 35651583, 268419885, 268435455, 268435455, 18860037, 266601343, 268435455, 268435455, 35641360, 267129727, 268435455, 268435455, 268435455),
    (267141119, 266879749, 71860133, 268435365, 268435455, 266883856, 266883845, 102760368, 268424063, 266359589, 4735871, 268435455, 268420991, 266502143, 266474541, 268435333),
    (268425087, 73400319, 4226957, 102760325, 267141119, 73400319, 6291455, 266960895, 267141119, 6291455, 71321727, 266960895, 266616831, 268419845, 6291455, 35651493),
    (268435455, 88098837, 268435455, 268435455, 268435455, 266356528, 267125549, 268425087, 268435455, 266881037, 268435373, 268435455, 268435455, 6291455, 71452799, 268435455),
    (268435455, 268435455, 268435455, 268435455, 266371071, 23068671, 73400319, 268435455, 268435341, 73400319, 268435455, 268435455, 90177535, 268424063, 268435343, 102760447),
    (268435455, 268435455, 268435455, 268435455, 268435455, 268435455, 268435455, 268435455, 268435455, 268435455, 268435455, 268435455, 268435455, 102760447, 268435455, 266960895),
    (98566143, 268435455, 268435455, 267157503, 268435455, 268435455, 268435455, 268435455, 98566143, 268435455, 268435455, 266698751, 268435455, 268435455, 268435455, 267011071),
    (48234495, 268435455, 268435455, 268420991, 268435455, 268435455, 268435455, 267026431, 268435455, 268435455, 268435455, 268435455, 268435455, 268435455, 268435455, 268435455),
    (268421892, 268435381, 268426111, 268435455, 268435455, 268435455, 268435455, 268435455, 23068671, 268435455, 268435455, 268435455, 268435455, 266895359, 268435455, 268435455),
    (266420223, 21659647, 268435455, 268435455, 14680063, 268435455, 268435455, 268435455, 268435455, 268435455, 268435455, 268435455, 268435455, 268435455, 268435455, 268435455),
    (268435455, 268435455, 268435455, 6291455, 98566143, 268435455, 268435455, 268435455, 268435455, 268435455, 268435455, 268435455, 266371071, 268435455, 268435455, 268435455),
    (268435455, 268435455, 268435455, 268422015, 268424964, 268435455, 268435455, 268435373, 268435455, 268435455, 268435455, 268435455, 268426111, 267026431, 268435455, 268435455),
    (268435455, 268435455, 88768429, 268435373, 268425252, 84039551, 268435455, 267091967, 266491775, 268435455, 88757247, 268435365, 268425343, 268435455, 21235199, 268419583),
    (268435364, 268435455, 268435455, 268435455, 268435455, 268425343, 268435455, 268435455, 268425343, 88233773, 21790719, 73400319, 268435455, 268435455, 268435455, 268435381),
    (268435455, 38032292, 268435375, 71892991, 268435455, 34242559, 267011856, 268419583, 268435332, 266606719, 268435455, 268435455, 268435343, 23058303, 90177535, 268435341),
    (268435455, 268435455, 21135359, 268425104, 268435455, 268435455, 90177535, 268435455, 268435455, 39845887, 268435455, 266502143, 106954751, 268420991, 268426239, 268435455),
    (268435455, 268435455, 268435455, 268435455, 266616831, 268435455, 266492685, 73388543, 268435455, 268435349, 268419583, 268435455, 266895359, 35651583, 268435455, 268435455),
    (106939391, 268435455, 268424191, 266403839, 31457279, 268435332, 35651583, 268435455, 268435455, 268435455, 268435455, 6279679, 267075583, 268435455, 268435455, 266567679),
    (268435455, 266502064, 268435455, 268435455, 106954636, 268435455, 268435455, 268435455, 268435455, 268435455, 268435455, 268435381, 268435455, 268435455, 268435455, 8388607),
    (268435372, 268435341, 268435455, 90177535, 268435372, 268435364, 268435455, 268435367, 268435364, 268435455, 268435455, 267207167, 268435455, 268435455, 102760447, 74273279),
    (27251711, 266606591, 268435455, 268435349, 268435455, 268435455, 268435455, 266567559, 268435455, 268435455, 268435455, 268435455, 268422015, 268435455, 39845887, 268435455),
    (31457164, 268435455, 268435455, 268435455, 268435455, 268435455, 268435455, 267157503, 266619007, 268435455, 268422015, 268435455, 268421247, 266633215, 268435455, 268435455),
    (268435455, 268435455, 106954751, 268435455, 268435455, 268422015, 268435455, 268435455, 268420991, 268435455, 268435455, 268435455, 268435455, 268435455, 268424703, 268420607),
    (268435455, 268426111, 268435455, 39845887, 267026431, 267157503, 268435455, 90177535, 268435455, 268435455, 100941823, 268435455, 268435455, 268435455, 268435455, 268435455),
    (268435380, 268435455, 39845813, 268435455, 268426111, 268435455, 268435455, 268424703, 268435455, 268435455, 105070591, 268435455, 268435455, 268435455, 268435455, 268435349),
    (268435455, 268435344, 268435455, 268435376, 39845887, 268435455, 268435455, 268435455, 268435455, 268435455, 268435455, 266436607, 268435455, 267157503, 268435455, 266698672),
    (268426111, 267157503, 268435344, 268435455, 268435455, 268435455, 268435455, 268435375, 94371756, 100958207, 268435455, 268420607, 268435455, 268435455, 106954751, 268435455),
    (44040191, 268435455, 268426239, 268435455, 266502143, 268435455, 38013823, 268420607, 115343359, 267157503, 268435455, 25165823, 268435455, 268435455, 268421631, 268435455),
    (115343252, 268435455, 268435455, 268435455, 115343359, 268426111, 23068597, 268435455, 266551295, 268435455, 268420607, 268435455, 267157503, 268435455, 268435455, 268424703),
    (268426239, 268435380, 268435455, 268435455, 268435380, 39845804, 268435455, 266698645, 268435455, 268435372, 268435349, 268435455, 39845887, 39832447, 268435455, 267091967),
    (268435455, 268435455, 102747135, 268435455, 268422015, 268435351, 268435455, 268435455, 268435455, 268435455, 268435455, 268435455, 268422143, 268435455, 268425727, 268435455),
    (268435455, 268435455, 268435455, 109051903, 268435455, 266616831, 268420607, 268435455, 268435340, 268435340, 268435455, 268435455, 268435455, 268435455, 268435351, 268435383),
    (268435455, 268435455, 268435455, 268435455, 48234388, 268435455, 268435455, 268435455, 268435455, 268435455, 268435455, 268435455, 268435455, 268435351, 268435455, 268425727),
    (268435455, 268435455, 268435455, 268435351, 268435455, 268435455, 268435455, 268435351, 268435455, 268435455, 266633215, 268424703, 268435455, 268435455, 268435455, 268435455),
    (268435455, 268435455, 268435348, 268435455, 266633215, 268435455, 268435455, 268435455, 268426111, 268435455, 39845887, 268435455, 266633215, 268435455, 268435455, 268435455),
    (268435455, 268435455, 266633215, 268435455, 268435455, 268435455, 268435455, 109042175, 268435455, 268435455, 268435455, 268435455, 268435455, 268435455, 268435455, 41929215),
    (268435455, 268435455, 268435455, 268435455, 268435455, 268435455, 102760447, 267223039, 267157396, 268435455, 268421631, 268435455, 268435455, 268435455, 268435455, 268435455),
    (268435455, 268435455, 268435455, 268435455, 268435455, 268435455, 268435455, 268435381, 268435455, 268435455, 268435455, 268425727, 268426239, 268435455, 268435455, 268435455),
    (268435455, 268435455, 268435455, 268435381, 268435455, 268435381, 268435372, 268435455, 48221055, 268435455, 268435455, 268435455, 268435455, 106954751, 268435455, 268435455),
    (268435455, 268435455, 268435455, 268435455, 268435455, 268435383, 106954751, 268421631, 268435455, 106954751, 268425727, 268435455, 268435455, 268435455, 268435455, 268435455),
    (268435455, 268435455, 268435455, 268435455, 268435455, 268435455, 268435455, 268435455, 268435455, 268435455, 268435455, 268435455, 268435455, 268435455, 268435455, 268435455),
    (268435455, 268435455, 268435455, 268435455, 268435455, 268435455, 268435383, 268435455, 268435455, 268435455, 268435455, 268435455, 268435455, 268435455, 268435455, 268435455),
    (268435455, 268435455, 268435455, 268435455, 268435455, 268435455, 268425727, 268435455, 268435380, 268435455, 268435455, 268435455, 268435455, 268435455, 268435455, 268435455),
    (268435455, 268435455, 268435455, 268435455, 268435455, 268435455, 268435455, 268435455, 268435455, 268435455, 268435455, 268435455, 268435455, 268435455, 268435455, 268435455),
    (268435455, 268435455, 268435455, 268435455, 268435455, 268435455, 268435349, 268435455, 268435455, 268435455, 268435455, 268435455, 268435455, 268435455, 268435455, 268435455),
    (268435455, 268435455, 268435455, 268435455, 268435455, 268435455, 268435455, 268435455, 268435455, 268435455, 268435455, 266652159, 268435455, 268435455, 268435455, 268435455),
    (268435455, 268435455, 268435455, 268435455, 268435455, 268435455, 268435455, 268435455, 268435455, 268435455, 268435455, 268435455, 268435455, 268435455, 268435455, 268435455),
    (268435455, 268435455, 268435455, 268435455, 268435455, 268435455, 268435455, 268435455, 268435455, 268435455, 268435455, 268435455, 268435455, 268435455, 268435455, 268435455),
    (268435455, 268435455, 268435455, 268435455, 268435455, 268435455, 268435455, 268435455, 268435455, 268435455, 268435455, 268435455, 268435455, 268435455, 268435455, 268435455),
    (268435455, 268435455, 268435455, 268435455, 268435455, 268435455, 268435455, 268435455, 268435455, 268435455, 268435455, 268435455, 268435455, 268435455, 268435455, 268435455),
    (268435455, 268435455, 268435455, 268435455, 268435455, 268435455, 268435455, 268435455, 268435455, 268435455, 268435455, 268435455, 268435455, 268435455, 268435455, 268435455),
    (268435455, 268435455, 268435455, 268435455, 268435455, 268435455, 268435455, 268435455, 268435455, 268435455, 268435455, 268435455, 268435455, 268435455, 268435455, 268435455),
    (268435455, 268435455, 268435455, 268435455, 268435455, 268435455, 268435455, 268435455, 268435455, 268435455, 268435455, 268435455, 268435455, 268435455, 268435455, 268435455),
    (268435455, 268435455, 268435455, 268435455, 268435455, 268435455, 268435455, 268435455, 268435455, 268435455, 268435455, 268435455, 268435455, 268435455, 268435455, 268435455),
)
COUNT = len(ARRIVALS)
LAG = 6
PARTS = 3
EARLY = 2
VMEM_LIMIT = 60 * 1024 * 1024


def pick(values, p):
    values = list(values)
    bit = 1
    while len(values) > 1:
        if len(values) % 2:
            values.append(values[-1])
        odd = (p // bit) % 2 == 1
        values = [jnp.where(odd, b, a) for a, b in zip(values[::2], values[1::2])]
        bit *= 2
    return values[0]


def kernel(
    q_ref, k_ref, v_ref, mask_ref, w_ref, out_ref,
    kv, qs, masks, bias, wts, att, attended, top, total, accum, proj,
    kv_recv, out_send, first_send, pass_send, q_recv, q_local, kv_local, swap_send,
    w_recv, w_send, w_local, w_pass_recv, w_pass_send, att_recv, att_send, mask_sem,
):
    i = lax.axis_index("ctx")
    z = lax.axis_index("head")
    c = i % 2
    p = i // 2
    x = p // 4
    y = p % 4
    twin = (p * 2 + 1 - c, z)
    neighbours = (((x + 1) % 4) * 4 + y, ((x + 3) % 4) * 4 + y, x * 4 + (y + 1) % 4, x * 4 + (y + 3) % 4)

    def slot_of(delta):
        slot = jnp.where(delta == -2, 3, jnp.where(delta == 2, 4, 7))
        slot = jnp.where(delta == -1, 1, jnp.where(delta == 1, 2, slot))
        slot = jnp.where((delta == -4) | (delta == 12), 5, slot)
        return jnp.where((delta == 4) | (delta == -12), 6, slot)

    def remote(src, dst, send, recv, device):
        return pltpu.make_async_remote_copy(
            src_ref=src, dst_ref=dst, send_sem=send, recv_sem=recv, device_id=device, device_id_type=MESH
        )

    barrier = pltpu.get_barrier_semaphore()
    greeted = [(there * 2 + core, z) for there in neighbours for core in (0, 1)] + [twin]
    for dz in (1, 2, 3):
        greeted += [(i, (z + dz) % 4), (p * 2 + 1 - c, (z + dz) % 4)]
    for device in greeted:
        pl.semaphore_signal(barrier, inc=1, device_id=device, device_id_type=MESH)

    my_rows = pl.ds(pl.multiple_of(c * FRAME, FRAME), FRAME)
    twin_rows = pl.ds(pl.multiple_of((1 - c) * FRAME, FRAME), FRAME)

    def columns(core, h):
        return pl.ds(pl.multiple_of((HEADS_CORE * core + h) * HEAD_DIM, HEAD_DIM), HEAD_DIM)

    def swap_kv(h, which):
        ref = (k_ref, v_ref)[which]
        return remote(ref.at[:, columns(1 - c, h)], kv.at[0, which, h, my_rows, :], swap_send.at[which, h], kv_recv.at[0, which, h], twin)

    def swap_q(h):
        return remote(q_ref.at[:, columns(1 - c, h)], qs.at[h, my_rows, :], swap_send.at[2, h], q_recv.at[h], twin)

    def keep_kv(h, which):
        ref = (k_ref, v_ref)[which]
        return pltpu.make_async_copy(ref.at[:, columns(c, h)], kv.at[0, which, h, my_rows, :], kv_local.at[which, h])

    def keep_q(h):
        return pltpu.make_async_copy(q_ref.at[:, columns(c, h)], qs.at[h, my_rows, :], q_local.at[h])

    swap_mask = remote(mask_ref, masks.at[c], mask_sem.at[0], mask_sem.at[1], twin)
    keep_mask = pltpu.make_async_copy(mask_ref, masks.at[c], mask_sem.at[2])

    def w_block(h, core, zz):
        rows = pl.ds(pl.multiple_of((HEADS_CORE * core + h) * HEAD_DIM, HEAD_DIM), HEAD_DIM)
        return w_ref.at[rows, pl.ds(pl.multiple_of(zz * 768, 768), 768)]

    def w_copy(h, dz):
        zz = (z + dz) % 4
        return remote(w_block(h, c, zz), wts.at[h, z * 2 + c], w_send.at[h, dz - 1], w_recv.at[h, dz - 1], (i, zz))

    def w_keep(h, core):
        return pltpu.make_async_copy(w_block(h, core, z), wts.at[h, z * 2 + core], w_local.at[h, core])

    def w_pass(h, dz):
        place = ((z + 4 - dz) % 4) * 2 + c
        return remote(wts.at[h, place], wts.at[h, place], w_pass_send.at[h, dz - 1], w_pass_recv.at[h, dz - 1], twin)

    def own_copy(h, which, group, direction, sem):
        there = neighbours[direction]
        ref = (k_ref, v_ref)[which]
        core = c if group == 0 else 1 - c
        return remote(
            ref.at[:, columns(core, h)], kv.at[slot_of(p - there), which, h, my_rows, :],
            sem, kv_recv.at[slot_of(p - there), which, h], (there * 2 + core, z),
        )

    def own_first(h, which, group, direction):
        ref = (k_ref, v_ref)[which]
        there = neighbours[direction]
        return remote(
            ref.at[:, columns(group, h)], kv.at[8, which, h, 0:FRAME, :],
            first_send.at[group, which, h, direction], kv_recv.at[8, which, h], (there * 2 + group, z),
        )

    def first_sent(word, action):
        slot = word & 15
        h = (word >> 4) & 3
        which = (word >> 6) & 1
        some = ((word >> 11) & 15) > 0

        @pl.when(some & (slot == 0) & (c == 0))
        def _():
            for direction in range(4):
                for kind in (0, 1):
                    @pl.when((((word >> (11 + direction)) & 1) == 1) & (which == kind))
                    def _():
                        for group in (0, 1):
                            action(own_first(h, kind, group, direction))

        @pl.when(some & (slot > 0))
        def _():
            for direction in range(4):
                @pl.when(((word >> (11 + direction)) & 1) == 1)
                def _():
                    action(remote(
                        kv.at[slot, which, h, 0:FRAME, :], kv.at[8, which, h, 0:FRAME, :],
                        pass_send.at[which, h, direction], kv_recv.at[8, which, h], (neighbours[direction] * 2 + c, z),
                    ))

    def out_done(direction, turn):
        whole = kv.at[0, 0, 0]
        remote(whole, whole, out_send.at[direction, turn], kv_recv.at[0, 0, 0], twin).wait_send()

    def send(packed, sent):
        after = []
        for direction in range(4):
            code = (packed >> (7 * direction)) & 127
            slot = code & 7
            h = (code >> 3) & 3
            which = (code >> 5) & 1
            turn = sent[direction] % 2

            @pl.when(code < 127)
            def _():
                pl.when(sent[direction] > 1)(lambda: out_done(direction, turn))
                sem = out_send.at[direction, turn]
                for kind in (0, 1):
                    @pl.when((slot == 0) & (which == kind))
                    def _():
                        for group in (0, 1):
                            own_copy(h, kind, group, direction, sem).start()

                @pl.when(slot > 0)
                def _():
                    there = neighbours[direction]
                    far = jnp.where(p < 8, 8, -8)
                    near = jnp.where(slot == 1, -1, jnp.where(slot == 2, 1, jnp.where(slot == 3, -2, 2)))
                    off = jnp.where(slot < 5, near, jnp.where(slot == 5, -4, jnp.where(slot == 6, 4, far)))
                    target = slot_of(p + off - there)
                    remote(
                        kv.at[slot, which, h], kv.at[target, which, h], sem, kv_recv.at[target, which, h], (there * 2 + c, z)
                    ).start()

            after.append(sent[direction] + jnp.where(code < 127, 1, 0))
        return tuple(after)

    def start(copy):
        copy.start()

    def finish(copy):
        copy.wait_send()

    for h in range(HEADS_CORE):
        keep_q(h).start()
        keep_kv(h, 0).start()
        keep_kv(h, 1).start()
    keep_mask.start()
    pl.semaphore_wait(barrier, len(greeted))
    sent = (jnp.int32(0),) * 4
    for n in range(EARLY):
        sent = send(pick(SENDS[n], p), sent)
        first_sent(pick(ARRIVALS[n], p), start)
    swap_mask.start()
    for h in range(HEADS_CORE):
        swap_q(h).start()
        swap_kv(h, 0).start()
        swap_kv(h, 1).start()
    for h in range(HEADS_CORE):
        for dz in (1, 3, 2):
            w_copy(h, dz).start()
    for h in range(HEADS_CORE):
        for core in (0, 1):
            w_keep(h, core).start()

    top[...] = jnp.full_like(top, NEG)
    total[...] = jnp.zeros_like(total)
    accum[...] = jnp.zeros_like(accum)
    proj[...] = jnp.zeros_like(proj)

    keep_mask.wait()
    swap_mask.wait_recv()
    blocks = masks.shape[2]
    same = lax.broadcasted_iota(jnp.int32, (blocks, blocks), 0) == lax.broadcasted_iota(jnp.int32, (blocks, blocks), 1)
    anchor_rows = lax.broadcasted_iota(jnp.int32, (blocks, BLOCK), 0) < FRAME // BLOCK
    for core in (0, 1):
        for b in (0, 1):
            line = jnp.where(same, jnp.broadcast_to(masks[core, b : b + 1, :], (blocks, blocks)), 0)
            column = jnp.sum(line.astype(jnp.float32), axis=1, keepdims=True)
            wide = jnp.broadcast_to(column, (blocks, BLOCK))
            added = jnp.where((wide > 0) & ~anchor_rows, 0.0, NEG).astype(jnp.float32)
            for n in range(blocks // 2):
                bias[core, n, :, b * BLOCK : (b + 1) * BLOCK] = added[2 * n : 2 * n + 2, :]
        bias[core, 32] = jnp.zeros_like(bias[core, 32])

    def attend(slot, h, source, parts):
        scores = []
        for frame, halves in parts:
            rows = slice(frame * FRAME, (frame + 1) * FRAME)
            held = slice(halves[0] * FRAME, (halves[-1] + 1) * FRAME)
            scores.append(lax.dot_general(
                kv[slot, 0, h, held, :], qs[h, rows, :], (((1,), (1,)), ((), ())), preferred_element_type=jnp.float32
            ))
        weights = []
        factors = []
        for (frame, halves), score in zip(parts, scores):
            rows = slice(frame * FRAME, (frame + 1) * FRAME)
            length = len(halves) * FRAME
            score = score * EXP2_SCALE
            if source is not None:
                added = [bias[frame, source * 2 + half] for half in halves]
                added = added[0] if len(added) == 1 else jnp.concatenate(added, axis=0)
                score = (score.reshape(length // BLOCK, BLOCK, FRAME) + added[:, None, :]).reshape(length, FRAME)
            before = top[h, :, rows]
            now = jnp.maximum(before, jnp.max(score, axis=0, keepdims=True))
            weight = jnp.exp2(score - now)
            factor = jnp.exp2(before - now)
            total[h, :, rows] = total[h, :, rows] * factor + jnp.sum(weight, axis=0, keepdims=True)
            top[h, :, rows] = now
            weights.append(weight.astype(jnp.bfloat16))
            factors.append(factor)
        for (frame, halves), weight, factor in zip(parts, weights, factors):
            rows = slice(frame * FRAME, (frame + 1) * FRAME)
            held = slice(halves[0] * FRAME, (halves[-1] + 1) * FRAME)
            mixed = lax.dot_general(
                kv[slot, 1, h, held, :], weight, (((0,), (0,)), ((), ())), preferred_element_type=jnp.float32
            )
            accum[h, :, rows] = accum[h, :, rows] * factor + mixed

    def att_copy(h, dz, cross):
        core = 1 - c if cross else c
        rows = twin_rows if cross else my_rows
        return remote(
            attended.at[h, rows, :], att.at[h, z * 2 + c], att_send.at[h, dz, cross], att_recv.at[h, dz, cross],
            (p * 2 + core, (z + dz) % 4),
        )

    def project(h):
        for core in (0, 1):
            w_keep(h, core).wait()
        for dz in (0, 1, 3, 2):
            for cross in (0, 1):
                if dz or cross:
                    att_copy(h, dz, cross).wait_recv()
            if dz:
                w_pass(h, dz).wait_recv()
            place = ((z + 4 - dz) % 4) * 2
            left = jnp.concatenate([att[h, place], att[h, place + 1]], axis=1)
            for n in range(3):
                cols = slice(n * 256, (n + 1) * 256)
                right = jnp.concatenate([wts[h, place, :, cols], wts[h, place + 1, :, cols]], axis=0)
                part = proj[:, cols] + jnp.dot(left, right, preferred_element_type=jnp.float32)
                if h == HEADS_CORE - 1 and dz == 2:
                    out_ref[:, cols] = part.astype(out_ref.dtype)
                else:
                    proj[:, cols] = part

    def step(arrivals, sends, n, carry):
        sent, recent = carry
        word = pick(arrivals, n)
        slot = word & 15
        h = (word >> 4) & 3
        which = (word >> 6) & 1
        source = (word >> 18) & 15

        @pl.when((slot > 0) & (slot < 8))
        def _():
            whole = kv.at[slot, which, h]
            remote(whole, whole, pass_send.at[0, 0, 0], kv_recv.at[slot, which, h], twin).wait_recv()

        @pl.when(slot == 8)
        def _():
            first = kv.at[8, which, h, 0:FRAME, :]
            remote(first, first, pass_send.at[0, 0, 0], kv_recv.at[8, which, h], twin).wait_recv()

        first_sent(word, start)
        sent = send(pick(sends, n), sent)

        @pl.when(slot == 9)
        def _():
            keep_q(h).wait()
            swap_q(h).wait_recv()
            for kind in (0, 1):
                keep_kv(h, kind).wait()
                swap_kv(h, kind).wait_recv()
            attend(0, h, p, ((0, (0, 1)), (1, (0, 1))))

        @pl.when(((word >> 15) & 1) == 1)
        def _():
            @pl.when(slot == 1)
            def _():
                attend(1, h, source, ((0, (0, 1)), (1, (1,))))

            @pl.when(slot == 2)
            def _():
                attend(2, h, source, ((0, (0,)), (1, (0, 1))))

            @pl.when((slot > 2) & (slot < 8))
            def _():
                attend(slot, h, source, ((0, (0,)), (1, (1,))))

        @pl.when(((word >> 17) & 1) == 1)
        def _():
            attend(jnp.where(slot == 9, 0, slot), h, None, ((0, (0,)), (1, (0,))))

        @pl.when(((word >> 16) & 1) == 1)
        def _():
            attended[h] = jnp.transpose(accum[h] * (1.0 / total[h])).astype(jnp.bfloat16)
            for dz in (2, 1, 3, 0):
                for cross in (0, 1):
                    if dz or cross:
                        att_copy(h, dz, cross).start()
            att[h, z * 2 + c] = attended[h, my_rows, :]

        @pl.when(slot == 10)
        def _():
            for dz in (1, 3, 2):
                w_copy(h, dz).wait_recv()
                w_pass(h, dz).start()

        first_sent(recent[0], finish)
        return sent, recent[1:] + (word,)

    carry = sent, (jnp.int32(15),) * (LAG - EARLY) + tuple(pick(line, p) for line in ARRIVALS[:EARLY])
    length = -(-(COUNT - EARLY) // PARTS)
    for begin in range(EARLY, COUNT, length):
        end = min(begin + length, COUNT)
        arrivals = [pick(line, p) for line in ARRIVALS[begin:end]]
        sends = [pick(line, p) for line in SENDS[begin:end]]
        carry = lax.fori_loop(0, end - begin, functools.partial(step, arrivals, sends), carry)
    recent = carry[1]

    def finish_heads(heads):
        for h in heads:
            for dz in range(4):
                for cross in (0, 1):
                    if dz or cross:
                        att_copy(h, dz, cross).wait_send()

    project(0)
    project(1)
    for word in recent:
        first_sent(word, finish)
    for direction in range(4):
        for turn in (0, 1):
            out_done(direction, turn)
    for h in range(HEADS_CORE):
        for which in (0, 1):
            swap_kv(h, which).wait_send()
        swap_q(h).wait_send()
        for dz in (1, 2, 3):
            w_copy(h, dz).wait_send()
            w_pass(h, dz).wait_send()
    swap_mask.wait_send()
    finish_heads((0, 1))
    project(2)
    finish_heads((2,))


def body(queries, keys, values, block_mask, w_out):
    bf16, f32, dma = jnp.bfloat16, jnp.float32, pltpu.SemaphoreType.DMA
    heads = HEADS_CORE
    anywhere = pl.BlockSpec(memory_space=pl.ANY)
    return pl.pallas_call(
        kernel,
        out_shape=jax.ShapeDtypeStruct((FRAME, 768), bf16),
        in_specs=[anywhere, anywhere, anywhere, pl.BlockSpec(memory_space=pltpu.VMEM), anywhere],
        out_specs=pl.BlockSpec(memory_space=pltpu.VMEM),
        scratch_shapes=[
            pltpu.VMEM((9, 2, heads, 2 * FRAME, HEAD_DIM), bf16),
            pltpu.VMEM((heads, 2 * FRAME, HEAD_DIM), bf16),
            pltpu.VMEM((2, 2, 64), jnp.int32),
            pltpu.VMEM((2, 33, 2, FRAME), f32),
            pltpu.VMEM((heads, 8, HEAD_DIM, 768), bf16),
            pltpu.VMEM((heads, 8, FRAME, HEAD_DIM), bf16),
            pltpu.VMEM((heads, 2 * FRAME, HEAD_DIM), bf16),
            pltpu.VMEM((heads, 1, 2 * FRAME), f32),
            pltpu.VMEM((heads, 1, 2 * FRAME), f32),
            pltpu.VMEM((heads, HEAD_DIM, 2 * FRAME), f32),
            pltpu.VMEM((FRAME, 768), f32),
            dma((9, 2, heads)), dma((4, 2)), dma((2, 2, heads, 4)), dma((2, heads, 4)), dma((heads,)), dma((heads,)), dma((2, heads)), dma((3, heads)),
            dma((heads, 3)), dma((heads, 3)), dma((heads, 2)), dma((heads, 3)), dma((heads, 3)),
            dma((heads, 4, 2)), dma((heads, 4, 2)), dma((3,)),
        ],
        compiler_params=pltpu.CompilerParams(
            collective_id=0, has_side_effects=True, vmem_limit_bytes=VMEM_LIMIT
        ),
        name="radial_attention",
    )(queries, keys, values, block_mask, w_out)


def solution(mesh):
    placed = (P("ctx", "head"), P("ctx", "head"), P("ctx", "head"), P("ctx", None), P("head", None))
    return jax.shard_map(
        body, mesh=mesh, in_specs=placed, out_specs=P("ctx", "head"), check_vma=False
    )
```

```python
import functools

import jax
import jax.numpy as jnp
from jax import lax
from jax.experimental import pallas as pl
from jax.experimental.pallas import tpu as pltpu
from jax.sharding import PartitionSpec as P

HEAD_DIM = 128
BLOCK = 128
FRAME = 256
HEADS_CORE = 3
MESH = pl.DeviceIdType.MESH
NEG = -1e30
EXP2_SCALE = HEAD_DIM ** (-0.5) * 1.4426950408889634

ARRIVALS = (
    (15, 15, 15, 15, 15, 15, 15, 15, 15, 15, 15, 15, 15, 15, 15, 15),
    (0, 15, 15, 15, 15, 15, 15, 15, 15, 15, 15, 15, 15, 15, 15, 15),
    (16448, 262153, 524297, 786441, 1048585, 1310729, 1572873, 1835017, 2097161, 2359305, 2621449, 2883593, 3145737, 3407881, 3670025, 3932169),
    (131081, 262169, 524313, 6216, 1048601, 1310745, 1572889, 1835033, 2097177, 2359321, 2621465, 2883609, 3145753, 3407897, 3670041, 3932185),
    (131097, 524354, 15, 786457, 15, 15, 15, 15, 15, 15, 15, 15, 15, 15, 15, 786518),
    (3145797, 262185, 524329, 786473, 1048617, 1310761, 1572905, 1835049, 2097193, 2359337, 2621481, 2883625, 3145769, 3407913, 3670057, 3932201),
    (131113, 3407877, 3670037, 3932229, 69, 262149, 524293, 786437, 1048581, 1310725, 1572933, 1835013, 22, 2359301, 2621509, 2883653),
    (1048582, 1310790, 1572934, 1835014, 2097222, 2359302, 2621446, 2883590, 3145798, 3407878, 3670086, 3932166, 2097157, 262214, 524310, 3670017),
    (262210, 1, 262209, 524289, 1310786, 1048657, 1310721, 1572929, 2359298, 2097153, 2359361, 2621441, 3407938, 3670082, 3407873, 2916357),
    (4112, 3407941, 786498, 3932165, 188421, 1572930, 1835074, 2883670, 1048661, 2621506, 2883586, 1867845, 2097173, 3145729, 3932162, 3702849),
    (20560, 1310742, 3670101, 1867846, 2097174, 262165, 557125, 1605633, 3178502, 1310805, 1572885, 2621457, 86, 2359381, 2654213, 72),
    (1081414, 163905, 1605638, 557121, 1343490, 2392134, 2621462, 819269, 2359378, 3440710, 3702790, 3932182, 3407890, 3145809, 524374, 15),
    (294914, 15, 819202, 15, 15, 1081361, 1343553, 16456, 15, 2129985, 2359377, 15, 38, 262230, 3407953, 15),
    (15, 15, 262161, 15, 16405, 1572882, 1835026, 2916374, 1081365, 2621474, 2916418, 15, 15, 3670034, 3964994, 2883605),
    (15, 15, 15, 1835094, 15, 15, 15, 15, 15, 15, 15, 15, 15, 15, 15, 3670033),
    (15, 15, 15, 3932245, 2129926, 15, 15, 15, 3145766, 1310821, 15, 15, 3407970, 15, 3407905, 15),
    (1048662, 15, 15, 524305, 1310738, 15, 2654294, 1572945, 15, 2621522, 15, 1835093, 2130005, 15, 15, 1835079),
    (524292, 15, 15, 1835110, 2097254, 262181, 15, 786533, 2359330, 15, 1605717, 2654289, 2097189, 2359397, 524326, 2883685),
    (557124, 3407957, 1572966, 3932261, 1343570, 2359318, 15, 3932183, 3145814, 15, 3670118, 786519, 10, 262246, 15, 3670049),
    (1081366, 1310822, 786450, 557137, 3145799, 1572898, 524309, 1605649, 15, 3407894, 2392081, 1867797, 24, 15, 2621477, 10),
    (262226, 15, 294993, 10, 10, 2392150, 1310801, 137224, 2392162, 2097233, 2883602, 2621537, 3670020, 15, 3932178, 3407939),
    (10, 1343526, 1605670, 4184, 786433, 294997, 1867858, 10, 10, 3440726, 3702822, 3932198, 3702852, 3178513, 2654309, 3407891),
    (2097159, 3407973, 10, 1048578, 1572868, 1605730, 557141, 3932231, 1835009, 2097249, 1572901, 10, 139352, 3702866, 3965010, 15),
    (32, 10, 2621511, 15, 15, 10, 1310753, 2097218, 26695, 10, 2359329, 3145794, 2883585, 3178561, 10, 15),
    (2097175, 4113, 262241, 524385, 15, 1048641, 10, 24, 2621444, 262151, 2916434, 2359299, 1048583, 3670050, 1572935, 15),
    (4192, 786500, 819282, 2883655, 180309, 2056, 1835106, 1310723, 165895, 2883588, 10, 3965014, 3670036, 10, 3145731, 15),
    (15, 163921, 2654215, 2883607, 3178503, 1081345, 3670087, 2097170, 15, 2916420, 524295, 15, 1081415, 1310727, 3145811, 1867783),
    (15, 819204, 15, 1081410, 1605700, 15, 2120, 3964935, 3178518, 262167, 2883682, 786439, 3702868, 1343559, 1605639, 3407971),
    (2130007, 2359367, 786466, 557089, 2130006, 3407879, 15, 786517, 2654276, 2129937, 524375, 2392131, 8264, 1310807, 1572887, 3440643),
    (2195527, 2392071, 2621463, 2916359, 1572884, 1835076, 15, 1343555, 3178598, 294999, 2097155, 2359379, 2883601, 1343511, 3932258, 2916389),
    (294930, 2359383, 67, 2916439, 8293, 2359334, 3702791, 819221, 2621476, 262183, 557079, 819271, 2883681, 3145825, 1572967, 3440723),
    (262242, 2392087, 2654295, 135176, 819265, 2392166, 1867810, 2359300, 2621460, 294983, 2392161, 15, 1048663, 3932228, 3178515, 1835095),
    (1048614, 786452, 165891, 262147, 1605716, 3440711, 3670039, 15, 2654292, 2056, 2916386, 16392, 3670052, 3964932, 1605719, 1867799),
    (524308, 33, 2621479, 26, 26, 1048609, 1048659, 1310803, 1572867, 2129953, 557127, 3407940, 24680, 3178529, 3964962, 4184),
    (15, 163937, 819298, 1048594, 3145767, 1835028, 3702871, 26, 26, 2883604, 2120, 3145762, 26, 4120, 1605671, 1835111),
    (622676, 15, 2654311, 3932197, 524291, 1081441, 1081363, 1343507, 15, 135240, 26, 2392083, 131080, 1310823, 15, 26),
    (294946, 819284, 1048580, 294979, 1310818, 15, 3670119, 147544, 15, 26, 3145732, 131144, 2621443, 139352, 15, 3440675),
    (26, 26, 26, 1310724, 622659, 3407895, 3702823, 1310755, 8279, 1835075, 2097235, 2359331, 3440642, 2883587, 26, 3702881),
    (1081446, 15, 14355, 2883687, 786529, 26, 26, 3965015, 180247, 2916436, 1605637, 26, 1081367, 15, 15, 3702865),
    (2097255, 15, 1572886, 262163, 1572964, 1867860, 2097220, 2097250, 1835025, 3407910, 3178564, 3407892, 2129989, 26, 3440657, 15),
    (524388, 1343494, 1048660, 1409092, 2129958, 3440727, 15, 2916422, 2392130, 1867779, 2097251, 15, 2654275, 3702786, 3440705, 4200),
    (15, 622594, 163923, 131096, 786513, 1605634, 1048643, 2392132, 1605699, 1343557, 2392065, 2392163, 3440722, 2916419, 2621461, 196616),
    (15, 3407909, 1605718, 294995, 524307, 786499, 15, 15, 1867841, 2883684, 3670038, 3964998, 2981953, 3932180, 72, 2916437),
    (557092, 786468, 1146900, 262243, 1343522, 294981, 2129924, 2359380, 1572883, 2719746, 133128, 1835045, 3440674, 8, 3145827, 1867815),
    (15, 2359335, 294913, 1867798, 3145751, 1835108, 2654278, 2195458, 1146949, 12312, 3702870, 2654273, 2621523, 3965012, 2654293, 42),
    (15, 2392167, 14371, 1310804, 819217, 131144, 2097172, 3932263, 26663, 2916388, 2129955, 3440644, 42, 1343527, 88, 196632),
    (15, 819300, 1146948, 2916391, 3178583, 1867812, 1343505, 1343587, 42, 1835091, 3145812, 88, 1048615, 131144, 204824, 15),
    (42, 1343574, 178275, 1081426, 1605668, 104, 131080, 819237, 2392082, 139352, 2195523, 3145746, 1081447, 2457669, 3440737, 196648),
    (15, 524306, 42, 42, 622675, 819203, 524389, 42, 2654308, 1343509, 524327, 3244034, 2654227, 4200, 3178531, 15),
    (2195495, 622674, 294945, 1409044, 42, 786451, 15, 2392084, 1605715, 42, 42, 819223, 2981969, 2392085, 3178563, 15),
    (15, 42, 1048612, 294947, 3178599, 1933316, 16472, 1572961, 1572963, 2654226, 24, 131096, 2130021, 2883603, 42, 15),
    (15, 15, 1146980, 40, 524387, 1605714, 1048611, 2359396, 1933393, 295015, 131160, 3440724, 2621475, 2981971, 196616, 15),
    (15, 524386, 15, 1310756, 557091, 3407975, 2130004, 2195538, 1835041, 1933331, 2129939, 786535, 131112, 3932196, 24616, 15),
    (15, 622626, 15, 1048674, 180261, 42, 196632, 2392100, 163943, 1835107, 3244052, 42, 3702884, 3702882, 196712, 15),
    (15, 15, 15, 131176, 884769, 88, 1081443, 2883686, 1605667, 104, 3145828, 20584, 2654307, 42, 15, 15),
    (15, 15, 15, 1867814, 15, 131096, 42, 1605665, 1048613, 1867811, 557159, 3244114, 2981921, 2392101, 15, 15),
    (15, 15, 15, 1343588, 15, 884819, 2097252, 3964967, 1867873, 131112, 1605733, 2654241, 15, 2883683, 15, 15),
    (15, 15, 15, 1146914, 15, 786467, 1081347, 104, 1146981, 1343525, 104, 1867877, 15, 3965028, 15, 15),
    (15, 15, 15, 15, 15, 819299, 2621478, 2129954, 15, 3440742, 3178532, 3178594, 15, 2916387, 15, 15),
    (15, 15, 15, 15, 15, 295013, 2129956, 2916390, 15, 2719842, 196648, 131112, 15, 196648, 15, 15),
    (15, 15, 15, 15, 15, 3440679, 1933314, 196648, 15, 15, 15, 3407972, 15, 15, 15, 15),
    (15, 15, 15, 15, 15, 196648, 18472, 15, 15, 15, 15, 3965030, 15, 15, 15, 15),
    (15, 15, 15, 15, 15, 15, 557093, 15, 15, 15, 15, 819239, 15, 15, 15, 15),
    (15, 15, 15, 15, 15, 15, 1343585, 15, 15, 15, 15, 3506212, 15, 15, 15, 15),
    (15, 15, 15, 15, 15, 15, 131176, 15, 15, 15, 15, 15, 15, 15, 15, 15),
    (15, 15, 15, 15, 15, 15, 2719846, 15, 15, 15, 15, 15, 15, 15, 15, 15),
)
SENDS = (
    (266339360, 67637248, 67109888, 69194752, 266993664, 67112960, 67637280, 69189632, 266342400, 524288, 67108896, 2080800, 266342432, 67108864, 67112968, 2080800),
    (266867712, 136200, 266867744, 2097056, 266473512, 525352, 16777224, 18862112, 266863624, 84545576, 33686528, 69194752, 266993791, 17436704, 17301544, 69190656),
    (268435455, 268435455, 268435455, 268435455, 268435455, 268435455, 268435455, 268435455, 268435455, 268435455, 268435455, 268435455, 268435455, 268435455, 268435455, 268435455),
    (268435455, 268435455, 268435455, 268435455, 268435455, 268435455, 268435455, 268435455, 268435455, 268435455, 268435455, 268435455, 268435455, 268435455, 268435455, 268435455),
    (268421128, 71964688, 266471432, 268435455, 266867720, 17438768, 34215976, 85972008, 266993704, 33686576, 84546576, 18859016, 266471551, 100926504, 84023423, 18863912),
    (266485669, 84688808, 267009960, 18874288, 266339455, 84150399, 100796432, 102750216, 267130896, 100930687, 267141040, 85983152, 266867839, 268424240, 33818751, 85968944),
    (267010047, 268435455, 268435455, 85983141, 268435365, 268435333, 268435455, 266436607, 268435455, 268435333, 268435455, 266436607, 268435455, 268435455, 268435365, 268435455),
    (14680063, 268424063, 268424063, 268435455, 81788927, 268435455, 268435455, 268435455, 81788927, 268435455, 268424063, 268435455, 268435333, 268435455, 268435455, 266371071),
    (268435455, 268435455, 268435455, 266371071, 268435455, 268435455, 268435455, 268435455, 6291455, 268435455, 268435455, 266371071, 73400319, 73400319, 268435455, 266436607),
    (268435455, 268435455, 73400319, 268435455, 268435455, 268435455, 268435455, 268435455, 268435455, 268435455, 6291455, 268435455, 268435341, 266371071, 268435455, 268435455),
    (268435368, 268435455, 268435455, 268424063, 31457157, 268435455, 268435455, 266371071, 268435455, 268435455, 268435455, 268435455, 268435455, 268435455, 268435333, 268435455),
    (81777535, 268435455, 268435455, 268435455, 268435455, 268435455, 268435455, 268435455, 268435455, 268435455, 268435455, 268420991, 23068671, 268435455, 268435455, 102749221),
    (268435455, 268420991, 6291455, 35651583, 268424063, 268435341, 268435455, 268435455, 266470149, 268435373, 268435455, 268435333, 268435455, 268435455, 268435455, 35651461),
    (268435376, 268435333, 268419967, 268435333, 268421247, 268435455, 268435455, 268420869, 268435455, 268435455, 73384831, 102760447, 267125887, 268435455, 268435455, 268435455),
    (266616831, 266895359, 268435341, 102749960, 266616831, 71979903, 266356485, 35641125, 266605695, 71321727, 268435341, 268435344, 266606719, 267026431, 71325567, 268435455),
    (267141119, 18874367, 267141119, 268435455, 268435455, 266502143, 73400319, 266960895, 268435455, 268435455, 266895359, 35651583, 268435455, 23068671, 268435455, 266567679),
    (268425087, 102760357, 268435373, 266502143, 267141119, 23068671, 268435455, 268435455, 48234495, 268435455, 267026431, 266502143, 106954669, 268424965, 268420991, 268435455),
    (268435455, 266371071, 266616831, 268426111, 268435455, 268435455, 266884901, 267026431, 268435455, 267131007, 268435373, 267026431, 268435455, 268435455, 267026431, 267223039),
    (268435455, 268435455, 268426111, 268435455, 268435455, 268420885, 23068671, 268435455, 268435455, 39845887, 268426111, 268425215, 268435455, 268435455, 6291455, 268435455),
    (268435455, 268435455, 23068671, 267026431, 23068671, 268435455, 268435455, 268435455, 39845887, 268435455, 268435455, 268435455, 268435455, 268435373, 268435349, 268435455),
    (6291455, 268426111, 268435455, 268435455, 268435455, 268435455, 268435455, 268435455, 268435455, 268435455, 23068671, 268435455, 268435455, 268424063, 268435455, 268423679),
    (268435455, 268435455, 268435455, 268435455, 268435455, 268435455, 268435455, 268435455, 268435455, 268435455, 268422015, 268435455, 268435455, 268435455, 268435381, 268420607),
    (268435455, 268435455, 268435455, 6291455, 268435332, 268435455, 268435455, 268435367, 268435455, 268435455, 268435349, 268435455, 268435455, 88244223, 268435455, 268435344),
    (268435332, 268435455, 268435455, 268435373, 268425343, 268435455, 268435455, 73400319, 268435455, 268435455, 268435455, 268435455, 266409855, 268435455, 268435455, 25165823),
    (268435455, 268435455, 268435455, 268435455, 115343359, 268435455, 268435455, 267223039, 266357508, 268435455, 90177535, 268419583, 268420991, 39845887, 268435455, 268435381),
    (268435455, 268435455, 90177535, 268435367, 266410879, 266895359, 268435455, 268419472, 268435455, 268435332, 266502143, 73400205, 268435455, 268435455, 268435455, 75497471),
    (31442815, 268435455, 266895271, 267157503, 266371071, 102760447, 268435455, 23068671, 268421247, 267011876, 268435455, 8388607, 268435455, 268421127, 21250559, 268435455),
    (268435364, 33704749, 266502064, 268435455, 268435364, 105005055, 268435455, 268435455, 268435455, 267157503, 268435455, 266567679, 94371839, 268424080, 88867839, 268435455),
    (268435455, 267026340, 39845887, 268435455, 268435455, 268435455, 267026431, 267091967, 266420132, 268435455, 268435455, 266916351, 268435455, 268435455, 268435343, 266403839),
    (266420223, 268435455, 268421119, 266633215, 268435340, 268435364, 90177535, 268423679, 77594623, 268435455, 106954751, 268435455, 266502143, 268435455, 268435455, 268419583),
    (268424191, 268424191, 268435455, 268425215, 268435455, 268422015, 268435455, 268435455, 31457279, 268435455, 268419583, 268435455, 268435455, 267157503, 268435455, 267059199),
    (90177535, 268435455, 268425215, 268435455, 268435455, 268426111, 268435455, 268435455, 268420991, 268424191, 267157503, 268424703, 268435455, 268435455, 268435455, 268424703),
    (268435455, 268435455, 268435455, 8388533, 267075583, 268435455, 105152399, 266567679, 268435455, 268435455, 268435455, 268435455, 268424191, 268435455, 268435375, 268435455),
    (266551180, 268435455, 268435455, 268435344, 268435455, 268435455, 268424703, 268424703, 268435455, 268435455, 39845887, 268435455, 268435455, 266633215, 268435455, 109051791),
    (106954751, 268435455, 106954751, 268435455, 268435455, 268435455, 268435375, 268435341, 268435455, 266633215, 268435455, 268435455, 268422015, 268435455, 268435455, 268435349),
    (267075583, 266633100, 268435455, 268435455, 268435372, 268435455, 268420607, 268435455, 266551212, 268435455, 268435455, 268435455, 268435455, 268435455, 39835135, 268435455),
    (268435372, 268435455, 268435332, 268435455, 106954751, 266633215, 39845887, 268435381, 268425087, 268435455, 266420223, 268435455, 268435455, 268435455, 268422015, 266665983),
    (268422015, 268421119, 268435455, 268435455, 268435455, 35651583, 268435455, 268420607, 268435455, 75497471, 268424703, 268435455, 268435455, 268435375, 268435455, 268435455),
    (268426111, 268435381, 268435455, 268435455, 268435455, 268435455, 268435455, 268435455, 268435455, 268435372, 268435455, 268435455, 268435455, 268421119, 102760447, 268435455),
    (268435455, 267157503, 268435351, 268435455, 111149055, 268435372, 268435455, 106954751, 42106764, 268435455, 268435364, 266534911, 268435455, 268435455, 268435455, 268426239),
    (268435380, 268435455, 267075583, 268435455, 268421940, 38567935, 268435364, 268435455, 115343359, 268419583, 268435455, 267142655, 268435455, 268435455, 268435455, 268435455),
    (39845887, 268435455, 268435455, 268435455, 267026431, 268435455, 268435455, 268435455, 268426004, 268435455, 268435455, 268435455, 268435455, 75488127, 268435455, 268435455),
    (267206655, 268435455, 268435455, 268435383, 268435455, 268435455, 268423679, 268421631, 268435455, 268435380, 268435455, 268435455, 268435455, 268435455, 268435455, 267082239),
    (268435455, 268435455, 268435455, 268435349, 268435455, 268435455, 266420223, 268435455, 268435455, 268435455, 268435455, 268425621, 268435455, 268435455, 268435455, 268435351),
    (113590271, 268422143, 268435455, 268435455, 268435455, 268435380, 268435455, 268435455, 268435455, 268435455, 268435455, 268435455, 268435455, 268435455, 268435455, 268435455),
    (268435348, 268435455, 268435383, 268435455, 268435455, 268435455, 268435340, 268435383, 268422143, 268435348, 268421631, 268435455, 268435455, 268435455, 268435455, 268435455),
    (268426239, 268435348, 268435455, 268435455, 268435381, 268435348, 268435455, 109042175, 268435455, 92274687, 267075583, 268435455, 268422143, 268435455, 106945023, 268421631),
    (268435455, 266616831, 268435455, 268435455, 44040191, 268435455, 268435455, 266698645, 268435455, 268435455, 268435455, 23068671, 268426239, 268435455, 268426239, 268435455),
    (48234495, 268435380, 268435455, 268435455, 268435455, 268435455, 268435455, 268435455, 267206580, 268435455, 268422143, 268435455, 268435455, 268422143, 268435455, 268435455),
    (268435455, 268435455, 268435455, 268435455, 268435348, 268435455, 268435381, 268435455, 268435455, 268435455, 268435455, 266684927, 268435455, 268435455, 268435455, 268435455),
    (268435455, 268435455, 268435455, 268435351, 268435455, 266420223, 268435455, 268435455, 268435455, 268435455, 268435455, 268435455, 268435455, 268435455, 268435455, 268435455),
    (268435455, 268435349, 268435455, 268435455, 268435455, 268435455, 268421631, 268435455, 268435455, 268426239, 268435455, 268435455, 268435455, 268435455, 268421631, 268435455),
    (268435455, 268435455, 268435455, 268435455, 268435455, 268435383, 267075583, 268435455, 268435455, 268435455, 268435455, 268435455, 268435455, 268435455, 268435455, 268435455),
    (268435455, 268435455, 268435455, 268435455, 268435455, 268435455, 268435455, 268435455, 268435455, 109051903, 268435455, 268435455, 268435455, 106954751, 268435455, 268435455),
    (268435455, 268435455, 268435455, 268435455, 268435455, 268435455, 268425727, 268435455, 268435455, 268435455, 268435455, 268435455, 268435455, 268435455, 268435455, 268435455),
    (268435455, 268435455, 268435455, 268435455, 268435455, 268435455, 268435455, 268435455, 268435455, 268435455, 268435455, 268435455, 268435455, 268435455, 268435455, 268435455),
    (268435455, 268435455, 268435455, 268435455, 268435455, 268435455, 268435455, 268435455, 268435455, 268435455, 268435455, 268435455, 268435455, 268435455, 268435455, 268435455),
    (268435455, 268435455, 268435455, 268435455, 268435455, 268435455, 268435455, 268435455, 268435455, 268435455, 268435455, 268435455, 268435455, 268435455, 268435455, 268435455),
    (268435455, 268435455, 268435455, 268435455, 268435455, 268435455, 268435455, 268435455, 268435455, 268435455, 268435455, 268435455, 268435455, 41943039, 268435455, 268435455),
    (268435455, 268435455, 268435455, 268435455, 268435455, 268435455, 266682367, 268435455, 268435455, 268435455, 268435455, 268435455, 268435455, 268435455, 268435455, 268435455),
    (268435455, 268435455, 268435455, 268435455, 268435455, 268435455, 268435455, 268435455, 268435455, 268435455, 268435455, 268435455, 268435455, 268435455, 268435455, 268435455),
    (268435455, 268435455, 268435455, 268435455, 268435455, 268435455, 268435455, 268435455, 268435455, 268435455, 268435455, 268435455, 268435455, 268435455, 268435455, 268435455),
    (268435455, 268435455, 268435455, 268435455, 268435455, 268435455, 268435455, 268435455, 268435455, 268435455, 268435455, 268435455, 268435455, 268435455, 268435455, 268435455),
    (268435455, 268435455, 268435455, 268435455, 268435455, 268435455, 268435455, 268435455, 268435455, 268435455, 268435455, 268435455, 268435455, 268435455, 268435455, 268435455),
    (268435455, 268435455, 268435455, 268435455, 268435455, 268435455, 268435455, 268435455, 268435455, 268435455, 268435455, 268435455, 268435455, 268435455, 268435455, 268435455),
    (268435455, 268435455, 268435455, 268435455, 268435455, 268435455, 268435455, 268435455, 268435455, 268435455, 268435455, 268435455, 268435455, 268435455, 268435455, 268435455),
)
COUNT = len(ARRIVALS)
LAG = 6
PARTS = 3
EARLY = 2
VMEM_LIMIT = 60 * 1024 * 1024


def pick(values, p):
    values = list(values)
    bit = 1
    while len(values) > 1:
        if len(values) % 2:
            values.append(values[-1])
        odd = (p // bit) % 2 == 1
        values = [jnp.where(odd, b, a) for a, b in zip(values[::2], values[1::2])]
        bit *= 2
    return values[0]


def kernel(
    q_ref, k_ref, v_ref, mask_ref, w_ref, out_ref,
    kv, qs, masks, bias, wts, att, attended, top, total, accum, proj,
    kv_recv, out_send, first_send, pass_send, q_recv, q_local, kv_local, swap_send,
    w_recv, w_send, w_local, w_pass_recv, w_pass_send, att_recv, att_send, mask_sem,
):
    i = lax.axis_index("ctx")
    z = lax.axis_index("head")
    c = i % 2
    p = i // 2
    x = p // 4
    y = p % 4
    twin = (p * 2 + 1 - c, z)
    neighbours = (((x + 1) % 4) * 4 + y, ((x + 3) % 4) * 4 + y, x * 4 + (y + 1) % 4, x * 4 + (y + 3) % 4)

    def slot_of(delta):
        slot = jnp.where(delta == -2, 3, jnp.where(delta == 2, 4, 7))
        slot = jnp.where(delta == -1, 1, jnp.where(delta == 1, 2, slot))
        slot = jnp.where((delta == -4) | (delta == 12), 5, slot)
        return jnp.where((delta == 4) | (delta == -12), 6, slot)

    def remote(src, dst, send, recv, device):
        return pltpu.make_async_remote_copy(
            src_ref=src, dst_ref=dst, send_sem=send, recv_sem=recv, device_id=device, device_id_type=MESH
        )

    barrier = pltpu.get_barrier_semaphore()
    greeted = [(there * 2 + core, z) for there in neighbours for core in (0, 1)] + [twin]
    for dz in (1, 2, 3):
        greeted += [(i, (z + dz) % 4), (p * 2 + 1 - c, (z + dz) % 4)]
    for device in greeted:
        pl.semaphore_signal(barrier, inc=1, device_id=device, device_id_type=MESH)

    my_rows = pl.ds(pl.multiple_of(c * FRAME, FRAME), FRAME)
    twin_rows = pl.ds(pl.multiple_of((1 - c) * FRAME, FRAME), FRAME)

    def columns(core, h):
        return pl.ds(pl.multiple_of((HEADS_CORE * core + h) * HEAD_DIM, HEAD_DIM), HEAD_DIM)

    def swap_kv(h, which):
        ref = (k_ref, v_ref)[which]
        return remote(ref.at[:, columns(1 - c, h)], kv.at[0, which, h, my_rows, :], swap_send.at[which, h], kv_recv.at[0, which, h], twin)

    def swap_q(h):
        return remote(q_ref.at[:, columns(1 - c, h)], qs.at[h, my_rows, :], swap_send.at[2, h], q_recv.at[h], twin)

    def keep_kv(h, which):
        ref = (k_ref, v_ref)[which]
        return pltpu.make_async_copy(ref.at[:, columns(c, h)], kv.at[0, which, h, my_rows, :], kv_local.at[which, h])

    def keep_q(h):
        return pltpu.make_async_copy(q_ref.at[:, columns(c, h)], qs.at[h, my_rows, :], q_local.at[h])

    swap_mask = remote(mask_ref, masks.at[c], mask_sem.at[0], mask_sem.at[1], twin)
    keep_mask = pltpu.make_async_copy(mask_ref, masks.at[c], mask_sem.at[2])

    def w_block(h, core, zz):
        rows = pl.ds(pl.multiple_of((HEADS_CORE * core + h) * HEAD_DIM, HEAD_DIM), HEAD_DIM)
        return w_ref.at[rows, pl.ds(pl.multiple_of(zz * 768, 768), 768)]

    def w_copy(h, dz):
        zz = (z + dz) % 4
        return remote(w_block(h, c, zz), wts.at[h, z * 2 + c], w_send.at[h, dz - 1], w_recv.at[h, dz - 1], (i, zz))

    def w_keep(h, core):
        return pltpu.make_async_copy(w_block(h, core, z), wts.at[h, z * 2 + core], w_local.at[h, core])

    def w_pass(h, dz):
        place = ((z + 4 - dz) % 4) * 2 + c
        return remote(wts.at[h, place], wts.at[h, place], w_pass_send.at[h, dz - 1], w_pass_recv.at[h, dz - 1], twin)

    def own_copy(h, which, group, direction, sem):
        there = neighbours[direction]
        ref = (k_ref, v_ref)[which]
        core = c if group == 0 else 1 - c
        return remote(
            ref.at[:, columns(core, h)], kv.at[slot_of(p - there), which, h, my_rows, :],
            sem, kv_recv.at[slot_of(p - there), which, h], (there * 2 + core, z),
        )

    def own_first(h, which, group, direction):
        ref = (k_ref, v_ref)[which]
        there = neighbours[direction]
        return remote(
            ref.at[:, columns(group, h)], kv.at[8, which, h, 0:FRAME, :],
            first_send.at[group, which, h, direction], kv_recv.at[8, which, h], (there * 2 + group, z),
        )

    def first_sent(word, action):
        slot = word & 15
        h = (word >> 4) & 3
        which = (word >> 6) & 1
        some = ((word >> 11) & 15) > 0

        @pl.when(some & (slot == 0) & (c == 0))
        def _():
            for direction in range(4):
                for kind in (0, 1):
                    @pl.when((((word >> (11 + direction)) & 1) == 1) & (which == kind))
                    def _():
                        for group in (0, 1):
                            action(own_first(h, kind, group, direction))

        @pl.when(some & (slot > 0))
        def _():
            for direction in range(4):
                @pl.when(((word >> (11 + direction)) & 1) == 1)
                def _():
                    action(remote(
                        kv.at[slot, which, h, 0:FRAME, :], kv.at[8, which, h, 0:FRAME, :],
                        pass_send.at[which, h, direction], kv_recv.at[8, which, h], (neighbours[direction] * 2 + c, z),
                    ))

    def out_done(direction, turn):
        whole = kv.at[0, 0, 0]
        remote(whole, whole, out_send.at[direction, turn], kv_recv.at[0, 0, 0], twin).wait_send()

    def send(packed, sent):
        after = []
        for direction in range(4):
            code = (packed >> (7 * direction)) & 127
            slot = code & 7
            h = (code >> 3) & 3
            which = (code >> 5) & 1
            turn = sent[direction] % 2

            @pl.when(code < 127)
            def _():
                pl.when(sent[direction] > 1)(lambda: out_done(direction, turn))
                sem = out_send.at[direction, turn]
                for kind in (0, 1):
                    @pl.when((slot == 0) & (which == kind))
                    def _():
                        for group in (0, 1):
                            own_copy(h, kind, group, direction, sem).start()

                @pl.when(slot > 0)
                def _():
                    there = neighbours[direction]
                    far = jnp.where(p < 8, 8, -8)
                    near = jnp.where(slot == 1, -1, jnp.where(slot == 2, 1, jnp.where(slot == 3, -2, 2)))
                    off = jnp.where(slot < 5, near, jnp.where(slot == 5, -4, jnp.where(slot == 6, 4, far)))
                    target = slot_of(p + off - there)
                    remote(
                        kv.at[slot, which, h], kv.at[target, which, h], sem, kv_recv.at[target, which, h], (there * 2 + c, z)
                    ).start()

            after.append(sent[direction] + jnp.where(code < 127, 1, 0))
        return tuple(after)

    def start(copy):
        copy.start()

    def finish(copy):
        copy.wait_send()

    for h in range(HEADS_CORE):
        keep_q(h).start()
        keep_kv(h, 0).start()
        keep_kv(h, 1).start()
    keep_mask.start()
    pl.semaphore_wait(barrier, len(greeted))
    sent = (jnp.int32(0),) * 4
    for n in range(EARLY):
        sent = send(pick(SENDS[n], p), sent)
        first_sent(pick(ARRIVALS[n], p), start)
    swap_mask.start()
    for h in range(HEADS_CORE):
        swap_q(h).start()
        swap_kv(h, 0).start()
        swap_kv(h, 1).start()
    for h in range(HEADS_CORE):
        for dz in (1, 3, 2):
            w_copy(h, dz).start()
    for h in range(HEADS_CORE):
        for core in (0, 1):
            w_keep(h, core).start()

    top[...] = jnp.full_like(top, NEG)
    total[...] = jnp.zeros_like(total)
    accum[...] = jnp.zeros_like(accum)
    proj[...] = jnp.zeros_like(proj)

    keep_mask.wait()
    swap_mask.wait_recv()
    blocks = masks.shape[2]
    same = lax.broadcasted_iota(jnp.int32, (blocks, blocks), 0) == lax.broadcasted_iota(jnp.int32, (blocks, blocks), 1)
    anchor_rows = lax.broadcasted_iota(jnp.int32, (blocks, BLOCK), 0) < FRAME // BLOCK
    for core in (0, 1):
        for b in (0, 1):
            line = jnp.where(same, jnp.broadcast_to(masks[core, b : b + 1, :], (blocks, blocks)), 0)
            column = jnp.sum(line.astype(jnp.float32), axis=1, keepdims=True)
            wide = jnp.broadcast_to(column, (blocks, BLOCK))
            added = jnp.where((wide > 0) & ~anchor_rows, 0.0, NEG).astype(jnp.float32)
            for n in range(blocks // 2):
                bias[core, n, :, b * BLOCK : (b + 1) * BLOCK] = added[2 * n : 2 * n + 2, :]
        bias[core, 32] = jnp.zeros_like(bias[core, 32])

    def attend(slot, h, source, parts):
        scores = []
        for frame, halves in parts:
            rows = slice(frame * FRAME, (frame + 1) * FRAME)
            held = slice(halves[0] * FRAME, (halves[-1] + 1) * FRAME)
            scores.append(lax.dot_general(
                kv[slot, 0, h, held, :], qs[h, rows, :], (((1,), (1,)), ((), ())), preferred_element_type=jnp.float32
            ))
        weights = []
        factors = []
        for (frame, halves), score in zip(parts, scores):
            rows = slice(frame * FRAME, (frame + 1) * FRAME)
            length = len(halves) * FRAME
            score = score * EXP2_SCALE
            if source is not None:
                added = [bias[frame, source * 2 + half] for half in halves]
                added = added[0] if len(added) == 1 else jnp.concatenate(added, axis=0)
                score = (score.reshape(length // BLOCK, BLOCK, FRAME) + added[:, None, :]).reshape(length, FRAME)
            before = top[h, :, rows]
            now = jnp.maximum(before, jnp.max(score, axis=0, keepdims=True))
            weight = jnp.exp2(score - now)
            factor = jnp.exp2(before - now)
            total[h, :, rows] = total[h, :, rows] * factor + jnp.sum(weight, axis=0, keepdims=True)
            top[h, :, rows] = now
            weights.append(weight.astype(jnp.bfloat16))
            factors.append(factor)
        for (frame, halves), weight, factor in zip(parts, weights, factors):
            rows = slice(frame * FRAME, (frame + 1) * FRAME)
            held = slice(halves[0] * FRAME, (halves[-1] + 1) * FRAME)
            mixed = lax.dot_general(
                kv[slot, 1, h, held, :], weight, (((0,), (0,)), ((), ())), preferred_element_type=jnp.float32
            )
            accum[h, :, rows] = accum[h, :, rows] * factor + mixed

    def att_copy(h, dz, cross):
        core = 1 - c if cross else c
        rows = twin_rows if cross else my_rows
        return remote(
            attended.at[h, rows, :], att.at[h, z * 2 + c], att_send.at[h, dz, cross], att_recv.at[h, dz, cross],
            (p * 2 + core, (z + dz) % 4),
        )

    def project(h):
        for core in (0, 1):
            w_keep(h, core).wait()
        for dz in (0, 1, 3, 2):
            for cross in (0, 1):
                if dz or cross:
                    att_copy(h, dz, cross).wait_recv()
            if dz:
                w_pass(h, dz).wait_recv()
            place = ((z + 4 - dz) % 4) * 2
            left = jnp.concatenate([att[h, place], att[h, place + 1]], axis=1)
            for n in range(3):
                cols = slice(n * 256, (n + 1) * 256)
                right = jnp.concatenate([wts[h, place, :, cols], wts[h, place + 1, :, cols]], axis=0)
                part = proj[:, cols] + jnp.dot(left, right, preferred_element_type=jnp.float32)
                if h == HEADS_CORE - 1 and dz == 2:
                    out_ref[:, cols] = part.astype(out_ref.dtype)
                else:
                    proj[:, cols] = part

    def step(arrivals, sends, n, carry):
        sent, recent = carry
        word = pick(arrivals, n)
        slot = word & 15
        h = (word >> 4) & 3
        which = (word >> 6) & 1
        source = (word >> 18) & 15

        @pl.when((slot > 0) & (slot < 8))
        def _():
            whole = kv.at[slot, which, h]
            remote(whole, whole, pass_send.at[0, 0, 0], kv_recv.at[slot, which, h], twin).wait_recv()

        @pl.when(slot == 8)
        def _():
            first = kv.at[8, which, h, 0:FRAME, :]
            remote(first, first, pass_send.at[0, 0, 0], kv_recv.at[8, which, h], twin).wait_recv()

        first_sent(word, start)
        sent = send(pick(sends, n), sent)

        @pl.when(slot == 9)
        def _():
            keep_q(h).wait()
            swap_q(h).wait_recv()
            for kind in (0, 1):
                keep_kv(h, kind).wait()
                swap_kv(h, kind).wait_recv()
            attend(0, h, p, ((0, (0, 1)), (1, (0, 1))))

        @pl.when(((word >> 15) & 1) == 1)
        def _():
            @pl.when(slot == 1)
            def _():
                attend(1, h, source, ((0, (0, 1)), (1, (1,))))

            @pl.when(slot == 2)
            def _():
                attend(2, h, source, ((0, (0,)), (1, (0, 1))))

            @pl.when((slot > 2) & (slot < 8))
            def _():
                attend(slot, h, source, ((0, (0,)), (1, (1,))))

        @pl.when(((word >> 17) & 1) == 1)
        def _():
            attend(jnp.where(slot == 9, 0, slot), h, None, ((0, (0,)), (1, (0,))))

        @pl.when(((word >> 16) & 1) == 1)
        def _():
            attended[h] = jnp.transpose(accum[h] * (1.0 / total[h])).astype(jnp.bfloat16)
            for dz in (2, 1, 3, 0):
                for cross in (0, 1):
                    if dz or cross:
                        att_copy(h, dz, cross).start()
            att[h, z * 2 + c] = attended[h, my_rows, :]

        @pl.when(slot == 10)
        def _():
            for dz in (1, 3, 2):
                w_copy(h, dz).wait_recv()
                w_pass(h, dz).start()

        first_sent(recent[0], finish)
        return sent, recent[1:] + (word,)

    carry = sent, (jnp.int32(15),) * (LAG - EARLY) + tuple(pick(line, p) for line in ARRIVALS[:EARLY])
    length = -(-(COUNT - EARLY) // PARTS)
    for begin in range(EARLY, COUNT, length):
        end = min(begin + length, COUNT)
        arrivals = [pick(line, p) for line in ARRIVALS[begin:end]]
        sends = [pick(line, p) for line in SENDS[begin:end]]
        carry = lax.fori_loop(0, end - begin, functools.partial(step, arrivals, sends), carry)
    recent = carry[1]

    def finish_heads(heads):
        for h in heads:
            for dz in range(4):
                for cross in (0, 1):
                    if dz or cross:
                        att_copy(h, dz, cross).wait_send()

    project(0)
    project(1)
    for word in recent:
        first_sent(word, finish)
    for direction in range(4):
        for turn in (0, 1):
            out_done(direction, turn)
    for h in range(HEADS_CORE):
        for which in (0, 1):
            swap_kv(h, which).wait_send()
        swap_q(h).wait_send()
        for dz in (1, 2, 3):
            w_copy(h, dz).wait_send()
            w_pass(h, dz).wait_send()
    swap_mask.wait_send()
    finish_heads((0, 1))
    project(2)
    finish_heads((2,))


def body(queries, keys, values, block_mask, w_out):
    bf16, f32, dma = jnp.bfloat16, jnp.float32, pltpu.SemaphoreType.DMA
    heads = HEADS_CORE
    anywhere = pl.BlockSpec(memory_space=pl.ANY)
    return pl.pallas_call(
        kernel,
        out_shape=jax.ShapeDtypeStruct((FRAME, 768), bf16),
        in_specs=[anywhere, anywhere, anywhere, pl.BlockSpec(memory_space=pltpu.VMEM), anywhere],
        out_specs=pl.BlockSpec(memory_space=pltpu.VMEM),
        scratch_shapes=[
            pltpu.VMEM((9, 2, heads, 2 * FRAME, HEAD_DIM), bf16),
            pltpu.VMEM((heads, 2 * FRAME, HEAD_DIM), bf16),
            pltpu.VMEM((2, 2, 64), jnp.int32),
            pltpu.VMEM((2, 33, 2, FRAME), f32),
            pltpu.VMEM((heads, 8, HEAD_DIM, 768), bf16),
            pltpu.VMEM((heads, 8, FRAME, HEAD_DIM), bf16),
            pltpu.VMEM((heads, 2 * FRAME, HEAD_DIM), bf16),
            pltpu.VMEM((heads, 1, 2 * FRAME), f32),
            pltpu.VMEM((heads, 1, 2 * FRAME), f32),
            pltpu.VMEM((heads, HEAD_DIM, 2 * FRAME), f32),
            pltpu.VMEM((FRAME, 768), f32),
            dma((9, 2, heads)), dma((4, 2)), dma((2, 2, heads, 4)), dma((2, heads, 4)), dma((heads,)), dma((heads,)), dma((2, heads)), dma((3, heads)),
            dma((heads, 3)), dma((heads, 3)), dma((heads, 2)), dma((heads, 3)), dma((heads, 3)),
            dma((heads, 4, 2)), dma((heads, 4, 2)), dma((3,)),
        ],
        compiler_params=pltpu.CompilerParams(
            collective_id=0, has_side_effects=True, vmem_limit_bytes=VMEM_LIMIT
        ),
        name="radial_attention",
    )(queries, keys, values, block_mask, w_out)


def solution(mesh):
    placed = (P("ctx", "head"), P("ctx", "head"), P("ctx", "head"), P("ctx", None), P("head", None))
    return jax.shard_map(
        body, mesh=mesh, in_specs=placed, out_specs=P("ctx", "head"), check_vma=False
    )
```

```python
import functools

import jax
import jax.numpy as jnp
from jax import lax
from jax.experimental import pallas as pl
from jax.experimental.pallas import tpu as pltpu
from jax.sharding import PartitionSpec as P

HEAD_DIM = 128
BLOCK = 128
FRAME = 256
HEADS_CORE = 3
MESH = pl.DeviceIdType.MESH
NEG = -1e30
EXP2_SCALE = HEAD_DIM ** (-0.5) * 1.4426950408889634

ARRIVALS = (
    (15, 15, 15, 15, 15, 15, 15, 15, 15, 15, 15, 15, 15, 15, 15, 15),
    (0, 15, 15, 15, 15, 15, 15, 15, 15, 15, 15, 15, 15, 15, 15, 15),
    (16448, 262153, 524297, 786441, 1048585, 1310729, 1572873, 1835017, 2097161, 2359305, 2621449, 2883593, 3145737, 3407881, 3670025, 3932169),
    (131081, 262169, 524313, 6216, 1048601, 1310745, 1572889, 1835033, 2097177, 2359321, 2621465, 2883609, 3145753, 3407897, 3670041, 3932185),
    (131097, 524354, 15, 786457, 15, 15, 15, 15, 15, 15, 15, 15, 15, 15, 15, 786518),
    (3145797, 262185, 524329, 786473, 1048617, 1310761, 1572905, 1835049, 2097193, 2359337, 2621481, 2883625, 3145769, 3407913, 3670057, 3932201),
    (131113, 3407877, 3670037, 3932229, 69, 262149, 524293, 786437, 1048581, 1310725, 1572933, 1835013, 22, 2359301, 2621509, 2883653),
    (1048582, 1310790, 1572934, 1835014, 2097222, 2359302, 2621446, 2883590, 3145798, 3407878, 3670086, 3932166, 2097157, 262214, 524310, 3670017),
    (262210, 1, 262209, 524289, 1310786, 1048657, 1310721, 1572929, 2359298, 2097153, 2359361, 2621441, 3407938, 3670082, 3407873, 2916357),
    (4112, 3407941, 786498, 3932165, 188421, 1572930, 1835074, 2883670, 1048661, 2621506, 2883586, 1867845, 2097173, 3145729, 3932162, 3702849),
    (20560, 1310742, 3670101, 1867846, 2097174, 262165, 557125, 1605633, 3178502, 1310805, 1572885, 2621457, 86, 2359381, 2654213, 72),
    (1081414, 163905, 1605638, 557121, 1343490, 2392134, 2621462, 819269, 2359378, 3440710, 3702790, 3932182, 3407890, 3145809, 524374, 15),
    (294914, 15, 819202, 15, 15, 1081361, 1343553, 16456, 15, 2129985, 2359377, 15, 38, 262230, 3407953, 15),
    (15, 15, 262161, 15, 16405, 1572882, 1835026, 2916374, 1081365, 2621474, 2916418, 15, 15, 3670034, 3964994, 2883605),
    (15, 15, 15, 1835094, 15, 15, 15, 15, 15, 15, 15, 15, 15, 15, 15, 3670033),
    (15, 15, 15, 3932245, 2129926, 15, 15, 15, 3145766, 1310821, 15, 15, 3407970, 15, 3407905, 15),
    (1048662, 15, 15, 524305, 1310738, 15, 2654294, 1572945, 15, 2621522, 15, 1835093, 2130005, 15, 15, 1835079),
    (524292, 15, 15, 1835110, 2097254, 262181, 15, 786533, 2359330, 15, 1605717, 2654289, 2097189, 2359397, 524326, 2883685),
    (557124, 3407957, 1572966, 3932261, 1343570, 2359318, 15, 3932183, 3145814, 15, 3670118, 786519, 10, 262246, 15, 3670049),
    (1081366, 1310822, 786450, 557137, 3145799, 1572898, 524309, 1605649, 15, 3407894, 2392081, 1867797, 24, 15, 2621477, 10),
    (262226, 15, 294993, 10, 10, 2392150, 1310801, 137224, 2392162, 2097233, 2883602, 2621537, 3670020, 15, 3932178, 3407939),
    (10, 1343526, 1605670, 4184, 786433, 294997, 1867858, 10, 10, 3440726, 3702822, 3932198, 3702852, 3178513, 2654309, 3407891),
    (2097159, 3407973, 10, 1048578, 1572868, 1605730, 557141, 3932231, 1835009, 2097249, 1572901, 10, 139352, 3702866, 3965010, 15),
    (32, 10, 2621511, 15, 15, 10, 1310753, 2097218, 26695, 10, 2359329, 3145794, 2883585, 3178561, 10, 15),
    (2097175, 4113, 262241, 524385, 15, 1048641, 10, 24, 2621444, 262151, 2916434, 2359299, 1048583, 3670050, 1572935, 15),
    (4192, 786500, 819282, 2883655, 180309, 2056, 1835106, 1310723, 165895, 2883588, 10, 3965014, 3670036, 10, 3145731, 15),
    (15, 163921, 2654215, 2883607, 3178503, 1081345, 3670087, 2097170, 15, 2916420, 524295, 15, 1081415, 1310727, 3145811, 1867783),
    (15, 819204, 15, 1081410, 1605700, 15, 2120, 3964935, 3178518, 262167, 2883682, 786439, 3702868, 1343559, 1605639, 3407971),
    (2130007, 2359367, 786466, 557089, 2130006, 3407879, 15, 786517, 2654276, 2129937, 524375, 2392131, 8264, 1310807, 1572887, 3440643),
    (2195527, 2392071, 2621463, 2916359, 1572884, 1835076, 15, 1343555, 3178598, 294999, 2097155, 2359379, 2883601, 1343511, 3932258, 2916389),
    (294930, 2359383, 67, 2916439, 8293, 2359334, 3702791, 819221, 2621476, 262183, 557079, 819271, 2883681, 3145825, 1572967, 3440723),
    (262242, 2392087, 2654295, 135176, 819265, 2392166, 1867810, 2359300, 2621460, 294983, 2392161, 15, 1048663, 3932228, 3178515, 1835095),
    (1048614, 786452, 165891, 262147, 1605716, 3440711, 3670039, 15, 2654292, 2056, 2916386, 16392, 3670052, 3964932, 1605719, 1867799),
    (524308, 33, 2621479, 26, 26, 1048609, 1048659, 1310803, 1572867, 2129953, 557127, 3407940, 24680, 3178529, 3964962, 4184),
    (15, 163937, 819298, 1048594, 3145767, 1835028, 3702871, 26, 26, 2883604, 2120, 3145762, 26, 4120, 1605671, 1835111),
    (622676, 15, 2654311, 3932197, 524291, 1081441, 1081363, 1343507, 15, 135240, 26, 2392083, 131080, 1310823, 15, 26),
    (294946, 819284, 1048580, 294979, 1310818, 15, 3670119, 147544, 15, 26, 3145732, 131144, 2621443, 139352, 15, 3440675),
    (26, 26, 26, 1310724, 622659, 3407895, 3702823, 1310755, 8279, 1835075, 2097235, 2359331, 3440642, 2883587, 26, 3702881),
    (1081446, 15, 14355, 2883687, 786529, 26, 26, 3965015, 180247, 2916436, 1605637, 26, 1081367, 15, 15, 3702865),
    (2097255, 15, 1572886, 262163, 1572964, 1867860, 2097220, 2097250, 1835025, 3407910, 3178564, 3407892, 2129989, 26, 3440657, 15),
    (524388, 1343494, 1048660, 1409092, 2129958, 3440727, 15, 2916422, 2392130, 1867779, 2097251, 15, 2654275, 3702786, 3440705, 4200),
    (15, 622594, 163923, 131096, 786513, 1605634, 1048643, 2392132, 1605699, 1343557, 2392065, 2392163, 3440722, 2916419, 2621461, 196616),
    (15, 3407909, 1605718, 294995, 524307, 786499, 15, 15, 1867841, 2883684, 3670038, 3964998, 2981953, 3932180, 72, 2916437),
    (557092, 786468, 1146900, 262243, 1343522, 294981, 2129924, 2359380, 1572883, 2719746, 133128, 1835045, 3440674, 8, 3145827, 1867815),
    (15, 2359335, 294913, 1867798, 3145751, 1835108, 2654278, 2195458, 1146949, 12312, 3702870, 2654273, 2621523, 3965012, 2654293, 42),
    (15, 2392167, 14371, 1310804, 819217, 131144, 2097172, 3932263, 26663, 2916388, 2129955, 3440644, 42, 1343527, 88, 196632),
    (15, 819300, 1146948, 2916391, 3178583, 1867812, 1343505, 1343587, 42, 1835091, 3145812, 88, 1048615, 131144, 204824, 15),
    (42, 1343574, 178275, 1081426, 1605668, 104, 131080, 819237, 2392082, 139352, 2195523, 3145746, 1081447, 2457669, 3440737, 196648),
    (15, 524306, 42, 42, 622675, 819203, 524389, 42, 2654308, 1343509, 524327, 3244034, 2654227, 4200, 3178531, 15),
    (2195495, 622674, 294945, 1409044, 42, 786451, 15, 2392084, 1605715, 42, 42, 819223, 2981969, 2392085, 3178563, 15),
    (15, 42, 1048612, 294947, 3178599, 1933316, 16472, 1572961, 1572963, 2654226, 24, 131096, 2130021, 2883603, 42, 15),
    (15, 15, 1146980, 40, 524387, 1605714, 1048611, 2359396, 1933393, 295015, 131160, 3440724, 2621475, 2981971, 196616, 15),
    (15, 524386, 15, 1310756, 557091, 3407975, 2130004, 2195538, 1835041, 1933331, 2129939, 786535, 131112, 3932196, 24616, 15),
    (15, 622626, 15, 1048674, 180261, 42, 196632, 2392100, 163943, 1835107, 3244052, 42, 3702884, 3702882, 196712, 15),
    (15, 15, 15, 131176, 884769, 88, 1081443, 2883686, 1605667, 104, 3145828, 20584, 2654307, 42, 15, 15),
    (15, 15, 15, 1867814, 15, 131096, 42, 1605665, 1048613, 1867811, 557159, 3244114, 2981921, 2392101, 15, 15),
    (15, 15, 15, 1343588, 15, 884819, 2097252, 3964967, 1867873, 131112, 1605733, 2654241, 15, 2883683, 15, 15),
    (15, 15, 15, 1146914, 15, 786467, 1081347, 104, 1146981, 1343525, 104, 1867877, 15, 3965028, 15, 15),
    (15, 15, 15, 15, 15, 819299, 2621478, 2129954, 15, 3440742, 3178532, 3178594, 15, 2916387, 15, 15),
    (15, 15, 15, 15, 15, 295013, 2129956, 2916390, 15, 2719842, 196648, 131112, 15, 196648, 15, 15),
    (15, 15, 15, 15, 15, 3440679, 1933314, 196648, 15, 15, 15, 3407972, 15, 15, 15, 15),
    (15, 15, 15, 15, 15, 196648, 18472, 15, 15, 15, 15, 3965030, 15, 15, 15, 15),
    (15, 15, 15, 15, 15, 15, 557093, 15, 15, 15, 15, 819239, 15, 15, 15, 15),
    (15, 15, 15, 15, 15, 15, 1343585, 15, 15, 15, 15, 3506212, 15, 15, 15, 15),
    (15, 15, 15, 15, 15, 15, 131176, 15, 15, 15, 15, 15, 15, 15, 15, 15),
    (15, 15, 15, 15, 15, 15, 2719846, 15, 15, 15, 15, 15, 15, 15, 15, 15),
)
SENDS = (
    (266339360, 67637248, 67109888, 69194752, 266993664, 67112960, 67637280, 69189632, 266342400, 524288, 67108896, 2080800, 266342432, 67108864, 67112968, 2080800),
    (266867712, 136200, 266867744, 2097056, 266473512, 525352, 16777224, 18862112, 266863624, 84545576, 33686528, 69194752, 266993791, 17436704, 17301544, 69190656),
    (268435455, 268435455, 268435455, 268435455, 268435455, 268435455, 268435455, 268435455, 268435455, 268435455, 268435455, 268435455, 268435455, 268435455, 268435455, 268435455),
    (268435455, 268435455, 268435455, 268435455, 268435455, 268435455, 268435455, 268435455, 268435455, 268435455, 268435455, 268435455, 268435455, 268435455, 268435455, 268435455),
    (268421128, 71964688, 266471432, 268435455, 266867720, 17438768, 34215976, 85972008, 266993704, 33686576, 84546576, 18859016, 266471551, 100926504, 84023423, 18863912),
    (266485669, 84688808, 267009960, 18874288, 266339455, 84150399, 100796432, 102750216, 267130896, 100930687, 267141040, 85983152, 266867839, 268424240, 33818751, 85968944),
    (267010047, 268435455, 268435455, 85983141, 268435365, 268435333, 268435455, 266436607, 268435455, 268435333, 268435455, 266436607, 268435455, 268435455, 268435365, 268435455),
    (14680063, 268424063, 268424063, 268435455, 81788927, 268435455, 268435455, 268435455, 81788927, 268435455, 268424063, 268435455, 268435333, 268435455, 268435455, 266371071),
    (268435455, 268435455, 268435455, 266371071, 268435455, 268435455, 268435455, 268435455, 6291455, 268435455, 268435455, 266371071, 73400319, 73400319, 268435455, 266436607),
    (268435455, 268435455, 73400319, 268435455, 268435455, 268435455, 268435455, 268435455, 268435455, 268435455, 6291455, 268435455, 268435341, 266371071, 268435455, 268435455),
    (268435368, 268435455, 268435455, 268424063, 31457157, 268435455, 268435455, 266371071, 268435455, 268435455, 268435455, 268435455, 268435455, 268435455, 268435333, 268435455),
    (81777535, 268435455, 268435455, 268435455, 268435455, 268435455, 268435455, 268435455, 268435455, 268435455, 268435455, 268420991, 23068671, 268435455, 268435455, 102749221),
    (268435455, 268420991, 6291455, 35651583, 268424063, 268435341, 268435455, 268435455, 266470149, 268435373, 268435455, 268435333, 268435455, 268435455, 268435455, 35651461),
    (268435376, 268435333, 268419967, 268435333, 268421247, 268435455, 268435455, 268420869, 268435455, 268435455, 73384831, 102760447, 267125887, 268435455, 268435455, 268435455),
    (266616831, 266895359, 268435341, 102749960, 266616831, 71979903, 266356485, 35641125, 266605695, 71321727, 268435341, 268435344, 266606719, 267026431, 71325567, 268435455),
    (267141119, 18874367, 267141119, 268435455, 268435455, 266502143, 73400319, 266960895, 268435455, 268435455, 266895359, 35651583, 268435455, 23068671, 268435455, 266567679),
    (268425087, 102760357, 268435373, 266502143, 267141119, 23068671, 268435455, 268435455, 48234495, 268435455, 267026431, 266502143, 106954669, 268424965, 268420991, 268435455),
    (268435455, 266371071, 266616831, 268426111, 268435455, 268435455, 266884901, 267026431, 268435455, 267131007, 268435373, 267026431, 268435455, 268435455, 267026431, 267223039),
    (268435455, 268435455, 268426111, 268435455, 268435455, 268420885, 23068671, 268435455, 268435455, 39845887, 268426111, 268425215, 268435455, 268435455, 6291455, 268435455),
    (268435455, 268435455, 23068671, 267026431, 23068671, 268435455, 268435455, 268435455, 39845887, 268435455, 268435455, 268435455, 268435455, 268435373, 268435349, 268435455),
    (6291455, 268426111, 268435455, 268435455, 268435455, 268435455, 268435455, 268435455, 268435455, 268435455, 23068671, 268435455, 268435455, 268424063, 268435455, 268423679),
    (268435455, 268435455, 268435455, 268435455, 268435455, 268435455, 268435455, 268435455, 268435455, 268435455, 268422015, 268435455, 268435455, 268435455, 268435381, 268420607),
    (268435455, 268435455, 268435455, 6291455, 268435332, 268435455, 268435455, 268435367, 268435455, 268435455, 268435349, 268435455, 268435455, 88244223, 268435455, 268435344),
    (268435332, 268435455, 268435455, 268435373, 268425343, 268435455, 268435455, 73400319, 268435455, 268435455, 268435455, 268435455, 266409855, 268435455, 268435455, 25165823),
    (268435455, 268435455, 268435455, 268435455, 115343359, 268435455, 268435455, 267223039, 266357508, 268435455, 90177535, 268419583, 268420991, 39845887, 268435455, 268435381),
    (268435455, 268435455, 90177535, 268435367, 266410879, 266895359, 268435455, 268419472, 268435455, 268435332, 266502143, 73400205, 268435455, 268435455, 268435455, 75497471),
    (31442815, 268435455, 266895271, 267157503, 266371071, 102760447, 268435455, 23068671, 268421247, 267011876, 268435455, 8388607, 268435455, 268421127, 21250559, 268435455),
    (268435364, 33704749, 266502064, 268435455, 268435364, 105005055, 268435455, 268435455, 268435455, 267157503, 268435455, 266567679, 94371839, 268424080, 88867839, 268435455),
    (268435455, 267026340, 39845887, 268435455, 268435455, 268435455, 267026431, 267091967, 266420132, 268435455, 268435455, 266916351, 268435455, 268435455, 268435343, 266403839),
    (266420223, 268435455, 268421119, 266633215, 268435340, 268435364, 90177535, 268423679, 77594623, 268435455, 106954751, 268435455, 266502143, 268435455, 268435455, 268419583),
    (268424191, 268424191, 268435455, 268425215, 268435455, 268422015, 268435455, 268435455, 31457279, 268435455, 268419583, 268435455, 268435455, 267157503, 268435455, 267059199),
    (90177535, 268435455, 268425215, 268435455, 268435455, 268426111, 268435455, 268435455, 268420991, 268424191, 267157503, 268424703, 268435455, 268435455, 268435455, 268424703),
    (268435455, 268435455, 268435455, 8388533, 267075583, 268435455, 105152399, 266567679, 268435455, 268435455, 268435455, 268435455, 268424191, 268435455, 268435375, 268435455),
    (266551180, 268435455, 268435455, 268435344, 268435455, 268435455, 268424703, 268424703, 268435455, 268435455, 39845887, 268435455, 268435455, 266633215, 268435455, 109051791),
    (106954751, 268435455, 106954751, 268435455, 268435455, 268435455, 268435375, 268435341, 268435455, 266633215, 268435455, 268435455, 268422015, 268435455, 268435455, 268435349),
    (267075583, 266633100, 268435455, 268435455, 268435372, 268435455, 268420607, 268435455, 266551212, 268435455, 268435455, 268435455, 268435455, 268435455, 39835135, 268435455),
    (268435372, 268435455, 268435332, 268435455, 106954751, 266633215, 39845887, 268435381, 268425087, 268435455, 266420223, 268435455, 268435455, 268435455, 268422015, 266665983),
    (268422015, 268421119, 268435455, 268435455, 268435455, 35651583, 268435455, 268420607, 268435455, 75497471, 268424703, 268435455, 268435455, 268435375, 268435455, 268435455),
    (268426111, 268435381, 268435455, 268435455, 268435455, 268435455, 268435455, 268435455, 268435455, 268435372, 268435455, 268435455, 268435455, 268421119, 102760447, 268435455),
    (268435455, 267157503, 268435351, 268435455, 111149055, 268435372, 268435455, 106954751, 42106764, 268435455, 268435364, 266534911, 268435455, 268435455, 268435455, 268426239),
    (268435380, 268435455, 267075583, 268435455, 268421940, 38567935, 268435364, 268435455, 115343359, 268419583, 268435455, 267142655, 268435455, 268435455, 268435455, 268435455),
    (39845887, 268435455, 268435455, 268435455, 267026431, 268435455, 268435455, 268435455, 268426004, 268435455, 268435455, 268435455, 268435455, 75488127, 268435455, 268435455),
    (267206655, 268435455, 268435455, 268435383, 268435455, 268435455, 268423679, 268421631, 268435455, 268435380, 268435455, 268435455, 268435455, 268435455, 268435455, 267082239),
    (268435455, 268435455, 268435455, 268435349, 268435455, 268435455, 266420223, 268435455, 268435455, 268435455, 268435455, 268425621, 268435455, 268435455, 268435455, 268435351),
    (113590271, 268422143, 268435455, 268435455, 268435455, 268435380, 268435455, 268435455, 268435455, 268435455, 268435455, 268435455, 268435455, 268435455, 268435455, 268435455),
    (268435348, 268435455, 268435383, 268435455, 268435455, 268435455, 268435340, 268435383, 268422143, 268435348, 268421631, 268435455, 268435455, 268435455, 268435455, 268435455),
    (268426239, 268435348, 268435455, 268435455, 268435381, 268435348, 268435455, 109042175, 268435455, 92274687, 267075583, 268435455, 268422143, 268435455, 106945023, 268421631),
    (268435455, 266616831, 268435455, 268435455, 44040191, 268435455, 268435455, 266698645, 268435455, 268435455, 268435455, 23068671, 268426239, 268435455, 268426239, 268435455),
    (48234495, 268435380, 268435455, 268435455, 268435455, 268435455, 268435455, 268435455, 267206580, 268435455, 268422143, 268435455, 268435455, 268422143, 268435455, 268435455),
    (268435455, 268435455, 268435455, 268435455, 268435348, 268435455, 268435381, 268435455, 268435455, 268435455, 268435455, 266684927, 268435455, 268435455, 268435455, 268435455),
    (268435455, 268435455, 268435455, 268435351, 268435455, 266420223, 268435455, 268435455, 268435455, 268435455, 268435455, 268435455, 268435455, 268435455, 268435455, 268435455),
    (268435455, 268435349, 268435455, 268435455, 268435455, 268435455, 268421631, 268435455, 268435455, 268426239, 268435455, 268435455, 268435455, 268435455, 268421631, 268435455),
    (268435455, 268435455, 268435455, 268435455, 268435455, 268435383, 267075583, 268435455, 268435455, 268435455, 268435455, 268435455, 268435455, 268435455, 268435455, 268435455),
    (268435455, 268435455, 268435455, 268435455, 268435455, 268435455, 268435455, 268435455, 268435455, 109051903, 268435455, 268435455, 268435455, 106954751, 268435455, 268435455),
    (268435455, 268435455, 268435455, 268435455, 268435455, 268435455, 268425727, 268435455, 268435455, 268435455, 268435455, 268435455, 268435455, 268435455, 268435455, 268435455),
    (268435455, 268435455, 268435455, 268435455, 268435455, 268435455, 268435455, 268435455, 268435455, 268435455, 268435455, 268435455, 268435455, 268435455, 268435455, 268435455),
    (268435455, 268435455, 268435455, 268435455, 268435455, 268435455, 268435455, 268435455, 268435455, 268435455, 268435455, 268435455, 268435455, 268435455, 268435455, 268435455),
    (268435455, 268435455, 268435455, 268435455, 268435455, 268435455, 268435455, 268435455, 268435455, 268435455, 268435455, 268435455, 268435455, 268435455, 268435455, 268435455),
    (268435455, 268435455, 268435455, 268435455, 268435455, 268435455, 268435455, 268435455, 268435455, 268435455, 268435455, 268435455, 268435455, 41943039, 268435455, 268435455),
    (268435455, 268435455, 268435455, 268435455, 268435455, 268435455, 266682367, 268435455, 268435455, 268435455, 268435455, 268435455, 268435455, 268435455, 268435455, 268435455),
    (268435455, 268435455, 268435455, 268435455, 268435455, 268435455, 268435455, 268435455, 268435455, 268435455, 268435455, 268435455, 268435455, 268435455, 268435455, 268435455),
    (268435455, 268435455, 268435455, 268435455, 268435455, 268435455, 268435455, 268435455, 268435455, 268435455, 268435455, 268435455, 268435455, 268435455, 268435455, 268435455),
    (268435455, 268435455, 268435455, 268435455, 268435455, 268435455, 268435455, 268435455, 268435455, 268435455, 268435455, 268435455, 268435455, 268435455, 268435455, 268435455),
    (268435455, 268435455, 268435455, 268435455, 268435455, 268435455, 268435455, 268435455, 268435455, 268435455, 268435455, 268435455, 268435455, 268435455, 268435455, 268435455),
    (268435455, 268435455, 268435455, 268435455, 268435455, 268435455, 268435455, 268435455, 268435455, 268435455, 268435455, 268435455, 268435455, 268435455, 268435455, 268435455),
    (268435455, 268435455, 268435455, 268435455, 268435455, 268435455, 268435455, 268435455, 268435455, 268435455, 268435455, 268435455, 268435455, 268435455, 268435455, 268435455),
)
COUNT = len(ARRIVALS)
LAG = 6
PARTS = 3
EARLY = 2
VMEM_LIMIT = 60 * 1024 * 1024


def pick(values, p):
    values = list(values)
    bit = 1
    while len(values) > 1:
        if len(values) % 2:
            values.append(values[-1])
        odd = (p // bit) % 2 == 1
        values = [jnp.where(odd, b, a) for a, b in zip(values[::2], values[1::2])]
        bit *= 2
    return values[0]


def kernel(
    q_ref, k_ref, v_ref, mask_ref, w_ref, out_ref,
    kv, qs, masks, bias, wts, att, attended, top, total, accum, proj,
    kv_recv, out_send, first_send, pass_send, q_recv, q_local, kv_local, swap_send,
    w_recv, w_send, w_local, w_pass_recv, w_pass_send, att_recv, att_send, mask_sem,
):
    i = lax.axis_index("ctx")
    z = lax.axis_index("head")
    c = i % 2
    p = i // 2
    x = p // 4
    y = p % 4
    twin = (p * 2 + 1 - c, z)
    neighbours = (((x + 1) % 4) * 4 + y, ((x + 3) % 4) * 4 + y, x * 4 + (y + 1) % 4, x * 4 + (y + 3) % 4)

    def slot_of(delta):
        slot = jnp.where(delta == -2, 3, jnp.where(delta == 2, 4, 7))
        slot = jnp.where(delta == -1, 1, jnp.where(delta == 1, 2, slot))
        slot = jnp.where((delta == -4) | (delta == 12), 5, slot)
        return jnp.where((delta == 4) | (delta == -12), 6, slot)

    def remote(src, dst, send, recv, device):
        return pltpu.make_async_remote_copy(
            src_ref=src, dst_ref=dst, send_sem=send, recv_sem=recv, device_id=device, device_id_type=MESH
        )

    barrier = pltpu.get_barrier_semaphore()
    greeted = [(there * 2 + core, z) for there in neighbours for core in (0, 1)] + [twin]
    for dz in (1, 2, 3):
        greeted += [(i, (z + dz) % 4), (p * 2 + 1 - c, (z + dz) % 4)]
    for device in greeted:
        pl.semaphore_signal(barrier, inc=1, device_id=device, device_id_type=MESH)

    my_rows = pl.ds(pl.multiple_of(c * FRAME, FRAME), FRAME)
    twin_rows = pl.ds(pl.multiple_of((1 - c) * FRAME, FRAME), FRAME)

    def columns(core, h):
        return pl.ds(pl.multiple_of((HEADS_CORE * core + h) * HEAD_DIM, HEAD_DIM), HEAD_DIM)

    def swap_kv(h, which):
        ref = (k_ref, v_ref)[which]
        return remote(ref.at[:, columns(1 - c, h)], kv.at[0, which, h, my_rows, :], swap_send.at[which, h], kv_recv.at[0, which, h], twin)

    def swap_q(h):
        return remote(q_ref.at[:, columns(1 - c, h)], qs.at[h, my_rows, :], swap_send.at[2, h], q_recv.at[h], twin)

    def keep_kv(h, which):
        ref = (k_ref, v_ref)[which]
        return pltpu.make_async_copy(ref.at[:, columns(c, h)], kv.at[0, which, h, my_rows, :], kv_local.at[which, h])

    def keep_q(h):
        return pltpu.make_async_copy(q_ref.at[:, columns(c, h)], qs.at[h, my_rows, :], q_local.at[h])

    swap_mask = remote(mask_ref, masks.at[c], mask_sem.at[0], mask_sem.at[1], twin)
    keep_mask = pltpu.make_async_copy(mask_ref, masks.at[c], mask_sem.at[2])

    def w_block(h, core, zz):
        rows = pl.ds(pl.multiple_of((HEADS_CORE * core + h) * HEAD_DIM, HEAD_DIM), HEAD_DIM)
        return w_ref.at[rows, pl.ds(pl.multiple_of(zz * 768, 768), 768)]

    def w_copy(h, dz):
        zz = (z + dz) % 4
        return remote(w_block(h, c, zz), wts.at[h, z * 2 + c], w_send.at[h, dz - 1], w_recv.at[h, dz - 1], (i, zz))

    def w_keep(h, core):
        return pltpu.make_async_copy(w_block(h, core, z), wts.at[h, z * 2 + core], w_local.at[h, core])

    def w_pass(h, dz):
        place = ((z + 4 - dz) % 4) * 2 + c
        return remote(wts.at[h, place], wts.at[h, place], w_pass_send.at[h, dz - 1], w_pass_recv.at[h, dz - 1], twin)

    def own_copy(h, which, group, direction, sem):
        there = neighbours[direction]
        ref = (k_ref, v_ref)[which]
        core = c if group == 0 else 1 - c
        return remote(
            ref.at[:, columns(core, h)], kv.at[slot_of(p - there), which, h, my_rows, :],
            sem, kv_recv.at[slot_of(p - there), which, h], (there * 2 + core, z),
        )

    def own_first(h, which, group, direction):
        ref = (k_ref, v_ref)[which]
        there = neighbours[direction]
        return remote(
            ref.at[:, columns(group, h)], kv.at[8, which, h, 0:FRAME, :],
            first_send.at[group, which, h, direction], kv_recv.at[8, which, h], (there * 2 + group, z),
        )

    def first_sent(word, action):
        slot = word & 15
        h = (word >> 4) & 3
        which = (word >> 6) & 1
        some = ((word >> 11) & 15) > 0

        @pl.when(some & (slot == 0) & (c == 0))
        def _():
            for direction in range(4):
                for kind in (0, 1):
                    @pl.when((((word >> (11 + direction)) & 1) == 1) & (which == kind))
                    def _():
                        for group in (0, 1):
                            action(own_first(h, kind, group, direction))

        @pl.when(some & (slot > 0))
        def _():
            for direction in range(4):
                @pl.when(((word >> (11 + direction)) & 1) == 1)
                def _():
                    action(remote(
                        kv.at[slot, which, h, 0:FRAME, :], kv.at[8, which, h, 0:FRAME, :],
                        pass_send.at[which, h, direction], kv_recv.at[8, which, h], (neighbours[direction] * 2 + c, z),
                    ))

    def out_done(direction, turn):
        whole = kv.at[0, 0, 0]
        remote(whole, whole, out_send.at[direction, turn], kv_recv.at[0, 0, 0], twin).wait_send()

    def send(packed, sent):
        after = []
        for direction in range(4):
            code = (packed >> (7 * direction)) & 127
            slot = code & 7
            h = (code >> 3) & 3
            which = (code >> 5) & 1
            turn = sent[direction] % 2

            @pl.when(code < 127)
            def _():
                pl.when(sent[direction] > 1)(lambda: out_done(direction, turn))
                sem = out_send.at[direction, turn]
                for kind in (0, 1):
                    @pl.when((slot == 0) & (which == kind))
                    def _():
                        for group in (0, 1):
                            own_copy(h, kind, group, direction, sem).start()

                @pl.when(slot > 0)
                def _():
                    there = neighbours[direction]
                    far = jnp.where(p < 8, 8, -8)
                    near = jnp.where(slot == 1, -1, jnp.where(slot == 2, 1, jnp.where(slot == 3, -2, 2)))
                    off = jnp.where(slot < 5, near, jnp.where(slot == 5, -4, jnp.where(slot == 6, 4, far)))
                    target = slot_of(p + off - there)
                    remote(
                        kv.at[slot, which, h], kv.at[target, which, h], sem, kv_recv.at[target, which, h], (there * 2 + c, z)
                    ).start()

            after.append(sent[direction] + jnp.where(code < 127, 1, 0))
        return tuple(after)

    def start(copy):
        copy.start()

    def finish(copy):
        copy.wait_send()

    for h in range(HEADS_CORE):
        keep_q(h).start()
        keep_kv(h, 0).start()
        keep_kv(h, 1).start()
    keep_mask.start()
    pl.semaphore_wait(barrier, len(greeted))
    sent = (jnp.int32(0),) * 4
    for n in range(EARLY):
        sent = send(pick(SENDS[n], p), sent)
        first_sent(pick(ARRIVALS[n], p), start)
    swap_mask.start()
    for h in range(HEADS_CORE):
        swap_q(h).start()
        swap_kv(h, 0).start()
        swap_kv(h, 1).start()
    for h in range(HEADS_CORE):
        for dz in (1, 3, 2):
            w_copy(h, dz).start()
    for h in range(HEADS_CORE):
        for core in (0, 1):
            w_keep(h, core).start()

    top[...] = jnp.full_like(top, NEG)
    total[...] = jnp.zeros_like(total)
    accum[...] = jnp.zeros_like(accum)
    proj[...] = jnp.zeros_like(proj)

    keep_mask.wait()
    swap_mask.wait_recv()
    blocks = masks.shape[2]
    same = lax.broadcasted_iota(jnp.int32, (blocks, blocks), 0) == lax.broadcasted_iota(jnp.int32, (blocks, blocks), 1)
    anchor_rows = lax.broadcasted_iota(jnp.int32, (blocks, BLOCK), 0) < FRAME // BLOCK
    for core in (0, 1):
        for b in (0, 1):
            line = jnp.where(same, jnp.broadcast_to(masks[core, b : b + 1, :], (blocks, blocks)), 0)
            column = jnp.sum(line.astype(jnp.float32), axis=1, keepdims=True)
            wide = jnp.broadcast_to(column, (blocks, BLOCK))
            added = jnp.where((wide > 0) & ~anchor_rows, 0.0, NEG).astype(jnp.float32)
            for n in range(blocks // 2):
                bias[core, n, :, b * BLOCK : (b + 1) * BLOCK] = added[2 * n : 2 * n + 2, :]
        bias[core, 32] = jnp.zeros_like(bias[core, 32])

    def attend(slot, h, source, parts):
        scores = []
        for frame, halves in parts:
            rows = slice(frame * FRAME, (frame + 1) * FRAME)
            held = slice(halves[0] * FRAME, (halves[-1] + 1) * FRAME)
            scores.append(lax.dot_general(
                kv[slot, 0, h, held, :], qs[h, rows, :], (((1,), (1,)), ((), ())), preferred_element_type=jnp.float32
            ))
        weights = []
        factors = []
        for (frame, halves), score in zip(parts, scores):
            rows = slice(frame * FRAME, (frame + 1) * FRAME)
            length = len(halves) * FRAME
            score = score * EXP2_SCALE
            if source is not None:
                added = [bias[frame, source * 2 + half] for half in halves]
                added = added[0] if len(added) == 1 else jnp.concatenate(added, axis=0)
                score = (score.reshape(length // BLOCK, BLOCK, FRAME) + added[:, None, :]).reshape(length, FRAME)
            before = top[h, :, rows]
            now = jnp.maximum(before, jnp.max(score, axis=0, keepdims=True))
            weight = jnp.exp2(score - now)
            factor = jnp.exp2(before - now)
            total[h, :, rows] = total[h, :, rows] * factor + jnp.sum(weight, axis=0, keepdims=True)
            top[h, :, rows] = now
            weights.append(weight.astype(jnp.bfloat16))
            factors.append(factor)
        for (frame, halves), weight, factor in zip(parts, weights, factors):
            rows = slice(frame * FRAME, (frame + 1) * FRAME)
            held = slice(halves[0] * FRAME, (halves[-1] + 1) * FRAME)
            mixed = lax.dot_general(
                kv[slot, 1, h, held, :], weight, (((0,), (0,)), ((), ())), preferred_element_type=jnp.float32
            )
            accum[h, :, rows] = accum[h, :, rows] * factor + mixed

    def att_copy(h, dz, cross):
        core = 1 - c if cross else c
        rows = twin_rows if cross else my_rows
        return remote(
            attended.at[h, rows, :], att.at[h, z * 2 + c], att_send.at[h, dz, cross], att_recv.at[h, dz, cross],
            (p * 2 + core, (z + dz) % 4),
        )

    def project(h):
        for core in (0, 1):
            w_keep(h, core).wait()
        for dz in (0, 1, 3, 2):
            for cross in (0, 1):
                if dz or cross:
                    att_copy(h, dz, cross).wait_recv()
            if dz:
                w_pass(h, dz).wait_recv()
            place = ((z + 4 - dz) % 4) * 2
            left = jnp.concatenate([att[h, place], att[h, place + 1]], axis=1)
            for n in range(3):
                cols = slice(n * 256, (n + 1) * 256)
                right = jnp.concatenate([wts[h, place, :, cols], wts[h, place + 1, :, cols]], axis=0)
                part = proj[:, cols] + jnp.dot(left, right, preferred_element_type=jnp.float32)
                if h == HEADS_CORE - 1 and dz == 2:
                    out_ref[:, cols] = part.astype(out_ref.dtype)
                else:
                    proj[:, cols] = part

    def step(arrivals, sends, n, carry):
        sent, recent = carry
        word = pick(arrivals, n)
        slot = word & 15
        h = (word >> 4) & 3
        which = (word >> 6) & 1
        source = (word >> 18) & 15

        @pl.when((slot > 0) & (slot < 8))
        def _():
            whole = kv.at[slot, which, h]
            remote(whole, whole, pass_send.at[0, 0, 0], kv_recv.at[slot, which, h], twin).wait_recv()

        @pl.when(slot == 8)
        def _():
            first = kv.at[8, which, h, 0:FRAME, :]
            remote(first, first, pass_send.at[0, 0, 0], kv_recv.at[8, which, h], twin).wait_recv()

        first_sent(word, start)
        sent = send(pick(sends, n), sent)

        @pl.when(slot == 9)
        def _():
            keep_q(h).wait()
            swap_q(h).wait_recv()
            for kind in (0, 1):
                keep_kv(h, kind).wait()
                swap_kv(h, kind).wait_recv()
            attend(0, h, p, ((0, (0, 1)), (1, (0, 1))))

        @pl.when(((word >> 15) & 1) == 1)
        def _():
            @pl.when(slot == 1)
            def _():
                attend(1, h, source, ((0, (0, 1)), (1, (1,))))

            @pl.when(slot == 2)
            def _():
                attend(2, h, source, ((0, (0,)), (1, (0, 1))))

            @pl.when((slot > 2) & (slot < 8))
            def _():
                attend(slot, h, source, ((0, (0,)), (1, (1,))))

        @pl.when(((word >> 17) & 1) == 1)
        def _():
            attend(jnp.where(slot == 9, 0, slot), h, None, ((0, (0,)), (1, (0,))))

        @pl.when(((word >> 16) & 1) == 1)
        def _():
            for cross in (1, 0):
                rows = twin_rows if cross else my_rows
                held = accum[h, :, rows] * (1.0 / total[h, :, rows])
                attended[h, rows, :] = jnp.transpose(held).astype(jnp.bfloat16)
                for dz in (2, 1, 3, 0):
                    if dz or cross:
                        att_copy(h, dz, cross).start()
            att[h, z * 2 + c] = attended[h, my_rows, :]

        @pl.when(slot == 10)
        def _():
            for dz in (1, 3, 2):
                w_copy(h, dz).wait_recv()
                w_pass(h, dz).start()

        first_sent(recent[0], finish)
        return sent, recent[1:] + (word,)

    carry = sent, (jnp.int32(15),) * (LAG - EARLY) + tuple(pick(line, p) for line in ARRIVALS[:EARLY])
    length = -(-(COUNT - EARLY) // PARTS)
    for begin in range(EARLY, COUNT, length):
        end = min(begin + length, COUNT)
        arrivals = [pick(line, p) for line in ARRIVALS[begin:end]]
        sends = [pick(line, p) for line in SENDS[begin:end]]
        carry = lax.fori_loop(0, end - begin, functools.partial(step, arrivals, sends), carry)
    recent = carry[1]

    def finish_heads(heads):
        for h in heads:
            for dz in range(4):
                for cross in (0, 1):
                    if dz or cross:
                        att_copy(h, dz, cross).wait_send()

    project(0)
    project(1)
    for word in recent:
        first_sent(word, finish)
    for direction in range(4):
        for turn in (0, 1):
            out_done(direction, turn)
    for h in range(HEADS_CORE):
        for which in (0, 1):
            swap_kv(h, which).wait_send()
        swap_q(h).wait_send()
        for dz in (1, 2, 3):
            w_copy(h, dz).wait_send()
            w_pass(h, dz).wait_send()
    swap_mask.wait_send()
    finish_heads((0, 1))
    project(2)
    finish_heads((2,))


def body(queries, keys, values, block_mask, w_out):
    bf16, f32, dma = jnp.bfloat16, jnp.float32, pltpu.SemaphoreType.DMA
    heads = HEADS_CORE
    anywhere = pl.BlockSpec(memory_space=pl.ANY)
    return pl.pallas_call(
        kernel,
        out_shape=jax.ShapeDtypeStruct((FRAME, 768), bf16),
        in_specs=[anywhere, anywhere, anywhere, pl.BlockSpec(memory_space=pltpu.VMEM), anywhere],
        out_specs=pl.BlockSpec(memory_space=pltpu.VMEM),
        scratch_shapes=[
            pltpu.VMEM((9, 2, heads, 2 * FRAME, HEAD_DIM), bf16),
            pltpu.VMEM((heads, 2 * FRAME, HEAD_DIM), bf16),
            pltpu.VMEM((2, 2, 64), jnp.int32),
            pltpu.VMEM((2, 33, 2, FRAME), f32),
            pltpu.VMEM((heads, 8, HEAD_DIM, 768), bf16),
            pltpu.VMEM((heads, 8, FRAME, HEAD_DIM), bf16),
            pltpu.VMEM((heads, 2 * FRAME, HEAD_DIM), bf16),
            pltpu.VMEM((heads, 1, 2 * FRAME), f32),
            pltpu.VMEM((heads, 1, 2 * FRAME), f32),
            pltpu.VMEM((heads, HEAD_DIM, 2 * FRAME), f32),
            pltpu.VMEM((FRAME, 768), f32),
            dma((9, 2, heads)), dma((4, 2)), dma((2, 2, heads, 4)), dma((2, heads, 4)), dma((heads,)), dma((heads,)), dma((2, heads)), dma((3, heads)),
            dma((heads, 3)), dma((heads, 3)), dma((heads, 2)), dma((heads, 3)), dma((heads, 3)),
            dma((heads, 4, 2)), dma((heads, 4, 2)), dma((3,)),
        ],
        compiler_params=pltpu.CompilerParams(
            collective_id=0, has_side_effects=True, vmem_limit_bytes=VMEM_LIMIT
        ),
        name="radial_attention",
    )(queries, keys, values, block_mask, w_out)


def solution(mesh):
    placed = (P("ctx", "head"), P("ctx", "head"), P("ctx", "head"), P("ctx", None), P("head", None))
    return jax.shard_map(
        body, mesh=mesh, in_specs=placed, out_specs=P("ctx", "head"), check_vma=False
    )
```
